32 devices in a mesh: blk: 4 (over y, core), dp: 8 (over z, x).
Axes of the slice: x: 2, y: 2, z: 4, core: 2. Of those that a mesh axis runs over, the one named last changes fastest.
Arguments:
- tokens: bfloat16 [8, 1024, 384], P('dp', 'blk'), may hold values from -6 to 6
- lengths: int32 [8], P('dp'), may hold values from 512 to 1024, as said below
- query_weight: bfloat16 [384, 384], replicated, may hold values from -0.3125 to 0.3125
- query_bias: bfloat16 [384], replicated, may hold values from -1.5 to 1.5
- key_weight: bfloat16 [384, 384], replicated, may hold values from -0.3125 to 0.3125
- key_bias: bfloat16 [384], replicated, may hold values from -1.5 to 1.5
- value_weight: bfloat16 [384, 384], replicated, may hold values from -0.3125 to 0.3125
- value_bias: bfloat16 [384], replicated, may hold values from -1.5 to 1.5
- output_weight: bfloat16 [384, 384], replicated, may hold values from -2.5 to 2.5
- output_bias: bfloat16 [384], replicated, may hold values from -1.5 to 1.5
- first_gain: bfloat16 [384], replicated, may hold values from 0.5 to 1.5
- first_bias: bfloat16 [384], replicated, may hold values from -1.5 to 1.5
- inner_weight: bfloat16 [384, 1536], replicated, may hold values from -0.3125 to 0.3125
- inner_bias: bfloat16 [1536], replicated, may hold values from -1.5 to 1.5
- outer_weight: bfloat16 [1536, 384], replicated, may hold values from -0.15625 to 0.15625
- outer_bias: bfloat16 [384], replicated, may hold values from -1.5 to 1.5
- second_gain: bfloat16 [384], replicated, may hold values from 0.5 to 1.5
- second_bias: bfloat16 [384], replicated, may hold values from -1.5 to 1.5
- relative_table: bfloat16 [512, 384], replicated, may hold values from -6 to 6
- cotangent: bfloat16 [8, 1024, 384], P('dp', 'blk'), may hold values from -18 to 18
Outputs:
- layer_out: float32 [8, 1024, 384], P('dp', 'blk')
- grad_tokens: float32 [8, 1024, 384], P('dp', 'blk')
- grad_query_weight: float32 [384, 384], replicated
- grad_query_bias: float32 [384], replicated
- grad_key_weight: float32 [384, 384], replicated
- grad_key_bias: float32 [384], replicated
- grad_value_weight: float32 [384, 384], replicated
- grad_value_bias: float32 [384], replicated
- grad_output_weight: float32 [384, 384], replicated
- grad_output_bias: float32 [384], replicated
- grad_first_gain: float32 [384], replicated
- grad_first_bias: float32 [384], replicated
- grad_inner_weight: float32 [384, 1536], replicated
- grad_inner_bias: float32 [1536], replicated
- grad_outer_weight: float32 [1536, 384], replicated
- grad_outer_bias: float32 [384], replicated
- grad_second_gain: float32 [384], replicated
- grad_second_bias: float32 [384], replicated
- grad_relative_table: float32 [512, 384], replicated
The draws below stay inside these ranges and needn't reach their ends.
Inputs may be any that keep to these rules, and one draw needn't show every extreme that they name: `lengths`: one sequence uses all 1024 positions and one uses 1024 // 2.
All inputs are finite; a program needn't handle non-finite values.
Results may differ from the reference program's by a relative error of at most 0.04.
Values may be sent and summed in bfloat16 or wider, within the bound.
No kernel may reach another device: no remote copies, remote signals or barrier semaphores. Data moves between devices by JAX's collectives and lax.ppermute only.
A program may use at most 320 MiB of HBM per device.

```python
import math
import jax
import jax.numpy as jnp
from jax import lax

D = 384
HEADS = 6
FF = 1536
SPAN = 256
REL = 512
SEQ_LEN = 1024
SEQS = 8


def draw_lengths(key, part):
    first_key, second_key = jax.random.split(jax.random.fold_in(key, 11))
    counts = jax.random.randint(first_key, (SEQS,), SEQ_LEN // 2, SEQ_LEN + 1)
    chosen = jax.random.randint(second_key, (), 0, SEQS)
    counts = counts.at[chosen].set(SEQ_LEN)
    counts = counts.at[(chosen + SEQS // 2) % SEQS].set(SEQ_LEN // 2)
    return counts.astype(jnp.int32)


def draw_cotangent(key, part):
    noise_key, scale_key = jax.random.split(jax.random.fold_in(key, 23))
    noise = jnp.clip(jax.random.normal(noise_key, (SEQS, SEQ_LEN, D), jnp.float32), -4.5, 4.5)
    row_scale = jnp.exp(jax.random.uniform(scale_key, (SEQS, SEQ_LEN, 1), jnp.float32, -0.8, 0.8))
    ramp = 3.0 ** (jnp.arange(SEQS, dtype=jnp.float32) / (SEQS - 1) - 0.5)
    return (noise * row_scale * ramp[:, None, None]).astype(jnp.bfloat16)


def block_levels(stream_key, shape, cuts, least, high):
    loudness = 1.0
    for position, shards_of in cuts:
        steps = jax.random.uniform(jax.random.fold_in(jax.random.fold_in(stream_key, 6), position), (shards_of,), jnp.float32, least / len(cuts), high / len(cuts))
        loudness = loudness * jnp.repeat(jnp.exp(steps), shape[position] // shards_of).reshape((-1,) + (1,) * (len(shape) - 1 - position))
    return loudness


def gaussian(stream_key, dims, scale, reach, cuts=(), held_as=jnp.bfloat16):
    values = scale * jax.random.normal(stream_key, dims, jnp.float32)
    if cuts:
        values = values * block_levels(stream_key, dims, cuts, -0.22, 0.18)
    return jnp.clip(values, -reach, reach).astype(held_as)


def setup_inputs(seed: int = 0) -> dict:
    key_of = jax.random.split(jax.random.key(seed), 21)
    return {
        "tokens": gaussian(key_of[0], (SEQS, SEQ_LEN, D), 1.0, 6.0, ((0, 8), (1, 4))),
        "lengths": draw_lengths(jax.random.fold_in(key_of[20], 71), 0),
        "query_weight": gaussian(key_of[2], (D, D), D ** -0.5, 0.3125),
        "query_bias": gaussian(key_of[3], (D,), 0.3, 1.5),
        "key_weight": gaussian(key_of[4], (D, D), D ** -0.5, 0.3125),
        "key_bias": gaussian(key_of[5], (D,), 0.3, 1.5),
        "value_weight": gaussian(key_of[6], (D, D), D ** -0.5, 0.3125),
        "value_bias": gaussian(key_of[7], (D,), 0.3, 1.5),
        "output_weight": gaussian(key_of[8], (D, D), (D // 64) ** -0.5, 2.5),
        "output_bias": gaussian(key_of[9], (D,), 0.3, 1.5),
        "first_gain": jnp.clip(1.0 + 0.1 * jax.random.normal(key_of[10], (D,), jnp.float32), 0.5, 1.5).astype(jnp.bfloat16),
        "first_bias": gaussian(key_of[11], (D,), 0.3, 1.5),
        "inner_weight": gaussian(key_of[12], (D, FF), D ** -0.5, 0.3125),
        "inner_bias": gaussian(key_of[13], (FF,), 0.3, 1.5),
        "outer_weight": gaussian(key_of[14], (FF, D), FF ** -0.5, 0.15625),
        "outer_bias": gaussian(key_of[15], (D,), 0.3, 1.5),
        "second_gain": jnp.clip(1.0 + 0.1 * jax.random.normal(key_of[16], (D,), jnp.float32), 0.5, 1.5).astype(jnp.bfloat16),
        "second_bias": gaussian(key_of[17], (D,), 0.3, 1.5),
        "relative_table": gaussian(key_of[18], (REL, D), 1.0, 6.0),
        "cotangent": draw_cotangent(jax.random.fold_in(key_of[20], 71), 0),
    }


@jax.custom_vjp
def low(v):
    return lax.optimization_barrier(v.astype(jnp.bfloat16)).astype(jnp.float32)

@jax.custom_vjp
def low_back(v):
    return v

def low_keep(v):
    return (low(v), None)

def low_pass(kept, grad):
    return (grad,)

def back_keep(v):
    return (v, None)

def back_low(kept, grad):
    return (low(grad),)
low.defvjp(low_keep, low_pass)
low_back.defvjp(back_keep, back_low)

def matmul(left_side, right_side):
    return jnp.dot(left_side, right_side, precision=lax.Precision.HIGHEST)

def layer_norm(values, gain_vec, bias_vec):
    center = values - lax.optimization_barrier(jnp.mean(values, axis=-1, keepdims=True))
    spread = lax.optimization_barrier(jnp.mean(center * center, axis=-1, keepdims=True))
    return center * lax.rsqrt(spread + 1e-07) * gain_vec + bias_vec

def one_sequence(tokens_f, length, weights):
    query_weight, query_bias, key_weight, key_bias, value_weight, value_bias, output_weight, output_bias, first_gain, first_bias, inner_weight, inner_bias, outer_weight, outer_bias, second_gain, second_bias, relative_table = weights
    row_total, model_width = tokens_f.shape
    head_dim = model_width // HEADS
    rel_count = relative_table.shape[0]
    query_rows = low_back(low(matmul(tokens_f, query_weight) + query_bias)).reshape(row_total, HEADS, head_dim)
    key_rows = low_back(low(matmul(tokens_f, key_weight) + key_bias)).reshape(row_total, HEADS, head_dim)
    value_rows = low_back(low(matmul(tokens_f, value_weight) + value_bias)).reshape(row_total, HEADS, head_dim)
    rel_keys = low(matmul(relative_table, key_weight) + key_bias).reshape(rel_count, HEADS, head_dim)
    rel_queries = low(matmul(relative_table, query_weight) + query_bias).reshape(rel_count, HEADS, head_dim)
    places = jnp.arange(row_total, dtype=jnp.int32)
    distance = jnp.clip(places[:, None] - places[None, :] + SPAN, 0, 2 * SPAN - 1).astype(jnp.int32)
    highest = lax.Precision.HIGHEST
    content = jnp.einsum('ihd,jhd->hij', query_rows, key_rows, precision=highest)
    query_table = jnp.einsum('ihd,rhd->hir', query_rows, rel_keys, precision=highest)
    to_position = jnp.take_along_axis(query_table, jnp.broadcast_to(distance[None], (HEADS, row_total, row_total)), axis=2)
    key_table = jnp.einsum('jhd,rhd->hjr', key_rows, rel_queries, precision=highest)
    from_position = jnp.take_along_axis(key_table, jnp.broadcast_to(distance.T[None], (HEADS, row_total, row_total)), axis=2)
    from_position = jnp.transpose(from_position, (0, 2, 1))
    scores = low_back((content + to_position + from_position) * (1.0 / math.sqrt(3.0 * head_dim)))
    usable = places < length
    scores = jnp.where(usable[None, None, :], scores, -1e+30)
    attention = jax.nn.softmax(scores, axis=-1)
    mixture = jnp.einsum('hij,jhd->ihd', low(attention), value_rows, precision=highest).reshape(row_total, model_width)
    mixture = low_back(low(mixture))
    branch_out = low_back(matmul(mixture, output_weight) + output_bias)
    normed = low_back(low(layer_norm(tokens_f + branch_out, first_gain, first_bias)))
    inner_pre = low_back(matmul(normed, inner_weight) + inner_bias)
    active = low(jax.nn.gelu(inner_pre, approximate=False))
    outer_out = low_back(matmul(active, outer_weight) + outer_bias)
    return layer_norm(normed + outer_out, second_gain, second_bias)

def reference(tokens, lengths, query_weight, query_bias, key_weight, key_bias, value_weight, value_bias, output_weight, output_bias, first_gain, first_bias, inner_weight, inner_bias, outer_weight, outer_bias, second_gain, second_bias, relative_table, cotangent):
    params = tuple((item.astype(jnp.float32) for item in (query_weight, query_bias, key_weight, key_bias, value_weight, value_bias, output_weight, output_bias, first_gain, first_bias, inner_weight, inner_bias, outer_weight, outer_bias, second_gain, second_bias, relative_table)))
    tokens_f = tokens.astype(jnp.float32)

    def forward(inputs, weights):

        def single(seq_pair):
            return jax.checkpoint(one_sequence)(seq_pair[0], seq_pair[1], weights)
        return lax.map(single, (inputs, lengths))
    layer_out, pullback = jax.vjp(forward, tokens_f, params)
    grad_inputs, grad_params = pullback(cotangent.astype(jnp.float32))
    g_query_weight, g_query_bias, g_key_weight, g_key_bias, g_value_weight, g_value_bias, g_output_weight, g_output_bias, g_first_gain, g_first_bias, g_inner_weight, g_inner_bias, g_outer_weight, g_outer_bias, g_second_gain, g_second_bias, g_relative = grad_params
    return (layer_out.astype(jnp.float32), grad_inputs.astype(jnp.float32), g_query_weight, g_query_bias, g_key_weight, g_key_bias, g_value_weight, g_value_bias, g_output_weight, g_output_bias, g_first_gain, g_first_bias, g_inner_weight, g_inner_bias, g_outer_weight, g_outer_bias, g_second_gain, g_second_bias, g_relative)
```

```python
import math

import jax
import jax.numpy as jnp
from jax import lax
from jax.experimental import pallas as pl
from jax.experimental.pallas import tpu as pltpu
from jax.sharding import PartitionSpec as P

HEADS = 6
BF = jnp.bfloat16
F32 = jnp.float32
LOG2E = math.log2(math.e)
EPS = 1e-07
VMEM_LIMIT = 56 * 1024 * 1024
EARLY_ROWS = 3584
LATE_ROWS = 1792


def nn(left, right):
    return lax.dot_general(left, right, (((1,), (0,)), ((), ())), preferred_element_type=F32)


def nt(left, right):
    return lax.dot_general(left, right, (((1,), (1,)), ((), ())), preferred_element_type=F32)


def tn(left, right):
    return lax.dot_general(left, right, (((0,), (0,)), ((), ())), preferred_element_type=F32)


def tt(left, right):
    return lax.dot_general(left, right, (((0,), (1,)), ((), ())), preferred_element_type=F32)


def lanes(shape):
    return lax.broadcasted_iota(jnp.int32, shape, len(shape) - 1)


def of_head(values, head):
    inside = (lanes(values.shape) // 64) == head
    return jnp.where(inside, values, jnp.zeros_like(values))


def pair_columns(pair):
    return pl.ds(pl.multiple_of(pair * 128, 128), 128)


def wide(column, width):
    return jnp.broadcast_to(column, (column.shape[0], width))


def reversal(size):
    rows = lax.broadcasted_iota(jnp.int32, (size, size), 0)
    cols = lax.broadcasted_iota(jnp.int32, (size, size), 1)
    return jnp.where(rows + cols == size - 1, 1.0, 0.0).astype(BF)


def place_blocks(block, x_all, own, core, far, diagonal):
    size = own.shape[0]
    even = block % 2 == 0
    core_at = jnp.where(even, 2 * size, 0)
    diagonal_at = jnp.where(even, 0, 2 * size)
    x_all[pl.ds(size, size), :] = own[...]
    x_all[pl.ds(3 * size, size), :] = far[...]
    x_all[pl.ds(pl.multiple_of(core_at, size), size), :] = core[...]
    x_all[pl.ds(pl.multiple_of(diagonal_at, size), size), :] = diagonal[...]


def position_terms(block, s_ref, own_rows, own_table, others, other_table, own_shift, other_shift):
    size = own_rows.shape[0]
    rel = own_table.shape[0]
    scores = nt(own_rows, own_table)
    last, first = scores[:, rel - 1 : rel], scores[:, 0:1]
    source = jnp.concatenate([scores, wide(last, size), wide(first, size)], axis=1)
    rolled = pltpu.roll(source, own_shift, 1, stride=1, stride_axis=0)
    for slot in range(3):
        rows = others(slot)
        if slot == 0:
            part = nt(rows, other_table[size:, :])
            part = jnp.concatenate([part, wide(part[:, size - 1 : size], size)], axis=1)
        elif slot == 1:
            part = nt(rows, other_table)
        else:
            part = nt(rows, other_table[:size, :])
            part = jnp.concatenate([wide(part[:, 0:1], size), part], axis=1)
        part = pltpu.roll(part, other_shift, 1, stride=1, stride_axis=0)[:, size:]
        span = slice(slot * size, (slot + 1) * size)
        s_ref[:, span] = rolled[:, span] + part.T
    low_half = block < 2
    constant = jnp.where(low_half, last, first)

    def constant_terms(slot):
        rows = others(slot)
        top = nt(other_table[0:16, :], rows)[0:1, :]
        bottom = nt(other_table[rel - 16 : rel, :], rows)[15:16, :]
        return constant + jnp.where(low_half, top, bottom)

    s_ref[:, 3 * size :] = constant_terms(3)

    @pl.when(block == 0)
    def _():
        s_ref[:, :size] = constant_terms(0)

    @pl.when(block == 3)
    def _():
        s_ref[:, 2 * size : 3 * size] = constant_terms(2)


def extend_table(block, ext_ref, table_ref):
    rel = table_ref.shape[0]
    half = rel // 2
    width = table_ref.shape[1]
    first, last = table_ref[0:1, :], table_ref[rel - 1 : rel, :]
    ext_ref[0:rel, :] = table_ref[...]
    ext_ref[rel : rel + half, :] = jnp.broadcast_to(last, (half, width))
    ext_ref[rel + half : 2 * rel, :] = jnp.broadcast_to(first, (half, width))
    far = jnp.where(block < 2, last.astype(F32), first.astype(F32)).astype(BF)
    ext_ref[2 * rel : 3 * rel, :] = jnp.broadcast_to(far, (rel, width))


def unskewed(block, wall_ref, near_ref, grad_rows, shift):
    size = grad_rows.shape[0]
    near_ref[:, : 3 * size] = grad_rows[:, : 3 * size]
    near_ref[:, 3 * size :] = jnp.zeros((size, size), BF)
    wall_ref[:, 4 * size : 5 * size] = grad_rows[:, 3 * size :]
    wall_ref[:, 5 * size :] = jnp.zeros((size, size), BF)

    @pl.when(block == 0)
    def _():
        wall_ref[:, 5 * size :] = near_ref[:, :size]
        near_ref[:, :size] = jnp.zeros((size, size), BF)

    @pl.when(block == 3)
    def _():
        wall_ref[:, 5 * size :] = near_ref[:, 2 * size : 3 * size]
        near_ref[:, 2 * size : 3 * size] = jnp.zeros((size, size), BF)

    wall_ref[:, : 4 * size] = pltpu.roll(near_ref[...], shift, 1, stride=1, stride_axis=0)


def table_grad(block, sums, scale):
    rel = sums.shape[1] // 3
    half = rel // 2
    over = jnp.sum(sums[:, rel : rel + half], axis=1, keepdims=True)
    under = jnp.sum(sums[:, rel + half : 2 * rel], axis=1, keepdims=True)
    far = jnp.sum(sums[:, 2 * rel :], axis=1, keepdims=True)
    over = over + jnp.where(block < 2, far, 0.0)
    under = under + jnp.where(block < 2, 0.0, far)
    at = lanes((sums.shape[0], rel))
    folded = sums[:, :rel] + jnp.where(at == rel - 1, over, 0.0) + jnp.where(at == 0, under, 0.0)
    return folded * scale


def affine(values, weight_ref, bias_ref):
    return nn(values, weight_ref[...]) + bias_ref[...].astype(F32)


def norm_forward(values):
    center = values - jnp.mean(values, axis=-1, keepdims=True)
    spread = jnp.mean(center * center, axis=-1, keepdims=True)
    rate = lax.rsqrt(spread + EPS)
    return center * rate, rate


def norm_backward(grad_hat, hat, rate):
    mean_grad = jnp.mean(grad_hat, axis=-1, keepdims=True)
    mean_along = jnp.mean(grad_hat * hat, axis=-1, keepdims=True)
    return rate * (grad_hat - mean_grad - hat * mean_along)


def column_sum(values):
    return jnp.sum(values.astype(F32), axis=0, keepdims=True)


def forward_kernel(
    block_ref, length_ref, own, core, far, diagonal,
    query_weight, query_bias, key_weight, key_bias, value_weight, value_bias,
    output_weight, output_bias, first_gain, first_bias, inner_weight, inner_bias,
    outer_weight, outer_bias, second_gain, second_bias, relative, relative_back, cotangent,
    layer_out, grad_first_out, chances_out, sent_out, query_out, key_out, value_out,
    rel_query_out, rel_key_out, grads_out,
    x_all, s_ref, mixture_ref, log_ref, active_ref, slope_ref,
):
    block = block_ref[0]
    length = length_ref[0]
    size, model_width = own.shape
    head_dim = model_width // HEADS
    factor = LOG2E / math.sqrt(3.0 * head_dim)
    place_blocks(block, x_all, own, core, far, diagonal)
    query_out[...] = affine(x_all[...], query_weight, query_bias).astype(BF)
    key_out[...] = affine(x_all[...], key_weight, key_bias).astype(BF)
    value_out[...] = affine(x_all[...], value_weight, value_bias).astype(BF)
    rel_query_out[...] = affine(relative[...], query_weight, query_bias).astype(BF)
    rel_key_out[...] = affine(relative_back[...], key_weight, key_bias).astype(BF)
    step = lanes((1, 4 * size))
    position = ((block + 3 + step // size) % 4) * size + step % size
    mask_row = jnp.where(position < length, 0.0, -1e30)
    stat_lane = lanes((size, 128))
    log_ref[...] = jnp.zeros_like(log_ref)

    def pair_step(pair, carry):
        columns = pair_columns(pair)
        total = jnp.zeros((size, 128), F32)
        for side in range(2):
            head = 2 * pair + side
            query_own = of_head(query_out[size : 2 * size, columns], side)
            position_terms(
                block,
                s_ref,
                query_own,
                rel_key_out[:, columns],
                lambda slot: key_out[slot * size : (slot + 1) * size, columns],
                of_head(rel_query_out[:, columns], side),
                1,
                0,
            )
            content = nt(query_own, key_out[:, columns])
            s_ref[...] = (s_ref[...] + content) * factor + mask_row
            top = jnp.max(s_ref[...], axis=1, keepdims=True)
            raised = jnp.exp2(s_ref[...] - top)
            s_ref[...] = raised
            row_sum = jnp.sum(raised, axis=1, keepdims=True)
            chances = (s_ref[...] * (1.0 / row_sum)).astype(BF)
            chances_out[head] = chances
            log_total = top + jnp.log2(row_sum)
            log_ref[...] = jnp.where(stat_lane % 8 == head, log_total, log_ref[...])
            total = total + nn(chances, of_head(value_out[:, columns], side))
        mixture_ref[:, columns] = total
        return carry

    lax.fori_loop(0, HEADS // 2, pair_step, 0)

    inner_width = inner_weight.shape[1]
    chunks = inner_width // model_width
    mixture_low = mixture_ref[...].astype(BF)
    first_sum = own[...].astype(F32) + affine(mixture_low, output_weight, output_bias)
    first_hat, first_rate = norm_forward(first_sum)
    normed = (first_hat * first_gain[...].astype(F32) + first_bias[...].astype(F32)).astype(BF)
    root_half = math.sqrt(0.5)
    density = 1.0 / math.sqrt(2.0 * math.pi)

    second_sum = normed.astype(F32) + outer_bias[...].astype(F32)
    for chunk in range(chunks):
        span = slice(chunk * model_width, (chunk + 1) * model_width)
        inner_pre = nn(normed, inner_weight[:, span]) + inner_bias[:, span].astype(F32)
        below = 0.5 + 0.5 * lax.erf(inner_pre * root_half)
        slope_ref[:, span] = below + inner_pre * density * jnp.exp(-0.5 * inner_pre * inner_pre)
        active_ref[:, span] = (inner_pre * below).astype(BF)
        second_sum = second_sum + nn(active_ref[:, span], outer_weight[span, :])
    second_hat, second_rate = norm_forward(second_sum)
    gain = second_gain[...].astype(F32)
    layer_out[...] = second_hat * gain + second_bias[...].astype(F32)
    cot = cotangent[...].astype(F32)
    grad_second = norm_backward(cot * gain, second_hat, second_rate)
    grad_outer = grad_second.astype(BF)
    outer_at, inner_at, output_at, small_at = 0, inner_width, 2 * inner_width, 2 * inner_width + model_width
    grads_out[small_at:, :] = jnp.zeros((grads_out.shape[0] - small_at, model_width), BF)
    small = [column_sum(grad_outer), column_sum(cot * second_hat), column_sum(cot)]
    grad_normed = grad_second
    for chunk in range(chunks):
        span = slice(chunk * model_width, (chunk + 1) * model_width)
        grads_out[outer_at + chunk * model_width : outer_at + (chunk + 1) * model_width, :] = tn(
            active_ref[:, span], grad_outer
        ).astype(BF)
        grad_inner = (nt(grad_outer, outer_weight[span, :]) * slope_ref[:, span]).astype(BF)
        small.append(column_sum(grad_inner))
        grads_out[inner_at + chunk * model_width : inner_at + (chunk + 1) * model_width, :] = tn(
            normed, grad_inner
        ).astype(BF)
        grad_normed = grad_normed + nt(grad_inner, inner_weight[:, span])
    grad_normed = grad_normed.astype(BF).astype(F32)
    grad_first = norm_backward(grad_normed * first_gain[...].astype(F32), first_hat, first_rate)
    grad_first_out[...] = grad_first
    grad_branch = grad_first.astype(BF)
    grads_out[output_at : output_at + model_width, :] = tn(mixture_low, grad_branch).astype(BF)
    small += [column_sum(grad_normed * first_hat), column_sum(grad_normed), column_sum(grad_branch)]
    small += [jnp.zeros((16 - len(small), model_width), F32)]
    grads_out[small_at : small_at + 16, :] = jnp.concatenate(small, axis=0).astype(BF)
    grad_mixture = nt(grad_branch, output_weight[...]).astype(BF)
    sent_out[:, :model_width] = grad_mixture
    along = grad_mixture.astype(F32) * mixture_ref[...]
    stats = jnp.where(stat_lane < 16, 0.0, log_ref[...])
    for head in range(HEADS):
        columns = slice((head // 2) * 128, (head // 2 + 1) * 128)
        delta = jnp.sum(of_head(along[:, columns], head % 2), axis=1, keepdims=True)
        stats = jnp.where((stat_lane == head) | (stat_lane == 8 + head), delta, stats)
    upper = stats.astype(BF).astype(F32)
    rest = stats - upper
    middle = rest.astype(BF).astype(F32)
    group = stat_lane // 8
    parts = jnp.where((group == 0) | (group == 2), upper, jnp.where((group == 1) | (group == 3), middle, rest - middle))
    sent_out[:, model_width:] = jnp.where(group < 5, parts, 0.0).astype(BF)


def position_backward(block, side, grad_scores, flip, other_pair, ext_pair, own_rows_back, wall_ref, near_ref, shift):
    grad_back = nn(flip, grad_scores).astype(BF)
    unskewed(block, wall_ref, near_ref, grad_back, shift)
    row_grad = nn(grad_back, of_head(other_pair, side)) + nn(wall_ref[...], of_head(ext_pair, side))
    return row_grad, tn(of_head(own_rows_back, side), wall_ref[...])


def query_kernel(
    block_ref, chances, sent, query_all, key_all, value_all, rel_key,
    grad_query_out, grad_rel_key_out,
    ext_ref, wall_ref, near_ref, back_ref, sum_ref, rows_ref,
):
    block = block_ref[0]
    size, model_width = grad_query_out.shape
    scale = 1.0 / math.sqrt(3.0 * (model_width // HEADS))
    flip = reversal(size)
    extend_table(block, ext_ref, rel_key)
    back_ref[...] = nn(flip, query_all[size : 2 * size, :]).astype(BF)
    stats = sent[:, model_width:].astype(F32)
    stat_lane = lanes((size, 128))

    def pair_step(pair, carry):
        columns = pair_columns(pair)
        row_grad = jnp.zeros((size, 128), F32)
        for side in range(2):
            head = 2 * pair + side
            delta = jnp.sum(
                jnp.where((stat_lane == head) | (stat_lane == 8 + head), stats, 0.0), axis=1, keepdims=True
            )
            grad_mixture = of_head(sent[:, columns], side)
            grad_chances = nt(grad_mixture, value_all[:, columns])
            grad_scores = (chances[head].astype(F32) * (grad_chances - delta)).astype(BF)
            rows, table = position_backward(
                block, side, grad_scores, flip, key_all[:, columns], ext_ref[:, columns],
                back_ref[:, columns], wall_ref, near_ref, 3 * size,
            )
            row_grad = row_grad + rows
            if side == 0:
                sum_ref[...] = table
            else:
                sum_ref[...] += table
        rows_ref[:, columns] = (row_grad * scale).astype(BF)
        grad_rel_key_out[columns, :] = table_grad(block, sum_ref[...], scale)
        return carry

    lax.fori_loop(0, HEADS // 2, pair_step, 0)
    grad_query_out[...] = nn(flip, rows_ref[...]).astype(BF)


def key_kernel(
    block_ref, length_ref, own, sent_own, sent_core, sent_far, sent_diagonal, query_all, key_all, value_all,
    rel_query, rel_key, grad_query, grad_rel_key, grad_first,
    query_weight, key_weight, value_weight, relative,
    grad_tokens_out, grads_out,
    sent_ref, s_ref, grad_ref, ext_ref, wall_ref, near_ref, back_ref, sum_ref, key_rows_ref, value_rows_ref,
    rel_grad_ref, stat_ref,
):
    block = block_ref[0]
    length = length_ref[0]
    size, model_width = own.shape
    rel = rel_query.shape[0]
    scale = 1.0 / math.sqrt(3.0 * (model_width // HEADS))
    factor = LOG2E * scale
    flip = reversal(size)
    place_blocks(block, sent_ref, sent_own, sent_core, sent_far, sent_diagonal)
    extend_table(block, ext_ref, rel_query)
    back_ref[...] = nn(flip, key_all[size : 2 * size, :]).astype(BF)
    stats = sent_ref[:, model_width:].astype(F32).T
    stat_ref[0:8, :] = stats[0:8, :] + stats[8:16, :]
    stat_ref[8:16, :] = stats[16:24, :] + (stats[24:32, :] + stats[32:40, :])
    position = block * size + lax.broadcasted_iota(jnp.int32, (size, 1), 0)
    mask_column = jnp.where(position < length, 0.0, -1e30)

    def pair_step(pair, carry):
        columns = pair_columns(pair)
        row_grad = jnp.zeros((size, 128), F32)
        value_grad = jnp.zeros((size, 128), F32)
        for side in range(2):
            head = 2 * pair + side
            key_own = of_head(key_all[size : 2 * size, columns], side)
            position_terms(
                block,
                s_ref,
                key_own,
                rel_query[:, columns],
                lambda slot: query_all[slot * size : (slot + 1) * size, columns],
                of_head(rel_key[:, columns], side),
                0,
                1,
            )
            content = nt(key_own, query_all[:, columns])
            shift = mask_column - stat_ref[pl.ds(8 + head, 1), :]
            s_ref[...] = jnp.exp2((s_ref[...] + content) * factor + shift)
            value_grad = value_grad + nn(s_ref[...].astype(BF), of_head(sent_ref[:, columns], side))
            grad_chances = nt(of_head(value_all[size : 2 * size, columns], side), sent_ref[:, columns])
            grad_ref[...] = (s_ref[...] * (grad_chances - stat_ref[pl.ds(head, 1), :])).astype(BF)
            rows, table = position_backward(
                block, side, grad_ref[...], flip, query_all[:, columns], ext_ref[:, columns],
                back_ref[:, columns], wall_ref, near_ref, 3 * size + 1,
            )
            row_grad = row_grad + rows
            if side == 0:
                sum_ref[...] = table
            else:
                sum_ref[...] += table
        key_rows_ref[:, columns] = (row_grad * scale).astype(BF)
        value_rows_ref[:, columns] = value_grad.astype(BF)
        rel_grad_ref[columns, :] = table_grad(block, sum_ref[...], scale)
        return carry

    lax.fori_loop(0, HEADS // 2, pair_step, 0)
    grad_key = nn(flip, key_rows_ref[...]).astype(BF)
    grad_value = value_rows_ref[...]
    rel_query_grad = rel_grad_ref[...]
    rel_key_grad = grad_rel_key[...]
    query_low = rel_query_grad.astype(BF)
    key_low = nn(rel_key_grad.astype(BF), reversal(rel)).astype(BF)
    tokens = own[...]
    table = relative[...]
    grads_out[0:model_width, :] = (tn(tokens, grad_query[...]) + tt(table, query_low)).astype(BF)
    grads_out[model_width : 2 * model_width, :] = (tn(tokens, grad_key) + tt(table, key_low)).astype(BF)
    grads_out[2 * model_width : 3 * model_width, :] = tn(tokens, grad_value).astype(BF)
    table_at = 3 * model_width
    grads_out[table_at : table_at + rel, :] = (
        tt(query_low, query_weight[...]) + tt(key_low, key_weight[...])
    ).astype(BF)
    small_at = table_at + rel
    grads_out[small_at:, :] = jnp.zeros((grads_out.shape[0] - small_at, model_width), BF)
    ones = jnp.ones((8, rel), BF)

    def lane_sums(values):
        high = values.astype(BF)
        low = (values - high.astype(F32)).astype(BF)
        return (nt(ones, high) + nt(ones, low))[0:1, :]

    small = [
        column_sum(grad_query[...]) + lane_sums(rel_query_grad),
        column_sum(grad_key) + lane_sums(rel_key_grad),
        column_sum(grad_value),
        jnp.zeros((13, model_width), F32),
    ]
    grads_out[small_at : small_at + 16, :] = jnp.concatenate(small, axis=0).astype(BF)
    grad_tokens_out[...] = (
        nt(grad_query[...], query_weight[...])
        + nt(grad_key, key_weight[...])
        + nt(grad_value, value_weight[...])
        + grad_first[...]
    )


def call(kernel, outs, scratch, *operands, scalars):
    in_specs = [pl.BlockSpec(memory_space=pltpu.SMEM)] * scalars
    in_specs += [pl.BlockSpec(memory_space=pltpu.VMEM)] * (len(operands) - scalars)
    return pl.pallas_call(
        kernel,
        out_shape=[jax.ShapeDtypeStruct(shape, kind) for shape, kind in outs],
        in_specs=in_specs,
        out_specs=[pl.BlockSpec(memory_space=pltpu.VMEM)] * len(outs),
        scratch_shapes=[pltpu.VMEM(shape, kind) for shape, kind in scratch],
        compiler_params=pltpu.CompilerParams(vmem_limit_bytes=VMEM_LIMIT),
    )(*operands)


def hop_table(blk_count, dp_count, bit_of):
    pairs = []
    for blk in range(blk_count):
        for dp in range(dp_count):
            axis, bit = bit_of(blk)
            there = (blk ^ bit, dp) if axis == 0 else (blk, dp ^ bit)
            pairs.append((blk * dp_count + dp, there[0] * dp_count + there[1]))
    return pairs


def all_sum(early, late, blk_count, dp_count):
    both = ("blk", "dp")
    blk, dp = lax.axis_index("blk"), lax.axis_index("dp")
    steps = [lambda b: (0, 1)]
    first, second = (0, 2), (1, 1)
    steps.append(lambda b: first if b % 2 == 0 else second)
    steps.append(lambda b: second if b % 2 == 0 else first)
    bit = 2
    while bit < dp_count:
        steps.append(lambda b, bit=bit: (1, bit))
        bit *= 2

    def my_bit(step):
        axis0, bit0 = step(0)
        axis1, bit1 = step(1)
        even = (blk if axis0 == 0 else dp) // bit0 % 2
        odd = (blk if axis1 == 0 else dp) // bit1 % 2
        return jnp.where(blk % 2 == 0, even, odd)

    def exchange(values, step):
        return lax.ppermute(values, both, hop_table(blk_count, dp_count, step))

    bit = my_bit(steps[0])

    def half(values, which):
        rows = values.shape[0] // 2
        return lax.dynamic_slice_in_dim(values, which * rows, rows, 0)

    early_in = exchange(half(early, 1 - bit), steps[0])
    late_in = exchange(half(late, 1 - bit), steps[0])
    mine = jnp.concatenate(
        [
            half(early, bit).astype(F32) + early_in.astype(F32),
            half(late, bit).astype(F32) + late_in.astype(F32),
        ],
        axis=0,
    )
    terms = [mine.astype(BF)]
    for step in steps[1:]:
        bit = my_bit(step)
        send = sum(half(t, 1 - bit).astype(F32) for t in terms).astype(BF)
        arrived = exchange(send, step)
        terms = [half(t, bit) for t in terms] + [arrived]
    held = sum(t.astype(F32) for t in terms).astype(BF)
    for step in reversed(steps[1:]):
        bit = my_bit(step)
        arrived = exchange(held, step)
        rows = held.shape[0]
        held = jnp.where(
            bit == 0, jnp.concatenate([held, arrived], axis=0), jnp.concatenate([arrived, held], axis=0)
        )
    bit = my_bit(steps[0])
    arrived = exchange(held, steps[0])
    low = jnp.where(bit == 0, held, arrived)
    high = jnp.where(bit == 0, arrived, held)
    cut = early.shape[0] // 2
    return (
        jnp.concatenate([low[:cut], high[:cut]], axis=0).astype(F32),
        jnp.concatenate([low[cut:], high[cut:]], axis=0).astype(F32),
    )


def on_device(
    blk_count, dp_count,
    tokens, lengths, query_weight, query_bias, key_weight, key_bias, value_weight, value_bias,
    output_weight, output_bias, first_gain, first_bias, inner_weight, inner_bias, outer_weight, outer_bias,
    second_gain, second_bias, relative_table, cotangent,
):
    seq_count, size, width = tokens.shape
    rel = relative_table.shape[0]
    inner_width = inner_weight.shape[1]
    own = tokens[0]
    block = lax.axis_index("blk").astype(jnp.int32).reshape(1)

    def along(values, bit):
        return lax.ppermute(values, "blk", [(i, i ^ bit) for i in range(blk_count)])

    def row(vector):
        return vector.reshape(1, -1)

    far = along(own, 2)
    core = along(own, 1)
    diagonal = along(far, 1)
    relative_back = jnp.flip(relative_table, 0)
    full = blk_count * size
    (
        layer_out, grad_first, chances, sent, query_all, key_all, value_all, rel_query, rel_key, early,
    ) = call(
        forward_kernel,
        [
            ((size, width), F32),
            ((size, width), F32),
            ((HEADS, size, full), BF),
            ((size, width + 128), BF),
            ((full, width), BF),
            ((full, width), BF),
            ((full, width), BF),
            ((rel, width), BF),
            ((rel, width), BF),
            ((EARLY_ROWS, width), BF),
        ],
        [
            ((full, width), BF),
            ((size, full), F32),
            ((size, width), F32),
            ((size, 128), F32),
            ((size, inner_width), BF),
            ((size, inner_width), F32),
        ],
        block, lengths, own, core, far, diagonal,
        query_weight, row(query_bias), key_weight, row(key_bias), value_weight, row(value_bias),
        output_weight, row(output_bias), row(first_gain), row(first_bias), inner_weight, row(inner_bias),
        outer_weight, row(outer_bias), row(second_gain), row(second_bias), relative_table, relative_back,
        cotangent[0],
        scalars=2,
    )
    sent_far = along(sent, 2)
    sent_core = along(sent, 1)
    sent_diagonal = along(sent, 3)
    shared_scratch = [
        ((3 * rel, width), BF),
        ((size, 3 * rel), BF),
        ((size, full), BF),
        ((size, width), BF),
        ((128, 3 * rel), F32),
        ((size, width), BF),
    ]
    grad_query, grad_rel_key = call(
        query_kernel,
        [((size, width), BF), ((width, rel), F32)],
        shared_scratch,
        block, chances, sent, query_all, key_all, value_all, rel_key,
        scalars=1,
    )
    grad_tokens, late = call(
        key_kernel,
        [((size, width), F32), ((LATE_ROWS, width), BF)],
        [((full, width + 128), BF), ((size, full), F32), ((size, full), BF)]
        + shared_scratch
        + [((size, width), BF), ((width, rel), F32), ((16, full), F32)],
        block, lengths, own, sent, sent_core, sent_far, sent_diagonal, query_all, key_all, value_all,
        rel_query, rel_key, grad_query, grad_rel_key, grad_first,
        query_weight, key_weight, value_weight, relative_table,
        scalars=2,
    )
    early, late = all_sum(early, late, blk_count, dp_count)
    inner_at, output_at = inner_width, 2 * inner_width
    small_at = output_at + width
    small = early[small_at : small_at + 16]
    late_at = 3 * width + rel
    late_small = late[late_at : late_at + 16]
    g_inner_weight = jnp.concatenate(
        [early[inner_at + k * width : inner_at + (k + 1) * width] for k in range(inner_width // width)], axis=1
    )
    chunks = inner_width // width
    return (
        layer_out[None],
        grad_tokens[None],
        late[0:width],
        late_small[0],
        late[width : 2 * width],
        late_small[1],
        late[2 * width : 3 * width],
        late_small[2],
        early[output_at : output_at + width],
        small[5 + chunks],
        small[3 + chunks],
        small[4 + chunks],
        g_inner_weight,
        small[3 : 3 + chunks].reshape(-1),
        early[0:inner_width],
        small[0],
        small[1],
        small[2],
        late[3 * width : 3 * width + rel],
    )


def solution(mesh):
    blk_count, dp_count = mesh.shape["blk"], mesh.shape["dp"]
    rows = P("dp", "blk", None)
    in_specs = (rows, P("dp")) + (P(),) * 17 + (rows,)
    out_specs = (rows, rows) + (P(),) * 17

    def whole(*arrays):
        return on_device(blk_count, dp_count, *arrays)

    return jax.shard_map(whole, mesh=mesh, in_specs=in_specs, out_specs=out_specs, check_vma=False)
```

```python
import math

import jax
import jax.numpy as jnp
from jax import lax
from jax.experimental import pallas as pl
from jax.experimental.pallas import tpu as pltpu
from jax.sharding import PartitionSpec as P

HEADS = 6
BF = jnp.bfloat16
F32 = jnp.float32
LOG2E = math.log2(math.e)
EPS = 1e-07
VMEM_LIMIT = 28 * 1024 * 1024
FIRST_PAIRS = 2
EARLY_ROWS = 3584
LATE_ROWS = 2048


def nn(left, right):
    return lax.dot_general(left, right, (((1,), (0,)), ((), ())), preferred_element_type=F32)


def nt(left, right):
    return lax.dot_general(left, right, (((1,), (1,)), ((), ())), preferred_element_type=F32)


def tn(left, right):
    return lax.dot_general(left, right, (((0,), (0,)), ((), ())), preferred_element_type=F32)


def tt(left, right):
    return lax.dot_general(left, right, (((0,), (1,)), ((), ())), preferred_element_type=F32)


def lanes(shape):
    return lax.broadcasted_iota(jnp.int32, shape, len(shape) - 1)


def of_head(values, head):
    inside = (lanes(values.shape) // 64) == head
    return jnp.where(inside, values, jnp.zeros_like(values))


def pair_columns(pair):
    return pl.ds(pl.multiple_of(pair * 128, 128), 128)


def wide(column, width):
    return jnp.broadcast_to(column, (column.shape[0], width))


def reversal(size):
    rows = lax.broadcasted_iota(jnp.int32, (size, size), 0)
    cols = lax.broadcasted_iota(jnp.int32, (size, size), 1)
    return jnp.where(rows + cols == size - 1, 1.0, 0.0).astype(BF)


def place_blocks(block, x_all, own, core, far, diagonal):
    size = own.shape[0]
    even = block % 2 == 0
    core_at = jnp.where(even, 2 * size, 0)
    diagonal_at = jnp.where(even, 0, 2 * size)
    x_all[pl.ds(size, size), :] = own[...]
    x_all[pl.ds(3 * size, size), :] = far[...]
    x_all[pl.ds(pl.multiple_of(core_at, size), size), :] = core[...]
    x_all[pl.ds(pl.multiple_of(diagonal_at, size), size), :] = diagonal[...]


def position_terms(block, s_ref, own_rows, own_table, others, other_table, own_shift, other_shift):
    size = own_rows.shape[0]
    rel = own_table.shape[0]
    scores = nt(own_rows, own_table)
    last, first = scores[:, rel - 1 : rel], scores[:, 0:1]
    source = jnp.concatenate([scores, wide(last, size), wide(first, size)], axis=1)
    rolled = pltpu.roll(source, own_shift, 1, stride=1, stride_axis=0)
    for slot in range(3):
        rows = others(slot)
        if slot == 0:
            part = nt(rows, other_table[size:, :])
            part = jnp.concatenate([part, wide(part[:, size - 1 : size], size)], axis=1)
        elif slot == 1:
            part = nt(rows, other_table)
        else:
            part = nt(rows, other_table[:size, :])
            part = jnp.concatenate([wide(part[:, 0:1], size), part], axis=1)
        part = pltpu.roll(part, other_shift, 1, stride=1, stride_axis=0)[:, size:]
        span = slice(slot * size, (slot + 1) * size)
        s_ref[:, span] = rolled[:, span] + part.T
    low_half = block < 2
    constant = jnp.where(low_half, last, first)

    def constant_terms(slot):
        rows = others(slot)
        top = nt(other_table[0:16, :], rows)[0:1, :]
        bottom = nt(other_table[rel - 16 : rel, :], rows)[15:16, :]
        return constant + jnp.where(low_half, top, bottom)

    s_ref[:, 3 * size :] = constant_terms(3)

    @pl.when(block == 0)
    def _():
        s_ref[:, :size] = constant_terms(0)

    @pl.when(block == 3)
    def _():
        s_ref[:, 2 * size : 3 * size] = constant_terms(2)


def extend_table(block, ext_ref, table_ref):
    rel = table_ref.shape[0]
    half = rel // 2
    width = table_ref.shape[1]
    first, last = table_ref[0:1, :], table_ref[rel - 1 : rel, :]
    ext_ref[0:rel, :] = table_ref[...]
    ext_ref[rel : rel + half, :] = jnp.broadcast_to(last, (half, width))
    ext_ref[rel + half : 2 * rel, :] = jnp.broadcast_to(first, (half, width))
    far = jnp.where(block < 2, last.astype(F32), first.astype(F32)).astype(BF)
    ext_ref[2 * rel : 3 * rel, :] = jnp.broadcast_to(far, (rel, width))


def unskewed(block, wall_ref, near_ref, grad_rows, shift):
    size = grad_rows.shape[0]
    near_ref[:, : 3 * size] = grad_rows[:, : 3 * size]
    near_ref[:, 3 * size :] = jnp.zeros((size, size), BF)
    wall_ref[:, 4 * size : 5 * size] = grad_rows[:, 3 * size :]
    wall_ref[:, 5 * size :] = jnp.zeros((size, size), BF)

    @pl.when(block == 0)
    def _():
        wall_ref[:, 5 * size :] = near_ref[:, :size]
        near_ref[:, :size] = jnp.zeros((size, size), BF)

    @pl.when(block == 3)
    def _():
        wall_ref[:, 5 * size :] = near_ref[:, 2 * size : 3 * size]
        near_ref[:, 2 * size : 3 * size] = jnp.zeros((size, size), BF)

    wall_ref[:, : 4 * size] = pltpu.roll(near_ref[...], shift, 1, stride=1, stride_axis=0)


def table_grad(block, sums, scale):
    rel = sums.shape[1] // 3
    half = rel // 2
    over = jnp.sum(sums[:, rel : rel + half], axis=1, keepdims=True)
    under = jnp.sum(sums[:, rel + half : 2 * rel], axis=1, keepdims=True)
    far = jnp.sum(sums[:, 2 * rel :], axis=1, keepdims=True)
    over = over + jnp.where(block < 2, far, 0.0)
    under = under + jnp.where(block < 2, 0.0, far)
    at = lanes((sums.shape[0], rel))
    folded = sums[:, :rel] + jnp.where(at == rel - 1, over, 0.0) + jnp.where(at == 0, under, 0.0)
    return folded * scale


def as_row(vector_ref):
    return vector_ref[...].astype(F32).reshape(1, -1)


def affine(values, weight_ref, bias_ref):
    return nn(values, weight_ref[...]) + as_row(bias_ref)


def norm_forward(values):
    center = values - jnp.mean(values, axis=-1, keepdims=True)
    spread = jnp.mean(center * center, axis=-1, keepdims=True)
    rate = lax.rsqrt(spread + EPS)
    return center * rate, rate


def norm_backward(grad_hat, hat, rate):
    mean_grad = jnp.mean(grad_hat, axis=-1, keepdims=True)
    mean_along = jnp.mean(grad_hat * hat, axis=-1, keepdims=True)
    return rate * (grad_hat - mean_grad - hat * mean_along)


def column_sum(values):
    return jnp.sum(values.astype(F32), axis=0, keepdims=True)


def forward_kernel(
    block_ref, length_ref, relative, query_weight, key_weight, own, core, far, diagonal, value_weight,
    output_weight, inner_weight, outer_weight, cotangent,
    query_bias, key_bias, value_bias, output_bias, first_gain, first_bias, inner_bias, outer_bias,
    second_gain, second_bias,
    layer_store, first_store, chances_store, sent_store, query_store, key_store, value_store,
    rel_query_store, rel_key_store, early_send_low, early_send_high, early_keep,
    x_all, s_ref, mixture_ref, log_ref, active_ref, slope_ref, grads_out,
):
    block = block_ref[0]
    length = length_ref[0]
    size, model_width = layer_store.shape
    query_bias, key_bias, value_bias = ready(query_bias, key_bias, value_bias)
    head_dim = model_width // HEADS
    factor = LOG2E / math.sqrt(3.0 * head_dim)
    query_out, key_out, value_out = query_store.ref, key_store.ref, value_store.ref
    rel_query_out, rel_key_out = rel_query_store.ref, rel_key_store.ref
    chances_out, sent_out = chances_store.ref, sent_store.ref
    relative, query_weight, key_weight = ready(relative, query_weight, key_weight)
    rel_query_out[...] = affine(relative[...], query_weight, query_bias).astype(BF)
    rel_query_store.push()
    rel_key_out[...] = affine(
        nn(reversal(relative.shape[0]), relative[...]).astype(BF), key_weight, key_bias
    ).astype(BF)
    rel_key_store.push()
    own, core, far, diagonal = ready(own, core, far, diagonal)
    place_blocks(block, x_all, own, core, far, diagonal)
    query_out[...] = affine(x_all[...], query_weight, query_bias).astype(BF)
    query_store.push()
    key_out[...] = affine(x_all[...], key_weight, key_bias).astype(BF)
    key_store.push()
    (value_weight,) = ready(value_weight)
    value_out[...] = affine(x_all[...], value_weight, value_bias).astype(BF)
    value_store.push()
    step = lanes((1, 4 * size))
    position = ((block + 3 + step // size) % 4) * size + step % size
    mask_row = jnp.where(position < length, 0.0, -1e30)
    stat_lane = lanes((size, 128))
    log_ref[...] = jnp.zeros_like(log_ref)

    def pair_step(pair, carry):
        columns = pair_columns(pair)
        total = jnp.zeros((size, 128), F32)
        for side in range(2):
            head = 2 * pair + side
            query_own = of_head(query_out[size : 2 * size, columns], side)
            position_terms(
                block,
                s_ref,
                query_own,
                rel_key_out[:, columns],
                lambda slot: key_out[slot * size : (slot + 1) * size, columns],
                of_head(rel_query_out[:, columns], side),
                1,
                0,
            )
            content = nt(query_own, key_out[:, columns])
            s_ref[...] = (s_ref[...] + content) * factor + mask_row
            top = jnp.max(s_ref[...], axis=1, keepdims=True)
            raised = jnp.exp2(s_ref[...] - top)
            s_ref[...] = raised
            row_sum = jnp.sum(raised, axis=1, keepdims=True)
            chances = (s_ref[...] * (1.0 / row_sum)).astype(BF)
            chances_out[head] = chances
            log_total = top + jnp.log2(row_sum)
            log_ref[...] = jnp.where(stat_lane % 8 == head, log_total, log_ref[...])
            total = total + nn(chances, of_head(value_out[:, columns], side))
        mixture_ref[:, columns] = total
        return carry

    lax.fori_loop(0, HEADS // 2, pair_step, 0)

    output_weight, inner_weight, outer_weight, cotangent = ready(output_weight, inner_weight, outer_weight, cotangent)
    output_bias, first_gain, first_bias, inner_bias, outer_bias, second_gain, second_bias = ready(
        output_bias, first_gain, first_bias, inner_bias, outer_bias, second_gain, second_bias
    )
    inner_width = inner_weight.shape[1]
    chunks = inner_width // model_width
    mixture_low = mixture_ref[...].astype(BF)
    first_sum = own[...].astype(F32) + affine(mixture_low, output_weight, output_bias)
    first_hat, first_rate = norm_forward(first_sum)
    normed = (first_hat * as_row(first_gain) + as_row(first_bias)).astype(BF)
    root_half = math.sqrt(0.5)
    density = 1.0 / math.sqrt(2.0 * math.pi)

    inner_row = as_row(inner_bias)
    second_sum = normed.astype(F32) + as_row(outer_bias)
    for chunk in range(chunks):
        span = slice(chunk * model_width, (chunk + 1) * model_width)
        inner_pre = nn(normed, inner_weight[:, span]) + inner_row[:, span]
        below = 0.5 + 0.5 * lax.erf(inner_pre * root_half)
        slope_ref[:, span] = below + inner_pre * density * jnp.exp(-0.5 * inner_pre * inner_pre)
        active_ref[:, span] = (inner_pre * below).astype(BF)
        second_sum = second_sum + nn(active_ref[:, span], outer_weight[span, :])
    second_hat, second_rate = norm_forward(second_sum)
    gain = as_row(second_gain)
    layer_store.ref[...] = second_hat * gain + as_row(second_bias)
    layer_store.push()
    cot = cotangent[...].astype(F32)
    grad_second = norm_backward(cot * gain, second_hat, second_rate)
    grad_outer = grad_second.astype(BF)
    outer_at, inner_at, output_at, small_at = 0, inner_width, 2 * inner_width, 2 * inner_width + model_width
    grads_out[small_at + 16 :, :] = jnp.zeros((grads_out.shape[0] - small_at - 16, model_width), BF)
    small = [column_sum(grad_outer), column_sum(cot * second_hat), column_sum(cot)]
    grad_normed = grad_second
    for chunk in range(chunks):
        span = slice(chunk * model_width, (chunk + 1) * model_width)
        grads_out[outer_at + chunk * model_width : outer_at + (chunk + 1) * model_width, :] = tn(
            active_ref[:, span], grad_outer
        ).astype(BF)
        grad_inner = (nt(grad_outer, outer_weight[span, :]) * slope_ref[:, span]).astype(BF)
        small.append(column_sum(grad_inner))
        grads_out[inner_at + chunk * model_width : inner_at + (chunk + 1) * model_width, :] = tn(
            normed, grad_inner
        ).astype(BF)
        grad_normed = grad_normed + nt(grad_inner, inner_weight[:, span])
    grad_normed = grad_normed.astype(BF).astype(F32)
    grad_first = norm_backward(grad_normed * as_row(first_gain), first_hat, first_rate)
    first_store.ref[...] = grad_first
    first_store.push()
    grad_branch = grad_first.astype(BF)
    grads_out[output_at : output_at + model_width, :] = tn(mixture_low, grad_branch).astype(BF)
    small += [column_sum(grad_normed * first_hat), column_sum(grad_normed), column_sum(grad_branch)]
    small += [jnp.zeros((16 - len(small), model_width), F32)]
    grads_out[small_at : small_at + 16, :] = jnp.concatenate(small, axis=0).astype(BF)
    push_halves(block % 2, grads_out, (early_send_low, early_send_high), early_keep)
    grad_mixture = nt(grad_branch, output_weight[...]).astype(BF)
    sent_out[:, :model_width] = grad_mixture
    along = grad_mixture.astype(F32) * mixture_ref[...]
    stats = jnp.where(stat_lane < 16, 0.0, log_ref[...])
    for head in range(HEADS):
        columns = slice((head // 2) * 128, (head // 2 + 1) * 128)
        delta = jnp.sum(of_head(along[:, columns], head % 2), axis=1, keepdims=True)
        stats = jnp.where((stat_lane == head) | (stat_lane == 8 + head), delta, stats)
    upper = stats.astype(BF).astype(F32)
    rest = stats - upper
    middle = rest.astype(BF).astype(F32)
    group = stat_lane // 8
    parts = jnp.where((group == 0) | (group == 2), upper, jnp.where((group == 1) | (group == 3), middle, rest - middle))
    sent_out[:, model_width:] = jnp.where(group < 5, parts, 0.0).astype(BF)
    sent_store.push()


def position_backward(block, side, grad_scores, flip, other_pair, ext_pair, own_rows_back, wall_ref, near_ref, shift):
    grad_back = nn(flip, grad_scores).astype(BF)
    unskewed(block, wall_ref, near_ref, grad_back, shift)
    row_grad = nn(grad_back, of_head(other_pair, side)) + nn(wall_ref[...], of_head(ext_pair, side))
    return row_grad, tn(of_head(own_rows_back, side), wall_ref[...])


def query_kernel(
    block_ref, rel_key, query_all, sent, value_all, key_all, chances_load,
    query_store, rel_key_grad_store,
    ext_ref, wall_ref, near_ref, back_ref, sum_ref, rows_ref,
):
    block = block_ref[0]
    size, model_width = query_store.shape
    scale = 1.0 / math.sqrt(3.0 * (model_width // HEADS))
    flip = reversal(size)
    chances = chances_load.buffer
    rel_key, query_all, sent, value_all, key_all = ready(rel_key, query_all, sent, value_all, key_all)
    extend_table(block, ext_ref, rel_key)
    back_ref[...] = nn(flip, query_all[size : 2 * size, :]).astype(BF)
    stats = sent[:, model_width:].astype(F32)
    stat_lane = lanes((size, 128))

    def pair_step(pair, carry):
        columns = pair_columns(pair)
        row_grad = jnp.zeros((size, 128), F32)
        for side in range(2):
            head = 2 * pair + side
            delta = jnp.sum(
                jnp.where((stat_lane == head) | (stat_lane == 8 + head), stats, 0.0), axis=1, keepdims=True
            )
            grad_mixture = of_head(sent[:, columns], side)
            grad_chances = nt(grad_mixture, value_all[:, columns])
            grad_scores = (chances[head].astype(F32) * (grad_chances - delta)).astype(BF)
            rows, table = position_backward(
                block, side, grad_scores, flip, key_all[:, columns], ext_ref[:, columns],
                back_ref[:, columns], wall_ref, near_ref, 3 * size,
            )
            row_grad = row_grad + rows
            if side == 0:
                sum_ref[...] = table
            else:
                sum_ref[...] += table
        rows_ref[:, columns] = (row_grad * scale).astype(BF)
        rel_key_grad_store.ref[columns, :] = table_grad(block, sum_ref[...], scale)
        return carry

    lax.fori_loop(0, HEADS // 2, pair_step, 0)
    query_store.ref[...] = nn(flip, rows_ref[...]).astype(BF)


def key_pairs(
    first, last, block_ref, length_ref, rel_query, key_all, rel_key, query_all, value_all,
    sent_own, sent_core, sent_far, sent_diagonal, key_rows_ref, value_rows_ref, rel_grad_ref,
    sent_ref, s_ref, grad_ref, ext_ref, wall_ref, near_ref, back_ref, sum_ref, stat_ref,
):
    block = block_ref[0]
    length = length_ref[0]
    size, model_width = key_rows_ref.shape
    scale = 1.0 / math.sqrt(3.0 * (model_width // HEADS))
    factor = LOG2E * scale
    flip = reversal(size)
    rel_query, key_all, rel_key, query_all, value_all = ready(rel_query, key_all, rel_key, query_all, value_all)
    extend_table(block, ext_ref, rel_query)
    back_ref[...] = nn(flip, key_all[size : 2 * size, :]).astype(BF)
    place_blocks(block, sent_ref, *ready(sent_own, sent_core, sent_far, sent_diagonal))
    stats = sent_ref[:, model_width:].astype(F32).T
    stat_ref[0:8, :] = stats[0:8, :] + stats[8:16, :]
    stat_ref[8:16, :] = stats[16:24, :] + (stats[24:32, :] + stats[32:40, :])
    position = block * size + lax.broadcasted_iota(jnp.int32, (size, 1), 0)
    mask_column = jnp.where(position < length, 0.0, -1e30)

    def pair_step(pair, carry):
        columns = pair_columns(pair)
        row_grad = jnp.zeros((size, 128), F32)
        value_grad = jnp.zeros((size, 128), F32)
        for side in range(2):
            head = 2 * pair + side
            key_head = of_head(key_all[size : 2 * size, columns], side)
            position_terms(
                block,
                s_ref,
                key_head,
                rel_query[:, columns],
                lambda slot: query_all[slot * size : (slot + 1) * size, columns],
                of_head(rel_key[:, columns], side),
                0,
                1,
            )
            content = nt(key_head, query_all[:, columns])
            shift = mask_column - stat_ref[pl.ds(8 + head, 1), :]
            s_ref[...] = jnp.exp2((s_ref[...] + content) * factor + shift)
            value_grad = value_grad + nn(s_ref[...].astype(BF), of_head(sent_ref[:, columns], side))
            grad_chances = nt(of_head(value_all[size : 2 * size, columns], side), sent_ref[:, columns])
            grad_ref[...] = (s_ref[...] * (grad_chances - stat_ref[pl.ds(head, 1), :])).astype(BF)
            rows, table = position_backward(
                block, side, grad_ref[...], flip, query_all[:, columns], ext_ref[:, columns],
                back_ref[:, columns], wall_ref, near_ref, 3 * size + 1,
            )
            row_grad = row_grad + rows
            if side == 0:
                sum_ref[...] = table
            else:
                sum_ref[...] += table
        key_rows_ref[:, columns] = (row_grad * scale).astype(BF)
        value_rows_ref[:, columns] = value_grad.astype(BF)
        rel_grad_ref[columns, :] = table_grad(block, sum_ref[...], scale)
        return carry

    lax.fori_loop(first, last, pair_step, 0)


def first_key_kernel(*refs):
    ins, outs, scratch = refs[:11], refs[11:14], refs[14:]
    key_pairs(0, FIRST_PAIRS, *ins, *(out.ref for out in outs), *scratch)


def last_key_kernel(*refs):
    ins, before, outs, scratch = refs[:11], refs[11:14], refs[14:17], refs[17:]
    done = FIRST_PAIRS * 128
    for old, out in zip(ready(*before), outs):
        if out.shape[0] == outs[0].shape[0]:
            out.ref[:, :done] = old[:, :done]
        else:
            out.ref[:done, :] = old[:done, :]
    key_pairs(FIRST_PAIRS, HEADS // 2, *ins, *(out.ref for out in outs), *scratch)


def final_kernel(
    block_ref, own, relative, key_rows, value_rows, rel_grad, grad_query, grad_rel_key, query_weight, key_weight,
    value_weight, grad_first, tokens_store, late_send_low, late_send_high, late_keep, grads_out,
):
    size, model_width = tokens_store.shape
    own, relative, key_rows_ref, value_rows_ref, rel_grad_ref, grad_query, grad_rel_key = ready(
        own, relative, key_rows, value_rows, rel_grad, grad_query, grad_rel_key
    )
    rel = relative.shape[0]
    grad_key = nn(reversal(size), key_rows_ref[...]).astype(BF)
    grad_value = value_rows_ref[...]
    rel_query_grad = rel_grad_ref[...]
    rel_key_grad = grad_rel_key[...]
    query_low = rel_query_grad.astype(BF)
    key_low = nn(rel_key_grad.astype(BF), reversal(rel)).astype(BF)
    tokens = own[...]
    table = relative[...]
    grads_out[0:model_width, :] = (tn(tokens, grad_query[...]) + tt(table, query_low)).astype(BF)
    grads_out[model_width : 2 * model_width, :] = (tn(tokens, grad_key) + tt(table, key_low)).astype(BF)
    grads_out[2 * model_width : 3 * model_width, :] = tn(tokens, grad_value).astype(BF)
    table_at = 3 * model_width
    query_weight, key_weight, value_weight, grad_first = ready(query_weight, key_weight, value_weight, grad_first)
    grads_out[table_at : table_at + rel, :] = (
        tt(query_low, query_weight[...]) + tt(key_low, key_weight[...])
    ).astype(BF)
    small_at = table_at + rel
    grads_out[small_at + 16 :, :] = jnp.zeros((grads_out.shape[0] - small_at - 16, model_width), BF)
    ones = jnp.ones((8, rel), BF)

    def lane_sums(values):
        high = values.astype(BF)
        low = (values - high.astype(F32)).astype(BF)
        return (nt(ones, high) + nt(ones, low))[0:1, :]

    small = [
        column_sum(grad_query[...]) + lane_sums(rel_query_grad),
        column_sum(grad_key) + lane_sums(rel_key_grad),
        column_sum(grad_value),
        jnp.zeros((13, model_width), F32),
    ]
    grads_out[small_at : small_at + 16, :] = jnp.concatenate(small, axis=0).astype(BF)
    push_halves(block_ref[0] % 2, grads_out, (late_send_low, late_send_high), late_keep)
    tokens_store.ref[...] = (
        nt(grad_query[...], query_weight[...])
        + nt(grad_key, key_weight[...])
        + nt(grad_value, value_weight[...])
        + grad_first[...]
    )


class Load:
    def __init__(self, source, buffer, sem):
        self.copy, self.buffer, self.waiting = pltpu.make_async_copy(source, buffer, sem), buffer, True
        self.copy.start()

    def ready(self):
        if self.waiting:
            self.copy.wait()
        self.waiting = False
        return self.buffer


def ready(*loads):
    return [load.ready() for load in loads]


class Store:
    def __init__(self, target, buffer, sem):
        self.copy, self.ref, self.shape, self.waiting = pltpu.make_async_copy(buffer, target, sem), buffer, buffer.shape, False

    def push(self):
        self.copy.start()
        self.waiting = True

    def finish(self):
        if not self.waiting:
            self.push()
        self.copy.wait()


class Here:
    def __init__(self, ref):
        self.ref = self.buffer = ref
        self.shape = ref.shape

    def ready(self):
        return self.ref

    def push(self):
        pass

    def finish(self):
        pass


class Raw:
    def __init__(self, target, sem):
        self.target, self.sem = target, sem
        self.shape = target.shape

    def push_from(self, source):
        self.copy = pltpu.make_async_copy(source, self.target, self.sem)
        self.copy.start()

    def finish(self):
        self.copy.wait()


def push_halves(core, rows_ref, sends, keep):
    half = keep.shape[0]
    for k, send in enumerate(sends):
        at = (1 - core) * half + k * send.shape[0]
        send.push_from(rows_ref.at[pl.ds(pl.multiple_of(at, 16), send.shape[0])])
    keep.push_from(rows_ref.at[pl.ds(pl.multiple_of(core * half, 16), half)])


class Kept:
    def __init__(self, *what):
        self.what = what


def call(kernel, outs, scratch, *operands, scalars, micros):
    kept_in = [isinstance(operand, Kept) for operand in operands]
    kept_out = [isinstance(out, Kept) for out in outs]
    operands = [
        operand if k < scalars
        else pltpu.with_memory_space_constraint(operand.what[0], pltpu.VMEM) if kept
        else pltpu.with_memory_space_constraint(operand, pltpu.HBM)
        for k, (operand, kept) in enumerate(zip(operands, kept_in))
    ]
    outs = [out.what if kept else out for out, kept in zip(outs, kept_out)]
    raw = [len(out) > 2 for out in outs]
    loads = [k for k in range(scalars, len(operands)) if not kept_in[k]]
    stores = [k for k in range(len(outs)) if not kept_out[k]]
    buffered = [k for k in stores if not raw[k]]

    def body(*refs):
        n, m = len(operands), len(outs)
        ins, results, rest = list(refs[:n]), list(refs[n : n + m]), list(refs[n + m :])
        in_sems, out_sems = rest.pop(), rest.pop()
        buffers = [rest.pop() for _ in range(len(loads) + len(buffered))][::-1]
        for k in range(scalars, n):
            if kept_in[k]:
                ins[k] = Here(ins[k])
        for place, k in enumerate(loads):
            ins[k] = Load(ins[k], buffers[place], in_sems.at[place])
        buffers = buffers[len(loads) :]
        for k in range(m):
            if kept_out[k]:
                results[k] = Here(results[k])
        for place, k in enumerate(stores):
            if raw[k]:
                results[k] = Raw(results[k], out_sems.at[place])
            else:
                results[k] = Store(results[k], buffers.pop(0), out_sems.at[place])
        kernel(*ins, *results, *rest)
        for k in stores:
            results[k].finish()

    spaces = [
        pltpu.SMEM if k < scalars else pltpu.VMEM if kept_in[k] else pltpu.HBM for k in range(len(operands))
    ]
    buffers = [(operands[k].shape, operands[k].dtype) for k in loads] + [outs[k][:2] for k in buffered]
    return pl.pallas_call(
        body,
        out_shape=[
            pltpu.VMEM(out[0], out[1]) if kept else pltpu.HBM(out[0], out[1])
            for out, kept in zip(outs, kept_out)
        ],
        in_specs=[pl.BlockSpec(memory_space=space) for space in spaces],
        out_specs=[pl.BlockSpec(memory_space=pltpu.VMEM if kept else pltpu.HBM) for kept in kept_out],
        scratch_shapes=[pltpu.VMEM(shape, kind) for shape, kind in list(scratch) + buffers]
        + [pltpu.SemaphoreType.DMA((max(len(stores), 1),)), pltpu.SemaphoreType.DMA((max(len(loads), 1),))],
        compiler_params=pltpu.CompilerParams(vmem_limit_bytes=VMEM_LIMIT),
        cost_estimate=pl.CostEstimate(flops=micros * 10**9, bytes_accessed=micros * 10**6, transcendentals=0),
    )(*operands)


class Group:
    def __init__(self, blk_count, dp_count, bits):
        self.blk_count, self.dp_count, self.bits = blk_count, dp_count, bits
        self.size = 2 ** len(bits)
        place = {"blk": lax.axis_index("blk"), "dp": lax.axis_index("dp")}
        self.digits = [(place[axis] >> (bit.bit_length() - 1)) & 1 for axis, bit in bits]
        self.me = sum(digit << k for k, digit in enumerate(self.digits))

    def pairs(self, mask):
        change = {"blk": 0, "dp": 0}
        for k, (axis, bit) in enumerate(self.bits):
            if mask >> k & 1:
                change[axis] |= bit
        return [
            (blk * self.dp_count + dp, (blk ^ change["blk"]) * self.dp_count + (dp ^ change["dp"]))
            for blk in range(self.blk_count)
            for dp in range(self.dp_count)
        ]

    def send(self, values, mask):
        return lax.ppermute(values, ("blk", "dp"), self.pairs(mask))

    def scatter(self, terms):
        def part(index):
            return [
                (array, first + index * (blocks // self.size), blocks // self.size) for array, first, blocks in terms
            ]

        outs = [total(part(self.me ^ mask)) for mask in range(1, self.size)]
        arrived = [self.send(out, mask + 1) for mask, out in enumerate(outs)]
        return outs, part(self.me) + [whole(array) for array in arrived]

    def pieces(self, held):
        return [held] + [self.send(held, mask) for mask in range(1, self.size)]

    def gather(self, held):
        parts = self.pieces(held)
        for k, digit in enumerate(self.digits):
            parts = [
                jnp.where(digit == 0, parts[q], parts[q ^ (1 << k)]) for q in range(self.size)
            ]
        return jnp.concatenate(parts, axis=0)


def groups_of(blk_count, dp_count):
    bits, bit = [], 2
    while bit < dp_count:
        bits.append(("dp", bit))
        bit *= 2
    groups = [[("blk", 1)], [("blk", 2), ("dp", 1)]]
    groups += [bits[k : k + 2] for k in range(0, len(bits), 2)]
    return [Group(blk_count, dp_count, group) for group in groups]


def whole(array):
    return array, 0, array.shape[0]


def total(terms):
    spans = []
    for array, first, blocks in terms:
        if isinstance(array, tuple):
            low, high = array
            size = low.shape[0]
            low = lax.dynamic_slice_in_dim(low, jnp.minimum(first, size - blocks), blocks, 0)
            high = lax.dynamic_slice_in_dim(high, jnp.maximum(first - size, 0), blocks, 0)
            spans.append(jnp.where(first < size, low, high))
        else:
            spans.append(lax.dynamic_slice_in_dim(array, first, blocks, 0))
    return sum(span.astype(F32) for span in spans).astype(BF)


def in_order(first, then):
    return lax.optimization_barrier((first, then))[1]


def halves_to_scratch(core_ref, held, arrived, both_ref):
    held, arrived = ready(held, arrived)
    rows = held.shape[0]
    mine = pl.multiple_of(core_ref[0] * rows, 16)
    theirs = pl.multiple_of((1 - core_ref[0]) * rows, 16)
    both_ref[pl.ds(mine, rows), :] = held[...]
    both_ref[pl.ds(theirs, rows), :] = arrived[...]


def early_kernel(
    core_ref, held, arrived,
    outer_weight, inner_weight, output_weight, outer_bias, second_gain, second_bias, inner_bias, first_gain, first_bias,
    output_bias,
    both_ref,
):
    halves_to_scratch(core_ref, held, arrived, both_ref)
    inner_width, width = outer_weight.shape
    chunks = inner_width // width
    outer_weight.ref[...] = both_ref[:inner_width, :].astype(F32)
    outer_weight.push()
    for chunk in range(chunks):
        at = inner_width + chunk * width
        inner_weight.ref[:, chunk * width : (chunk + 1) * width] = both_ref[at : at + width, :].astype(F32)
    at = 2 * inner_width
    output_weight.ref[...] = both_ref[at : at + width, :].astype(F32)
    output_weight.push()
    small = both_ref[at + width : at + width + 16, :].astype(F32)

    def vector(out, row):
        out.ref[...] = small[row, :]
        out.push()

    vector(outer_bias, 0)
    vector(second_gain, 1)
    vector(second_bias, 2)
    inner_bias.ref[...] = jnp.concatenate([small[3 + k : 4 + k, :] for k in range(chunks)], axis=1)[0, :]
    inner_bias.push()
    vector(first_gain, 3 + chunks)
    vector(first_bias, 4 + chunks)
    vector(output_bias, 5 + chunks)


def late_kernel(
    core_ref, held, arrived,
    query_weight, query_bias, key_weight, key_bias, value_weight, value_bias, relative,
    both_ref,
):
    halves_to_scratch(core_ref, held, arrived, both_ref)
    width = query_weight.shape[0]
    rel = relative.shape[0]
    for k, out in enumerate((query_weight, key_weight, value_weight)):
        out.ref[...] = both_ref[k * width : (k + 1) * width, :].astype(F32)
        out.push()
    at = 3 * width
    relative.ref[...] = both_ref[at : at + rel, :].astype(F32)
    small = both_ref[at + rel : at + rel + 16, :].astype(F32)
    query_bias.ref[...] = small[0, :]
    key_bias.ref[...] = small[1, :]
    value_bias.ref[...] = small[2, :]


def on_device(
    blk_count, dp_count,
    tokens, lengths, query_weight, query_bias, key_weight, key_bias, value_weight, value_bias,
    output_weight, output_bias, first_gain, first_bias, inner_weight, inner_bias, outer_weight, outer_bias,
    second_gain, second_bias, relative_table, cotangent,
):
    seq_count, size, width = tokens.shape
    rel = relative_table.shape[0]
    inner_width = inner_weight.shape[1]
    own = tokens[0]
    block = lax.axis_index("blk").astype(jnp.int32).reshape(1)
    groups = groups_of(blk_count, dp_count)
    chips = groups[1:]
    shards = blk_count * dp_count

    def along(values, bit):
        return lax.ppermute(values, "blk", [(i, i ^ bit) for i in range(blk_count)])

    def blocks(rows, share):
        return rows.reshape(shards // share, -1, width)

    def first_terms(keep, low, high):
        arrived = tuple(groups[0].send(blocks(piece, 4), 1) for piece in (low, high))
        return [whole(blocks(keep, 2)), (arrived, 0, shards // 2)]

    def flat(values):
        return values.reshape(-1, width)

    far = along(own, 2)
    core = along(own, 1)
    diagonal = along(far, 1)
    full = blk_count * size
    (
        layer_out, grad_first, chances, sent, query_all, key_all, value_all, rel_query, rel_key,
        early_send_low, early_send_high, early_keep,
    ) = call(
        forward_kernel,
        [
            ((size, width), F32),
            Kept((size, width), F32),
            Kept((HEADS, size, full), BF),
            Kept((size, width + 128), BF),
            Kept((full, width), BF),
            Kept((full, width), BF),
            Kept((full, width), BF),
            Kept((rel, width), BF),
            Kept((rel, width), BF),
            ((EARLY_ROWS // 4, width), BF, "raw"),
            ((EARLY_ROWS // 4, width), BF, "raw"),
            ((EARLY_ROWS // 2, width), BF, "raw"),
        ],
        [
            ((full, width), BF),
            ((size, full), F32),
            ((size, width), F32),
            ((size, 128), F32),
            ((size, inner_width), BF),
            ((size, inner_width), F32),
            ((EARLY_ROWS, width), BF),
        ],
        block, lengths, relative_table, query_weight, key_weight, own, Kept(core), Kept(far), Kept(diagonal), value_weight,
        output_weight, inner_weight, outer_weight, cotangent[0],
        query_bias, key_bias, value_bias, output_bias, first_gain, first_bias, inner_bias, outer_bias,
        second_gain, second_bias,
        scalars=2, micros=27,
    )
    early_terms = first_terms(early_keep, early_send_low, early_send_high)
    sent_far = along(sent, 2)
    sent_core = along(sent, 1)
    sent_diagonal = along(sent, 3)
    position_scratch = [
        ((3 * rel, width), BF),
        ((size, 3 * rel), BF),
        ((size, full), BF),
        ((size, width), BF),
        ((128, 3 * rel), F32),
    ]
    grad_query, grad_rel_key = call(
        query_kernel,
        [Kept((size, width), BF), Kept((width, rel), F32)],
        position_scratch + [((size, width), BF)],
        block, *map(Kept, (rel_key, query_all, sent, value_all, key_all, chances)),
        scalars=1, micros=8,
    )
    key_scratch = (
        [((full, width + 128), BF), ((size, full), F32), ((size, full), BF)] + position_scratch + [((16, full), F32)]
    )
    key_arrays = tuple(
        map(Kept, (rel_query, key_all, rel_key, query_all, value_all, sent, sent_core, sent_far, sent_diagonal))
    )
    key_outs = [Kept((size, width), BF), Kept((size, width), BF), Kept((width, rel), F32)]
    sending, early_terms = chips[0].scatter(early_terms)
    key_rows, value_rows, rel_grad = call(
        first_key_kernel, key_outs, key_scratch, in_order(sending, block), lengths, *key_arrays,
        scalars=2, micros=13,
    )
    for group in chips[1:]:
        sending, early_terms = group.scatter(early_terms)
    key_parts = call(
        last_key_kernel, key_outs, key_scratch, in_order(sending, block), lengths, *key_arrays,
        *map(Kept, (key_rows, value_rows, rel_grad)), scalars=2, micros=8,
    )
    early_held = total(early_terms)
    grad_tokens, late_send_low, late_send_high, late_keep = call(
        final_kernel,
        [((size, width), F32)] + [((LATE_ROWS // 4, width), BF, "raw")] * 2 + [((LATE_ROWS // 2, width), BF, "raw")],
        [((LATE_ROWS, width), BF)],
        in_order(early_held, block), own, relative_table, *map(Kept, (*key_parts, grad_query, grad_rel_key)), query_weight,
        key_weight, value_weight, Kept(grad_first),
        scalars=1, micros=4,
    )
    for group in reversed(chips[1:]):
        early_held = group.gather(early_held)
    late_terms = first_terms(late_keep, late_send_low, late_send_high)
    for group in chips:
        sending, late_terms = group.scatter(late_terms)
    early_held = chips[0].gather(in_order(sending, early_held))
    late_held = total(late_terms)
    for group in reversed(chips):
        late_held = group.gather(late_held)
    my_core = groups[0].me.astype(jnp.int32).reshape(1)
    square, vector = ((width, width), F32), ((width,), F32)
    (
        g_outer_weight, g_inner_weight, g_output_weight, g_outer_bias, g_second_gain, g_second_bias, g_inner_bias,
        g_first_gain, g_first_bias, g_output_bias,
    ) = call(
        early_kernel,
        [((inner_width, width), F32), ((width, inner_width), F32), square, vector, vector, vector,
         ((inner_width,), F32), vector, vector, vector],
        [((EARLY_ROWS, width), BF)],
        my_core, *(Kept(flat(piece)) for piece in groups[0].pieces(early_held)),
        scalars=1, micros=4,
    )
    (
        g_query_weight, g_query_bias, g_key_weight, g_key_bias, g_value_weight, g_value_bias, g_relative,
    ) = call(
        late_kernel,
        [square, vector, square, vector, square, vector, ((rel, width), F32)],
        [((LATE_ROWS, width), BF)],
        my_core, *(Kept(flat(piece)) for piece in groups[0].pieces(late_held)),
        scalars=1, micros=2,
    )
    return (
        layer_out[None], grad_tokens[None], g_query_weight, g_query_bias, g_key_weight, g_key_bias,
        g_value_weight, g_value_bias, g_output_weight, g_output_bias, g_first_gain, g_first_bias,
        g_inner_weight, g_inner_bias, g_outer_weight, g_outer_bias, g_second_gain, g_second_bias, g_relative,
    )


def solution(mesh):
    blk_count, dp_count = mesh.shape["blk"], mesh.shape["dp"]
    rows = P("dp", "blk", None)
    in_specs = (rows, P("dp")) + (P(),) * 17 + (rows,)
    out_specs = (rows, rows) + (P(),) * 17

    def whole(*arrays):
        return on_device(blk_count, dp_count, *arrays)

    return jax.shard_map(whole, mesh=mesh, in_specs=in_specs, out_specs=out_specs, check_vma=False)
```

```python
import math

import jax
import jax.numpy as jnp
from jax import lax
from jax.experimental import pallas as pl
from jax.experimental.pallas import tpu as pltpu
from jax.sharding import PartitionSpec as P

HEADS = 6
BF = jnp.bfloat16
F32 = jnp.float32
LOG2E = math.log2(math.e)
EPS = 1e-07
VMEM_LIMIT = 28 * 1024 * 1024
FIRST_PAIRS = 2
EARLY_ROWS = 3584
LATE_ROWS = 1792


def nn(left, right):
    return lax.dot_general(left, right, (((1,), (0,)), ((), ())), preferred_element_type=F32)


def nt(left, right):
    return lax.dot_general(left, right, (((1,), (1,)), ((), ())), preferred_element_type=F32)


def tn(left, right):
    return lax.dot_general(left, right, (((0,), (0,)), ((), ())), preferred_element_type=F32)


def tt(left, right):
    return lax.dot_general(left, right, (((0,), (1,)), ((), ())), preferred_element_type=F32)


def lanes(shape):
    return lax.broadcasted_iota(jnp.int32, shape, len(shape) - 1)


def of_head(values, head):
    inside = (lanes(values.shape) // 64) == head
    return jnp.where(inside, values, jnp.zeros_like(values))


def pair_columns(pair):
    if isinstance(pair, int):
        return slice(pair * 128, (pair + 1) * 128)
    return pl.ds(pl.multiple_of(pair * 128, 128), 128)


def wide(column, width):
    return jnp.broadcast_to(column, (column.shape[0], width))


def reversal(size):
    rows = lax.broadcasted_iota(jnp.int32, (size, size), 0)
    cols = lax.broadcasted_iota(jnp.int32, (size, size), 1)
    return jnp.where(rows + cols == size - 1, 1.0, 0.0).astype(BF)


def place_blocks(block, x_all, own, core, far, diagonal):
    size = own.shape[0]
    even = block % 2 == 0
    core_at = jnp.where(even, 2 * size, 0)
    diagonal_at = jnp.where(even, 0, 2 * size)
    x_all[pl.ds(size, size), :] = own[...]
    x_all[pl.ds(3 * size, size), :] = far[...]
    x_all[pl.ds(pl.multiple_of(core_at, size), size), :] = core[...]
    x_all[pl.ds(pl.multiple_of(diagonal_at, size), size), :] = diagonal[...]


def rolled_window(source, shift):
    half = source.shape[0] // 2
    upper = pltpu.roll(source[:half, half:], shift, 1, stride=1, stride_axis=0)[:, half:]
    lower = pltpu.roll(source[half:, : 3 * half], shift, 1, stride=1, stride_axis=0)[:, half:]
    return jnp.concatenate([upper, lower], axis=0)


def own_terms(block, s_ref, own_rows, own_table, shift):
    size = own_rows.shape[0]
    rel = own_table.shape[0]
    scores = nt(own_rows, own_table)
    last, first = scores[:, rel - 1 : rel], scores[:, 0:1]
    source = jnp.concatenate([scores, wide(last, size), wide(first, size)], axis=1)
    s_ref[:, : 3 * size] = pltpu.roll(source, shift, 1, stride=1, stride_axis=0)[:, : 3 * size]
    constant = wide(jnp.where(block < 2, last, first), size)
    s_ref[:, 3 * size :] = constant

    @pl.when(block == 0)
    def _():
        s_ref[:, :size] = constant

    @pl.when(block == 3)
    def _():
        s_ref[:, 2 * size : 3 * size] = constant


def other_terms(block, s_ref, others, other_table, shift, slots):
    size = s_ref.shape[0]
    rel = other_table.shape[0]

    def near(slot):
        if slot == 0:
            part = nt(others(slot), other_table[size:, :])
            part = jnp.concatenate([part, wide(part[:, size - 1 : size], size)], axis=1)
        elif slot == 1:
            part = nt(others(slot), other_table)
        else:
            part = nt(others(slot), other_table[:size, :])
            part = jnp.concatenate([wide(part[:, 0:1], size), part], axis=1)
        s_ref[:, slot * size : (slot + 1) * size] += rolled_window(part, shift).T

    def constant(slot):
        rows = others(slot)
        top = nt(other_table[0:16, :], rows)[0:1, :]
        bottom = nt(other_table[rel - 16 : rel, :], rows)[15:16, :]
        s_ref[:, slot * size : (slot + 1) * size] += jnp.where(block < 2, top, bottom)

    for slot in slots:
        if slot == 1:
            near(1)
        elif slot == 3:
            constant(3)
        else:
            past = block == (0 if slot == 0 else 3)
            pl.when(past)(lambda: constant(slot))
            pl.when(jnp.logical_not(past))(lambda: near(slot))


def extend_table(block, ext_ref, table_ref):
    rel = table_ref.shape[0]
    half = rel // 2
    width = table_ref.shape[1]
    first, last = table_ref[0:1, :], table_ref[rel - 1 : rel, :]
    ext_ref[0:rel, :] = table_ref[...]
    ext_ref[rel : rel + half, :] = jnp.broadcast_to(last, (half, width))
    ext_ref[rel + half : 2 * rel, :] = jnp.broadcast_to(first, (half, width))
    far = jnp.where(block < 2, last.astype(F32), first.astype(F32)).astype(BF)
    ext_ref[2 * rel : 3 * rel, :] = jnp.broadcast_to(far, (rel, width))


def unskewed(block, wall_ref, near_ref, grad_rows, shift):
    size = grad_rows.shape[0]
    near_ref[:, : 3 * size] = grad_rows[:, : 3 * size]
    near_ref[:, 3 * size :] = jnp.zeros((size, size), BF)
    wall_ref[:, 4 * size : 5 * size] = grad_rows[:, 3 * size :]
    wall_ref[:, 5 * size :] = jnp.zeros((size, size), BF)

    @pl.when(block == 0)
    def _():
        wall_ref[:, 5 * size :] = near_ref[:, :size]
        near_ref[:, :size] = jnp.zeros((size, size), BF)

    @pl.when(block == 3)
    def _():
        wall_ref[:, 5 * size :] = near_ref[:, 2 * size : 3 * size]
        near_ref[:, 2 * size : 3 * size] = jnp.zeros((size, size), BF)

    wall_ref[:, : 4 * size] = pltpu.roll(near_ref[...], shift, 1, stride=1, stride_axis=0)


def table_grad(block, sums, scale):
    rel = sums.shape[1] // 3
    half = rel // 2
    over = jnp.sum(sums[:, rel : rel + half], axis=1, keepdims=True)
    under = jnp.sum(sums[:, rel + half : 2 * rel], axis=1, keepdims=True)
    far = jnp.sum(sums[:, 2 * rel :], axis=1, keepdims=True)
    over = over + jnp.where(block < 2, far, 0.0)
    under = under + jnp.where(block < 2, 0.0, far)
    at = lanes((sums.shape[0], rel))
    folded = sums[:, :rel] + jnp.where(at == rel - 1, over, 0.0) + jnp.where(at == 0, under, 0.0)
    return folded * scale


def as_row(vector_ref):
    return vector_ref[...].astype(F32).reshape(1, -1)


def affine(values, weight_ref, bias_ref):
    return nn(values, weight_ref[...]) + as_row(bias_ref)


def norm_forward(values):
    center = values - jnp.mean(values, axis=-1, keepdims=True)
    spread = jnp.mean(center * center, axis=-1, keepdims=True)
    rate = lax.rsqrt(spread + EPS)
    return center * rate, rate


def norm_backward(grad_hat, hat, rate):
    mean_grad = jnp.mean(grad_hat, axis=-1, keepdims=True)
    mean_along = jnp.mean(grad_hat * hat, axis=-1, keepdims=True)
    return rate * (grad_hat - mean_grad - hat * mean_along)


def column_sum(values):
    return jnp.sum(values.astype(F32), axis=0, keepdims=True)


def first_kernel(
    block_ref, relative, query_weight, key_weight, query_bias, key_bias, own, value_weight,
    value_bias, *rest,
):
    rel_query_store, rel_key_store, *terms_stores, query_ref, key_ref = rest
    block = block_ref[0]
    relative, query_weight, key_weight, query_bias, key_bias = ready(
        relative, query_weight, key_weight, query_bias, key_bias
    )
    rel_query_out, rel_key_out = rel_query_store.ref, rel_key_store.ref
    rel_query_out[...] = affine(relative[...], query_weight, query_bias).astype(BF)
    rel_key_out[...] = affine(
        nn(reversal(relative.shape[0]), relative[...]).astype(BF), key_weight, key_bias
    ).astype(BF)
    (own,) = ready(own)
    size = own.shape[0]
    query_ref[...] = affine(own[...], query_weight, query_bias).astype(BF)
    key_ref[...] = affine(own[...], key_weight, key_bias).astype(BF)

    def pair_step(pair):
        columns = pair_columns(pair)
        for side in range(2):
            s_ref = terms_stores[2 * pair + side].ref
            query_own = of_head(query_ref[:, columns], side)
            own_terms(block, s_ref, query_own, rel_key_out[:, columns], 1)
            other_terms(
                block, s_ref, lambda slot: key_ref[:, columns], of_head(rel_query_out[:, columns], side), 0, (1,)
            )
            s_ref[:, size : 2 * size] += nt(query_own, key_ref[:, columns])
            terms_stores[2 * pair + side].push()

    for pair in range(HEADS // 2):
        pair_step(pair)


def forward_kernel(
    block_ref, length_ref, own, core, far, diagonal, rel_query, rel_key, *rest
):
    terms = rest[:HEADS]
    (
        query_weight, key_weight, query_bias, key_bias, value_weight, value_bias, output_weight,
        output_bias, first_gain, first_bias, inner_weight, inner_bias, outer_weight, outer_bias, second_gain,
        second_bias, cotangent,
        layer_store, first_store, chances_store, sent_store, query_store, key_store, value_store,
        early_send_low, early_send_high, early_keep,
        x_all, s_ref, mixture_ref, log_ref, active_ref, slope_ref, grads_out,
    ) = rest[HEADS:]
    block = block_ref[0]
    length = length_ref[0]
    size, model_width = layer_store.shape
    head_dim = model_width // HEADS
    factor = LOG2E / math.sqrt(3.0 * head_dim)
    query_out, key_out, value_out = query_store.ref, key_store.ref, value_store.ref
    chances_out, sent_out = chances_store.ref, sent_store.ref
    own, core, far, diagonal, rel_query_out = ready(own, core, far, diagonal, rel_query)
    query_weight, key_weight, query_bias, key_bias = ready(query_weight, key_weight, query_bias, key_bias)
    value_weight, value_bias = ready(value_weight, value_bias)
    place_blocks(block, x_all, own, core, far, diagonal)
    query_out[...] = affine(x_all[...], query_weight, query_bias).astype(BF)
    key_out[...] = affine(x_all[...], key_weight, key_bias).astype(BF)
    value_out[...] = affine(x_all[...], value_weight, value_bias).astype(BF)
    step = lanes((1, 4 * size))
    position = ((block + 3 + step // size) % 4) * size + step % size
    mask_row = jnp.where(position < length, 0.0, -1e30)
    stat_lane = lanes((size, 128))
    log_ref[...] = jnp.zeros_like(log_ref)

    def pair_step(pair):
        columns = pair_columns(pair)
        total = jnp.zeros((size, 128), F32)
        for side in range(2):
            head = 2 * pair + side
            query_own = of_head(query_out[size : 2 * size, columns], side)
            s_ref[...] = terms[head].ready()[...]
            other_terms(
                block,
                s_ref,
                lambda slot: key_out[slot * size : (slot + 1) * size, columns],
                of_head(rel_query_out[:, columns], side),
                0,
                (0, 2, 3),
            )
            before = s_ref[:, :size] + nt(query_own, key_out[:size, columns])
            s_ref[:, :size] = before * factor + mask_row[:, :size]
            s_ref[:, size : 2 * size] = s_ref[:, size : 2 * size] * factor + mask_row[:, size : 2 * size]
            after = s_ref[:, 2 * size :] + nt(query_own, key_out[2 * size :, columns])
            s_ref[:, 2 * size :] = after * factor + mask_row[:, 2 * size :]
            top = jnp.max(s_ref[...], axis=1, keepdims=True)
            raised = jnp.exp2(s_ref[...] - top)
            s_ref[...] = raised
            row_sum = jnp.sum(raised, axis=1, keepdims=True)
            chances = (s_ref[...] * (1.0 / row_sum)).astype(BF)
            chances_out[head] = chances
            log_total = top + jnp.log2(row_sum)
            log_ref[...] = jnp.where(stat_lane % 8 == head, log_total, log_ref[...])
            total = total + nn(chances, of_head(value_out[:, columns], side))
        mixture_ref[:, columns] = total

    for pair in range(HEADS // 2):
        pair_step(pair)

    (
        output_weight, output_bias, first_gain, first_bias, inner_weight, inner_bias, outer_weight, outer_bias,
        second_gain, second_bias, cotangent,
    ) = ready(
        output_weight, output_bias, first_gain, first_bias, inner_weight, inner_bias, outer_weight, outer_bias,
        second_gain, second_bias, cotangent,
    )
    inner_width = inner_weight.shape[1]
    chunks = inner_width // model_width
    mixture_low = mixture_ref[...].astype(BF)
    first_sum = own[...].astype(F32) + affine(mixture_low, output_weight, output_bias)
    first_hat, first_rate = norm_forward(first_sum)
    normed = (first_hat * as_row(first_gain) + as_row(first_bias)).astype(BF)
    root_half = math.sqrt(0.5)
    density = 1.0 / math.sqrt(2.0 * math.pi)

    inner_row = as_row(inner_bias)
    second_sum = normed.astype(F32) + as_row(outer_bias)
    for chunk in range(chunks):
        span = slice(chunk * model_width, (chunk + 1) * model_width)
        inner_pre = nn(normed, inner_weight[:, span]) + inner_row[:, span]
        below = 0.5 + 0.5 * lax.erf(inner_pre * root_half)
        slope_ref[:, span] = below + inner_pre * density * jnp.exp(-0.5 * inner_pre * inner_pre)
        active_ref[:, span] = (inner_pre * below).astype(BF)
        second_sum = second_sum + nn(active_ref[:, span], outer_weight[span, :])
    second_hat, second_rate = norm_forward(second_sum)
    gain = as_row(second_gain)
    layer_store.ref[...] = second_hat * gain + as_row(second_bias)
    layer_store.push()
    cot = cotangent[...].astype(F32)
    grad_second = norm_backward(cot * gain, second_hat, second_rate)
    grad_outer = grad_second.astype(BF)
    outer_at, inner_at, output_at, small_at = 0, inner_width, 2 * inner_width, 2 * inner_width + model_width
    grads_out[small_at + 16 :, :] = jnp.zeros((grads_out.shape[0] - small_at - 16, model_width), BF)
    small = [column_sum(grad_outer), column_sum(cot * second_hat), column_sum(cot)]
    grad_normed = grad_second
    outer_turned, normed_turned = grad_outer.T, normed.T
    for chunk in range(chunks):
        span = slice(chunk * model_width, (chunk + 1) * model_width)
        grads_out[outer_at + chunk * model_width : outer_at + (chunk + 1) * model_width, :] = nn(
            outer_turned, active_ref[:, span]
        ).astype(BF)
        grad_inner = (nt(grad_outer, outer_weight[span, :]) * slope_ref[:, span]).astype(BF)
        small.append(column_sum(grad_inner))
        grads_out[inner_at + chunk * model_width : inner_at + (chunk + 1) * model_width, :] = nn(
            normed_turned, grad_inner
        ).astype(BF)
        grad_normed = grad_normed + nt(grad_inner, inner_weight[:, span])
    grad_normed = grad_normed.astype(BF).astype(F32)
    grad_first = norm_backward(grad_normed * as_row(first_gain), first_hat, first_rate)
    first_store.ref[...] = grad_first
    first_store.push()
    grad_branch = grad_first.astype(BF)
    grads_out[output_at : output_at + model_width, :] = tn(mixture_low, grad_branch).astype(BF)
    small += [column_sum(grad_normed * first_hat), column_sum(grad_normed), column_sum(grad_branch)]
    small += [jnp.zeros((16 - len(small), model_width), F32)]
    grads_out[small_at : small_at + 16, :] = jnp.concatenate(small, axis=0).astype(BF)
    push_halves(block % 2, grads_out, (early_send_low, early_send_high), early_keep)
    grad_mixture = nt(grad_branch, output_weight[...]).astype(BF)
    sent_out[:, :model_width] = grad_mixture
    along = grad_mixture.astype(F32) * mixture_ref[...]
    stats = jnp.where(stat_lane < 16, 0.0, log_ref[...])
    for head in range(HEADS):
        columns = slice((head // 2) * 128, (head // 2 + 1) * 128)
        delta = jnp.sum(of_head(along[:, columns], head % 2), axis=1, keepdims=True)
        stats = jnp.where((stat_lane == head) | (stat_lane == 8 + head), delta, stats)
    upper = stats.astype(BF).astype(F32)
    rest = stats - upper
    middle = rest.astype(BF).astype(F32)
    group = stat_lane // 8
    parts = jnp.where((group == 0) | (group == 2), upper, jnp.where((group == 1) | (group == 3), middle, rest - middle))
    sent_out[:, model_width:] = jnp.where(group < 5, parts, 0.0).astype(BF)
    sent_store.push()


def position_backward(block, side, grad_scores, flip, other_pair, ext_pair, own_rows_back, wall_ref, near_ref, shift):
    grad_back = nn(flip, grad_scores).astype(BF)
    unskewed(block, wall_ref, near_ref, grad_back, shift)
    row_grad = nn(grad_back, of_head(other_pair, side)) + nn(wall_ref[...], of_head(ext_pair, side))
    return row_grad, tn(of_head(own_rows_back, side), wall_ref[...])


def query_kernel(
    block_ref, rel_key, query_all, sent, value_all, key_all, chances_load,
    query_store, rel_key_grad_store,
    ext_ref, wall_ref, near_ref, back_ref, sum_ref, rows_ref,
):
    block = block_ref[0]
    size, model_width = query_store.shape
    scale = 1.0 / math.sqrt(3.0 * (model_width // HEADS))
    flip = reversal(size)
    chances = chances_load.buffer
    rel_key, query_all, sent, value_all, key_all = ready(rel_key, query_all, sent, value_all, key_all)
    extend_table(block, ext_ref, rel_key)
    back_ref[...] = nn(flip, query_all[size : 2 * size, :]).astype(BF)
    stats = sent[:, model_width:].astype(F32)
    stat_lane = lanes((size, 128))

    def pair_step(pair, carry):
        columns = pair_columns(pair)
        row_grad = jnp.zeros((size, 128), F32)
        for side in range(2):
            head = 2 * pair + side
            delta = jnp.sum(
                jnp.where((stat_lane == head) | (stat_lane == 8 + head), stats, 0.0), axis=1, keepdims=True
            )
            grad_mixture = of_head(sent[:, columns], side)
            grad_chances = nt(grad_mixture, value_all[:, columns])
            grad_scores = (chances[head].astype(F32) * (grad_chances - delta)).astype(BF)
            rows, table = position_backward(
                block, side, grad_scores, flip, key_all[:, columns], ext_ref[:, columns],
                back_ref[:, columns], wall_ref, near_ref, 3 * size,
            )
            row_grad = row_grad + rows
            if side == 0:
                sum_ref[...] = table
            else:
                sum_ref[...] += table
        rows_ref[:, columns] = (row_grad * scale).astype(BF)
        rel_key_grad_store.ref[columns, :] = table_grad(block, sum_ref[...], scale)
        return carry

    lax.fori_loop(0, HEADS // 2, pair_step, 0)
    query_store.ref[...] = nn(flip, rows_ref[...]).astype(BF)


def key_pairs(
    first, last, block_ref, length_ref, rel_query, key_all, rel_key, query_all, value_all,
    sent_own, sent_core, sent_far, sent_diagonal, key_rows_ref, value_rows_ref, rel_grad_ref,
    sent_ref, s_ref, grad_ref, ext_ref, wall_ref, near_ref, back_ref, sum_ref, stat_ref,
):
    block = block_ref[0]
    length = length_ref[0]
    size, model_width = key_rows_ref.shape
    scale = 1.0 / math.sqrt(3.0 * (model_width // HEADS))
    factor = LOG2E * scale
    flip = reversal(size)
    rel_query, key_all, rel_key, query_all, value_all = ready(rel_query, key_all, rel_key, query_all, value_all)
    extend_table(block, ext_ref, rel_query)
    back_ref[...] = nn(flip, key_all[size : 2 * size, :]).astype(BF)
    place_blocks(block, sent_ref, *ready(sent_own, sent_core, sent_far, sent_diagonal))
    stats = sent_ref[:, model_width:].astype(F32).T
    stat_ref[0:8, :] = stats[0:8, :] + stats[8:16, :]
    stat_ref[8:16, :] = stats[16:24, :] + (stats[24:32, :] + stats[32:40, :])
    position = block * size + lax.broadcasted_iota(jnp.int32, (size, 1), 0)
    mask_column = jnp.where(position < length, 0.0, -1e30)

    def pair_step(pair, carry):
        columns = pair_columns(pair)
        row_grad = jnp.zeros((size, 128), F32)
        value_grad = jnp.zeros((size, 128), F32)
        for side in range(2):
            head = 2 * pair + side
            key_head = of_head(key_all[size : 2 * size, columns], side)
            own_terms(block, s_ref, key_head, rel_query[:, columns], 0)
            other_terms(
                block,
                s_ref,
                lambda slot: query_all[slot * size : (slot + 1) * size, columns],
                of_head(rel_key[:, columns], side),
                1,
                range(4),
            )
            content = nt(key_head, query_all[:, columns])
            shift = mask_column - stat_ref[pl.ds(8 + head, 1), :]
            s_ref[...] = jnp.exp2((s_ref[...] + content) * factor + shift)
            value_grad = value_grad + nn(s_ref[...].astype(BF), of_head(sent_ref[:, columns], side))
            grad_chances = nt(of_head(value_all[size : 2 * size, columns], side), sent_ref[:, columns])
            grad_ref[...] = (s_ref[...] * (grad_chances - stat_ref[pl.ds(head, 1), :])).astype(BF)
            rows, table = position_backward(
                block, side, grad_ref[...], flip, query_all[:, columns], ext_ref[:, columns],
                back_ref[:, columns], wall_ref, near_ref, 3 * size + 1,
            )
            row_grad = row_grad + rows
            if side == 0:
                sum_ref[...] = table
            else:
                sum_ref[...] += table
        key_rows_ref[:, columns] = (row_grad * scale).astype(BF)
        value_rows_ref[:, columns] = value_grad.astype(BF)
        rel_grad_ref[columns, :] = table_grad(block, sum_ref[...], scale)
        return carry

    lax.fori_loop(first, last, pair_step, 0)


def first_key_kernel(*refs):
    ins, outs, scratch = refs[:11], refs[11:14], refs[14:]
    key_pairs(0, FIRST_PAIRS, *ins, *(out.ref for out in outs), *scratch)


def last_key_kernel(*refs):
    ins, before, outs, scratch = refs[:11], refs[11:14], refs[14:17], refs[17:]
    done = FIRST_PAIRS * 128
    for old, out in zip(ready(*before), outs):
        if out.shape[0] == outs[0].shape[0]:
            out.ref[:, :done] = old[:, :done]
        else:
            out.ref[:done, :] = old[:done, :]
    key_pairs(FIRST_PAIRS, HEADS // 2, *ins, *(out.ref for out in outs), *scratch)


def final_kernel(
    block_ref, own, relative, key_rows, value_rows, rel_grad, grad_query, grad_rel_key, query_weight, key_weight,
    value_weight, grad_first, tokens_store, late_send_low, late_send_high, late_keep, grads_out,
):
    size, model_width = tokens_store.shape
    own, relative, key_rows_ref, value_rows_ref, rel_grad_ref, grad_query, grad_rel_key = ready(
        own, relative, key_rows, value_rows, rel_grad, grad_query, grad_rel_key
    )
    rel = relative.shape[0]
    grad_key = nn(reversal(size), key_rows_ref[...]).astype(BF)
    grad_value = value_rows_ref[...]
    rel_query_grad = rel_grad_ref[...]
    rel_key_grad = grad_rel_key[...]
    query_low = rel_query_grad.astype(BF)
    key_low = nn(rel_key_grad.astype(BF), reversal(rel)).astype(BF)
    tokens = own[...]
    table = relative[...]
    grads_out[0:model_width, :] = (tn(tokens, grad_query[...]) + tt(table, query_low)).astype(BF)
    grads_out[model_width : 2 * model_width, :] = (tn(tokens, grad_key) + tt(table, key_low)).astype(BF)
    grads_out[2 * model_width : 3 * model_width, :] = tn(tokens, grad_value).astype(BF)
    table_at = 3 * model_width
    query_weight, key_weight, value_weight, grad_first = ready(query_weight, key_weight, value_weight, grad_first)
    grads_out[table_at : table_at + rel, :] = (
        tt(query_low, query_weight[...]) + tt(key_low, key_weight[...])
    ).astype(BF)
    small_at = table_at + rel
    grads_out[small_at + 16 :, :] = jnp.zeros((grads_out.shape[0] - small_at - 16, model_width), BF)
    ones = jnp.ones((8, rel), BF)

    def lane_sums(values):
        high = values.astype(BF)
        low = (values - high.astype(F32)).astype(BF)
        return (nt(ones, high) + nt(ones, low))[0:1, :]

    small = [
        column_sum(grad_query[...]) + lane_sums(rel_query_grad),
        column_sum(grad_key) + lane_sums(rel_key_grad),
        column_sum(grad_value),
        jnp.zeros((13, model_width), F32),
    ]
    grads_out[small_at : small_at + 16, :] = jnp.concatenate(small, axis=0).astype(BF)
    push_halves(block_ref[0] % 2, grads_out, (late_send_low, late_send_high), late_keep)
    tokens_store.ref[...] = (
        nt(grad_query[...], query_weight[...])
        + nt(grad_key, key_weight[...])
        + nt(grad_value, value_weight[...])
        + grad_first[...]
    )


class Load:
    def __init__(self, source, buffer, sem):
        self.copy, self.buffer, self.waiting = pltpu.make_async_copy(source, buffer, sem), buffer, True
        self.copy.start()

    def ready(self):
        if self.waiting:
            self.copy.wait()
        self.waiting = False
        return self.buffer


def ready(*loads):
    return [load.ready() for load in loads]


class Store:
    def __init__(self, target, buffer, sem):
        self.copy, self.ref, self.shape, self.waiting = pltpu.make_async_copy(buffer, target, sem), buffer, buffer.shape, False

    def push(self):
        self.copy.start()
        self.waiting = True

    def finish(self):
        if not self.waiting:
            self.push()
        self.copy.wait()


class Here:
    def __init__(self, ref):
        self.ref = self.buffer = ref
        self.shape = ref.shape

    def ready(self):
        return self.ref

    def push(self):
        pass

    def finish(self):
        pass


def terms_after(first, terms):
    arrays = in_order(first, [array for array, _, _ in terms])
    return [(array, start, blocks) for array, (_, start, blocks) in zip(arrays, terms)]


class Raw:
    def __init__(self, target, sem):
        self.target, self.sem = target, sem
        self.shape = target.shape

    def push_from(self, source):
        self.copy = pltpu.make_async_copy(source, self.target, self.sem)
        self.copy.start()

    def finish(self):
        self.copy.wait()


def push_halves(core, rows_ref, sends, keep):
    half = keep.shape[0]
    for k, send in enumerate(sends):
        at = (1 - core) * half + k * send.shape[0]
        send.push_from(rows_ref.at[pl.ds(pl.multiple_of(at, 16), send.shape[0])])
    keep.push_from(rows_ref.at[pl.ds(pl.multiple_of(core * half, 16), half)])


class Kept:
    def __init__(self, *what):
        self.what = what


class Fetch:
    def __init__(self, what):
        self.what = what


def call(kernel, outs, scratch, *operands, scalars, micros):
    fetched = [k for k, operand in enumerate(operands) if isinstance(operand, Fetch)]
    operands = [operand.what if isinstance(operand, Fetch) else operand for operand in operands]
    outs = list(outs) + [Kept(operands[k].shape, operands[k].dtype) for k in fetched]
    kept_in = [isinstance(operand, Kept) for operand in operands]
    kept_out = [isinstance(out, Kept) for out in outs]
    operands = [
        operand if k < scalars
        else pltpu.with_memory_space_constraint(operand.what[0], pltpu.VMEM) if kept
        else pltpu.with_memory_space_constraint(operand, pltpu.HBM)
        for k, (operand, kept) in enumerate(zip(operands, kept_in))
    ]
    outs = [out.what if kept else out for out, kept in zip(outs, kept_out)]
    raw = [len(out) > 2 for out in outs]
    loads = [k for k in range(scalars, len(operands)) if not kept_in[k]]
    stores = [k for k in range(len(outs)) if not kept_out[k]]
    buffered = [k for k in stores if not raw[k]]
    own_loads = [k for k in loads if k not in fetched]

    def body(*refs):
        n, m = len(operands), len(outs)
        ins, results, rest = list(refs[:n]), list(refs[n : n + m]), list(refs[n + m :])
        in_sems, out_sems = rest.pop(), rest.pop()
        buffers = [rest.pop() for _ in range(len(own_loads) + len(buffered))][::-1]
        targets = dict(zip(own_loads, buffers)) | dict(zip(fetched, results[m - len(fetched) :]))
        results = results[: m - len(fetched)]
        for k in range(scalars, n):
            if kept_in[k]:
                ins[k] = Here(ins[k])
        for place, k in enumerate(loads):
            ins[k] = Load(ins[k], targets[k], in_sems.at[place])
        buffers = buffers[len(own_loads) :]
        for k in range(len(results)):
            if kept_out[k]:
                results[k] = Here(results[k])
        for place, k in enumerate(stores):
            if raw[k]:
                results[k] = Raw(results[k], out_sems.at[place])
            else:
                results[k] = Store(results[k], buffers.pop(0), out_sems.at[place])
        kernel(*ins, *results, *rest)
        for k in fetched:
            ins[k].ready()
        for k in stores:
            results[k].finish()

    spaces = [
        pltpu.SMEM if k < scalars else pltpu.VMEM if kept_in[k] else pltpu.HBM for k in range(len(operands))
    ]
    buffers = [(operands[k].shape, operands[k].dtype) for k in own_loads] + [outs[k][:2] for k in buffered]
    return pl.pallas_call(
        body,
        out_shape=[
            pltpu.VMEM(out[0], out[1]) if kept else pltpu.HBM(out[0], out[1])
            for out, kept in zip(outs, kept_out)
        ],
        in_specs=[pl.BlockSpec(memory_space=space) for space in spaces],
        out_specs=[pl.BlockSpec(memory_space=pltpu.VMEM if kept else pltpu.HBM) for kept in kept_out],
        scratch_shapes=[pltpu.VMEM(shape, kind) for shape, kind in list(scratch) + buffers]
        + [pltpu.SemaphoreType.DMA((max(len(stores), 1),)), pltpu.SemaphoreType.DMA((max(len(loads), 1),))],
        compiler_params=pltpu.CompilerParams(vmem_limit_bytes=VMEM_LIMIT),
        cost_estimate=pl.CostEstimate(flops=micros * 10**9, bytes_accessed=micros * 10**6, transcendentals=0),
    )(*operands)


class Group:
    def __init__(self, blk_count, dp_count, bits):
        self.blk_count, self.dp_count, self.bits = blk_count, dp_count, bits
        self.size = 2 ** len(bits)
        place = {"blk": lax.axis_index("blk"), "dp": lax.axis_index("dp")}
        self.digits = [(place[axis] >> (bit.bit_length() - 1)) & 1 for axis, bit in bits]
        self.me = sum(digit << k for k, digit in enumerate(self.digits))

    def pairs(self, mask):
        change = {"blk": 0, "dp": 0}
        for k, (axis, bit) in enumerate(self.bits):
            if mask >> k & 1:
                change[axis] |= bit
        return [
            (blk * self.dp_count + dp, (blk ^ change["blk"]) * self.dp_count + (dp ^ change["dp"]))
            for blk in range(self.blk_count)
            for dp in range(self.dp_count)
        ]

    def send(self, values, mask):
        return lax.ppermute(values, ("blk", "dp"), self.pairs(mask))

    def scatter(self, terms):
        def part(index):
            return [
                (array, first + index * (blocks // self.size), blocks // self.size) for array, first, blocks in terms
            ]

        outs = [total(part(self.me ^ mask)) for mask in range(1, self.size)]
        arrived = [self.send(out, mask + 1) for mask, out in enumerate(outs)]
        return outs, part(self.me) + [whole(array) for array in arrived]

    def pieces(self, held):
        return [held] + [self.send(held, mask) for mask in range(1, self.size)]

    def gather(self, held):
        return self.arrange(self.pieces(held))

    def arrange(self, parts):
        for k, digit in enumerate(self.digits):
            parts = [
                jnp.where(digit == 0, parts[q], parts[q ^ (1 << k)]) for q in range(self.size)
            ]
        return jnp.concatenate(parts, axis=0)


def groups_of(blk_count, dp_count):
    bits, bit = [], 2
    while bit < dp_count:
        bits.append(("dp", bit))
        bit *= 2
    groups = [[("blk", 1)], [("blk", 2), ("dp", 1)]]
    groups += [bits[k : k + 2] for k in range(0, len(bits), 2)]
    return [Group(blk_count, dp_count, group) for group in groups]


def whole(array):
    return array, 0, array.shape[0]


def total(terms):
    spans = []
    for array, first, blocks in terms:
        if isinstance(array, tuple):
            low, high = array
            size = low.shape[0]
            low = lax.dynamic_slice_in_dim(low, jnp.minimum(first, size - blocks), blocks, 0)
            high = lax.dynamic_slice_in_dim(high, jnp.maximum(first - size, 0), blocks, 0)
            spans.append(jnp.where(first < size, low, high))
        else:
            spans.append(lax.dynamic_slice_in_dim(array, first, blocks, 0))
    return sum(span.astype(F32) for span in spans).astype(BF)


def in_order(first, then):
    return lax.optimization_barrier((first, then))[1]


def halves_to_scratch(core_ref, held, arrived, both_ref):
    held, arrived = ready(held, arrived)
    rows = held.shape[0]
    mine = pl.multiple_of(core_ref[0] * rows, 16)
    theirs = pl.multiple_of((1 - core_ref[0]) * rows, 16)
    both_ref[pl.ds(mine, rows), :] = held[...]
    both_ref[pl.ds(theirs, rows), :] = arrived[...]


def early_kernel(
    core_ref, held, arrived,
    outer_weight, inner_weight, output_weight, outer_bias, second_gain, second_bias, inner_bias, first_gain, first_bias,
    output_bias,
    both_ref,
):
    halves_to_scratch(core_ref, held, arrived, both_ref)
    inner_width, width = outer_weight.shape
    chunks = inner_width // width
    for chunk in range(chunks):
        span = slice(chunk * width, (chunk + 1) * width)
        outer_weight.ref[span, :] = both_ref[span, :].T.astype(F32)
    outer_weight.push()
    for chunk in range(chunks):
        at = inner_width + chunk * width
        inner_weight.ref[:, chunk * width : (chunk + 1) * width] = both_ref[at : at + width, :].astype(F32)
    at = 2 * inner_width
    output_weight.ref[...] = both_ref[at : at + width, :].astype(F32)
    output_weight.push()
    small = both_ref[at + width : at + width + 16, :].astype(F32)

    def vector(out, row):
        out.ref[...] = small[row, :]
        out.push()

    vector(outer_bias, 0)
    vector(second_gain, 1)
    vector(second_bias, 2)
    inner_bias.ref[...] = jnp.concatenate([small[3 + k : 4 + k, :] for k in range(chunks)], axis=1)[0, :]
    inner_bias.push()
    vector(first_gain, 3 + chunks)
    vector(first_bias, 4 + chunks)
    vector(output_bias, 5 + chunks)


def late_kernel(
    core_ref, held, arrived,
    query_weight, query_bias, key_weight, key_bias, value_weight, value_bias, relative,
    both_ref,
):
    halves_to_scratch(core_ref, held, arrived, both_ref)
    width = query_weight.shape[0]
    rel = relative.shape[0]
    for k, out in enumerate((query_weight, key_weight, value_weight)):
        out.ref[...] = both_ref[k * width : (k + 1) * width, :].astype(F32)
        out.push()
    at = 3 * width
    relative.ref[...] = both_ref[at : at + rel, :].astype(F32)
    small = both_ref[at + rel : at + rel + 16, :].astype(F32)
    query_bias.ref[...] = small[0, :]
    key_bias.ref[...] = small[1, :]
    value_bias.ref[...] = small[2, :]


def on_device(
    blk_count, dp_count,
    tokens, lengths, query_weight, query_bias, key_weight, key_bias, value_weight, value_bias,
    output_weight, output_bias, first_gain, first_bias, inner_weight, inner_bias, outer_weight, outer_bias,
    second_gain, second_bias, relative_table, cotangent,
):
    seq_count, size, width = tokens.shape
    rel = relative_table.shape[0]
    inner_width = inner_weight.shape[1]
    own = tokens[0]
    block = lax.axis_index("blk").astype(jnp.int32).reshape(1)
    groups = groups_of(blk_count, dp_count)
    chips = groups[1:]
    shards = blk_count * dp_count

    def along(values, bit):
        return lax.ppermute(values, "blk", [(i, i ^ bit) for i in range(blk_count)])

    def blocks(rows, share):
        return rows.reshape(shards // share, -1, width)

    def first_terms(keep, low, high):
        arrived = tuple(groups[0].send(blocks(piece, 4), 1) for piece in (low, high))
        return [whole(blocks(keep, 2)), (arrived, 0, shards // 2)]

    def flat(values):
        return values.reshape(-1, width)

    core = along(own, 1)
    far = along(own, 2)
    diagonal = along(own, 3)
    full = blk_count * size
    head_terms = [((size, full), F32)] * HEADS
    (
        rel_query, rel_key, *terms, relative_kept, query_weight, key_weight, query_bias, key_bias, own, value_weight, value_bias,
    ) = call(
        first_kernel,
        [Kept((rel, width), BF), Kept((rel, width), BF), *head_terms],
        [((size, width), BF), ((size, width), BF)],
        block,
        *map(Fetch, (relative_table, query_weight, key_weight, query_bias, key_bias, own, value_weight, value_bias)),
        scalars=1, micros=9,
    )
    (
        layer_out, grad_first, chances, sent, query_all, key_all, value_all,
        early_send_low, early_send_high, early_keep,
    ) = call(
        forward_kernel,
        [
            ((size, width), F32),
            Kept((size, width), F32),
            Kept((HEADS, size, full), BF),
            Kept((size, width + 128), BF),
            Kept((full, width), BF),
            Kept((full, width), BF),
            Kept((full, width), BF),
            ((EARLY_ROWS // 4, width), BF, "raw"),
            ((EARLY_ROWS // 4, width), BF, "raw"),
            ((EARLY_ROWS // 2, width), BF, "raw"),
        ],
        [
            ((full, width), BF),
            ((size, full), F32),
            ((size, width), F32),
            ((size, 128), F32),
            ((size, inner_width), BF),
            ((size, inner_width), F32),
            ((EARLY_ROWS, width), BF),
        ],
        block, lengths,
        *map(Kept, (own, core, far, diagonal, rel_query, rel_key)),
        *terms,
        *map(Kept, (query_weight, key_weight, query_bias, key_bias, value_weight, value_bias)),
        output_weight, output_bias, first_gain, first_bias, inner_weight, inner_bias, outer_weight, outer_bias,
        second_gain, second_bias, cotangent[0],
        scalars=2, micros=20,
    )
    early_terms = first_terms(early_keep, early_send_low, early_send_high)
    sent_far = along(sent, 2)
    sent_core = along(sent, 1)
    sent_diagonal = along(sent, 3)
    position_scratch = [
        ((3 * rel, width), BF),
        ((size, 3 * rel), BF),
        ((size, full), BF),
        ((size, width), BF),
        ((128, 3 * rel), F32),
    ]
    grad_query, grad_rel_key = call(
        query_kernel,
        [Kept((size, width), BF), Kept((width, rel), F32)],
        position_scratch + [((size, width), BF)],
        block, *map(Kept, (rel_key, query_all, sent, value_all, key_all, chances)),
        scalars=1, micros=8,
    )
    key_scratch = (
        [((full, width + 128), BF), ((size, full), F32), ((size, full), BF)] + position_scratch + [((16, full), F32)]
    )
    key_arrays = tuple(
        map(Kept, (rel_query, key_all, rel_key, query_all, value_all, sent, sent_core, sent_far, sent_diagonal))
    )
    key_outs = [Kept((size, width), BF), Kept((size, width), BF), Kept((width, rel), F32)]
    sending, early_terms = chips[0].scatter(early_terms)
    key_rows, value_rows, rel_grad = call(
        first_key_kernel, key_outs, key_scratch, in_order(sending, block), lengths, *key_arrays,
        scalars=2, micros=13,
    )
    for group in chips[1:]:
        sending, early_terms = group.scatter(early_terms)
    key_parts = call(
        last_key_kernel, key_outs, key_scratch, in_order(sending, block), lengths, *key_arrays,
        *map(Kept, (key_rows, value_rows, rel_grad)), scalars=2, micros=8,
    )
    early_held = total(early_terms)
    grad_tokens, late_send_low, late_send_high, late_keep = call(
        final_kernel,
        [((size, width), F32)] + [((LATE_ROWS // 4, width), BF, "raw")] * 2 + [((LATE_ROWS // 2, width), BF, "raw")],
        [((LATE_ROWS, width), BF)],
        in_order(early_held, block),
        *map(Kept, (own, relative_kept, *key_parts, grad_query, grad_rel_key, query_weight, key_weight, value_weight,
                    grad_first)),
        scalars=1, micros=4,
    )
    for group in reversed(chips[1:]):
        early_held = group.gather(early_held)
    late_terms = terms_after(early_held, first_terms(late_keep, late_send_low, late_send_high))
    sending, late_terms = chips[0].scatter(late_terms)
    for group in chips[1:]:
        sending, late_terms = group.scatter(late_terms)
    early_pieces = chips[0].pieces(in_order(sending, early_held))
    late_held = total(terms_after(early_pieces[1], late_terms))
    early_pieces = in_order(late_held, early_pieces)
    for group in reversed(chips[1:]):
        late_held = group.gather(late_held)
    late_held, early_pieces = lax.optimization_barrier((late_held, early_pieces))
    early_held = chips[0].arrange(early_pieces)
    late_pieces = chips[0].pieces(late_held)
    my_core = groups[0].me.astype(jnp.int32).reshape(1)
    square, vector = ((width, width), F32), ((width,), F32)
    (
        g_outer_weight, g_inner_weight, g_output_weight, g_outer_bias, g_second_gain, g_second_bias, g_inner_bias,
        g_first_gain, g_first_bias, g_output_bias,
    ) = call(
        early_kernel,
        [((inner_width, width), F32), ((width, inner_width), F32), square, vector, vector, vector,
         ((inner_width,), F32), vector, vector, vector],
        [((EARLY_ROWS, width), BF)],
        my_core, *(Kept(flat(piece)) for piece in groups[0].pieces(early_held)),
        scalars=1, micros=4,
    )
    late_held = chips[0].arrange(in_order(g_output_bias, late_pieces))
    (
        g_query_weight, g_query_bias, g_key_weight, g_key_bias, g_value_weight, g_value_bias, g_relative,
    ) = call(
        late_kernel,
        [square, vector, square, vector, square, vector, ((rel, width), F32)],
        [((LATE_ROWS, width), BF)],
        my_core, *(Kept(flat(piece)) for piece in groups[0].pieces(late_held)),
        scalars=1, micros=2,
    )
    return (
        layer_out[None], grad_tokens[None], g_query_weight, g_query_bias, g_key_weight, g_key_bias,
        g_value_weight, g_value_bias, g_output_weight, g_output_bias, g_first_gain, g_first_bias,
        g_inner_weight, g_inner_bias, g_outer_weight, g_outer_bias, g_second_gain, g_second_bias, g_relative,
    )


def solution(mesh):
    blk_count, dp_count = mesh.shape["blk"], mesh.shape["dp"]
    rows = P("dp", "blk", None)
    in_specs = (rows, P("dp")) + (P(),) * 17 + (rows,)
    out_specs = (rows, rows) + (P(),) * 17

    def whole(*arrays):
        return on_device(blk_count, dp_count, *arrays)

    return jax.shard_map(whole, mesh=mesh, in_specs=in_specs, out_specs=out_specs, check_vma=False)
```

```python
import math

import jax
import jax.numpy as jnp
from jax import lax
from jax.experimental import pallas as pl
from jax.experimental.pallas import tpu as pltpu
from jax.sharding import PartitionSpec as P

HEADS = 6
BF = jnp.bfloat16
F32 = jnp.float32
LOG2E = math.log2(math.e)
EPS = 1e-07
MIB = 1024 * 1024
EARLY_ROWS = 3584
LATE_ROWS = 1792


def nn(left, right):
    return lax.dot_general(left, right, (((1,), (0,)), ((), ())), preferred_element_type=F32)


def nt(left, right):
    return lax.dot_general(left, right, (((1,), (1,)), ((), ())), preferred_element_type=F32)


def tn(left, right):
    return lax.dot_general(left, right, (((0,), (0,)), ((), ())), preferred_element_type=F32)


def tt(left, right):
    return lax.dot_general(left, right, (((0,), (1,)), ((), ())), preferred_element_type=F32)


def lanes(shape):
    return lax.broadcasted_iota(jnp.int32, shape, len(shape) - 1)


def of_head(values, head):
    inside = (lanes(values.shape) // 64) == head
    return jnp.where(inside, values, jnp.zeros_like(values))


def stacked(values):
    return jnp.concatenate([of_head(values, 0), of_head(values, 1)], axis=0)


def abreast(values):
    rows = values.shape[0] // 2
    return jnp.concatenate([values[:rows], values[rows:]], axis=1)


def pair_columns(pair):
    if isinstance(pair, int):
        return slice(pair * 128, (pair + 1) * 128)
    return pl.ds(pl.multiple_of(pair * 128, 128), 128)


def wide(column, width):
    return jnp.broadcast_to(column, (column.shape[0], width))


def reversal(size):
    rows = lax.broadcasted_iota(jnp.int32, (size, size), 0)
    cols = lax.broadcasted_iota(jnp.int32, (size, size), 1)
    return jnp.where(rows + cols == size - 1, 1.0, 0.0).astype(BF)


def placed(block, size, own, core, far, diagonal):
    even = block % 2 == 0
    core_at = pl.multiple_of(jnp.where(even, 2 * size, 0), size)
    diagonal_at = pl.multiple_of(jnp.where(even, 0, 2 * size), size)
    return (size, own), (3 * size, far), (core_at, core), (diagonal_at, diagonal)


def rolled_window(source, shift):
    half = source.shape[0] // 2
    upper = pltpu.roll(source[:half, half:], shift, 1, stride=1, stride_axis=0)[:, half:]
    lower = pltpu.roll(source[half:, : 3 * half], shift, 1, stride=1, stride_axis=0)[:, half:]
    return jnp.concatenate([upper, lower], axis=0)


def own_terms(block, s_ref, own_rows, own_table, shift):
    size = own_rows.shape[0] // 2
    rel = own_table.shape[0]
    scores = nt(own_rows, own_table)
    last, first = scores[:, rel - 1 : rel], scores[:, 0:1]
    source = jnp.concatenate([scores, wide(last, size), wide(first, size)], axis=1)
    for side in range(2):
        rows = slice(side * size, (side + 1) * size)
        s_ref[rows, : 3 * size] = pltpu.roll(source[rows], shift, 1, stride=1, stride_axis=0)[:, : 3 * size]
    s_ref[:, 3 * size :] = wide(jnp.where(block < 2, last, first), size)


def other_terms(block, s_ref, others, tables, shift, slots):
    size = s_ref.shape[0] // 2
    rel = tables.shape[0] // 2

    def both(start, rows):
        return jnp.concatenate([tables[start : start + rows], tables[rel + start : rel + start + rows]], axis=0)

    def near(slot):
        if slot == 1:
            product = nt(others(slot), tables)
            parts = [product[:, :rel], product[:, rel:]]
        else:
            product = nt(others(slot), both(size if slot == 0 else 0, size))
            parts = [product[:, :size], product[:, size:]]
        if slot == 0:
            parts = [jnp.concatenate([part, wide(part[:, size - 1 : size], size)], axis=1) for part in parts]
        elif slot == 2:
            parts = [jnp.concatenate([wide(part[:, 0:1], size), part], axis=1) for part in parts]
        return [rolled_window(part, shift).T for part in parts]

    def constant(slot):
        rows = others(slot)
        top = nt(both(0, 16), rows)
        bottom = nt(both(rel - 16, 16), rows)
        return [
            s_ref[side * size : (side + 1) * size, 3 * size :]
            + jnp.where(block < 2, top[16 * side : 16 * side + 1], bottom[16 * side + 15 : 16 * side + 16])
            for side in range(2)
        ]

    for slot in slots:
        span = slice(slot * size, (slot + 1) * size)
        terms = near(slot) if slot < 3 else None
        fixed = constant(slot) if slot != 1 else None
        past = block == (0 if slot == 0 else 3)
        for side in range(2):
            rows = slice(side * size, (side + 1) * size)
            if slot == 1:
                s_ref[rows, span] += terms[side]
            elif slot == 3:
                s_ref[rows, span] = fixed[side]
            else:
                s_ref[rows, span] = jnp.where(past, fixed[side], s_ref[rows, span] + terms[side])


def extend_table(ext_ref, table_ref):
    rel = table_ref.shape[0]
    half = rel // 2
    width = table_ref.shape[1]
    ext_ref[0:rel, :] = table_ref[...]
    ext_ref[rel : rel + half, :] = jnp.broadcast_to(table_ref[rel - 1 : rel, :], (half, width))
    ext_ref[rel + half : 2 * rel, :] = jnp.broadcast_to(table_ref[0:1, :], (half, width))


def unskewed(block, wall_ref, grad_rows, shift):
    size = grad_rows.shape[0]
    before, own, after, far = (grad_rows[:, k * size : (k + 1) * size] for k in range(4))
    none = jnp.zeros_like(own)
    no_before, no_after = block == 0, block == 3
    near = jnp.concatenate(
        [jnp.where(no_before, none, before), own, jnp.where(no_after, none, after), none], axis=1
    )
    rolled = pltpu.roll(near, shift, 1, stride=1, stride_axis=0)
    far = far + jnp.where(no_before, before, jnp.where(no_after, after, none))
    wall_ref[:, : 2 * size] = rolled[:, : 2 * size]
    wall_ref[:, 2 * size : 3 * size] = rolled[:, 2 * size : 3 * size] + jnp.where(block < 2, far, none)
    wall_ref[:, 3 * size :] = rolled[:, 3 * size :] + jnp.where(block < 2, none, far)


def table_grad(sums, scale):
    rel = sums.shape[1] // 2
    half = rel // 2
    over = jnp.sum(sums[:, rel : rel + half], axis=1, keepdims=True)
    under = jnp.sum(sums[:, rel + half :], axis=1, keepdims=True)
    at = lanes((sums.shape[0], rel))
    folded = sums[:, :rel] + jnp.where(at == rel - 1, over, 0.0) + jnp.where(at == 0, under, 0.0)
    return folded * scale


def as_row(vector_ref):
    return vector_ref[...].astype(F32).reshape(1, -1)


def affine(values, weight_ref, bias_ref):
    return nn(values, weight_ref[...]) + as_row(bias_ref)


def norm_forward(values):
    center = values - jnp.mean(values, axis=-1, keepdims=True)
    spread = jnp.mean(center * center, axis=-1, keepdims=True)
    rate = lax.rsqrt(spread + EPS)
    return center * rate, rate


def norm_backward(grad_hat, hat, rate):
    mean_grad = jnp.mean(grad_hat, axis=-1, keepdims=True)
    mean_along = jnp.mean(grad_hat * hat, axis=-1, keepdims=True)
    return rate * (grad_hat - mean_grad - hat * mean_along)


def column_sum(values):
    return jnp.sum(values.astype(F32), axis=0, keepdims=True)


def slab_copy(source, target, sems, k):
    return pltpu.make_async_copy(source.at[k], target.at[k], sems.at[k])


def first_kernel(
    block_ref, relative, query_weight, key_weight, query_bias, key_bias, own, value_weight,
    value_bias, *rest,
):
    rel_query_store, rel_key_store, terms_out, query_ref, key_ref, terms_ref, sems = rest
    block = block_ref[0]
    relative, query_weight, key_weight, query_bias, key_bias = ready(
        relative, query_weight, key_weight, query_bias, key_bias
    )
    rel_query_out, rel_key_out = rel_query_store.ref, rel_key_store.ref
    rel_query_out[...] = affine(relative[...], query_weight, query_bias).astype(BF)
    rel_key_out[...] = affine(
        nn(reversal(relative.shape[0]), relative[...]).astype(BF), key_weight, key_bias
    ).astype(BF)
    (own,) = ready(own)
    size = own.shape[0]
    query_ref[...] = affine(own[...], query_weight, query_bias).astype(BF)
    key_ref[...] = affine(own[...], key_weight, key_bias).astype(BF)

    def pair_step(pair, carry):
        columns = pair_columns(pair)
        s_ref = terms_ref.at[pair]
        query_own = stacked(query_ref[:, columns])
        own_terms(block, s_ref, query_own, rel_key_out[:, columns], 1)
        other_terms(block, s_ref, lambda slot: key_ref[:, columns], stacked(rel_query_out[:, columns]), 0, (1,))
        s_ref[:, size : 2 * size] += nt(query_own, key_ref[:, columns])
        slab_copy(terms_ref, terms_out, sems, pair).start()
        return carry

    lax.fori_loop(0, HEADS // 2, pair_step, 0)
    for pair in range(HEADS // 2):
        slab_copy(terms_ref, terms_out, sems, pair).wait()


def forward_kernel(
    block_ref, length_ref, place_ref, own, core, far, diagonal, rel_query, rel_key, *rest
):
    (
        terms, query_weight, key_weight, query_bias, key_bias, value_weight, value_bias, output_weight,
        output_bias, first_gain, first_bias, inner_weight, inner_bias, outer_weight, outer_bias, second_gain,
        second_bias, cotangent,
        layer_store, first_store, chances_store, sent_store, stats_store, query_store, key_store, value_store,
        early_send_low, early_send_high, early_keep,
        x_all, s_ref, mixture_ref, log_ref, active_ref, slope_ref, grads_out, terms_ref, sums_ref, small_ref, bias_ref, sems,
    ) = rest
    block = block_ref[0]
    length = length_ref[0]
    size, model_width = layer_store.shape
    head_dim = model_width // HEADS
    factor = LOG2E / math.sqrt(3.0 * head_dim)
    query_out, key_out, value_out = query_store.ref, key_store.ref, value_store.ref
    chances_out, sent_out = chances_store.ref, sent_store.ref
    for pair in range(HEADS // 2):
        slab_copy(terms, terms_ref, sems, pair).start()
    own, core, far, diagonal, rel_query_out = ready(own, core, far, diagonal, rel_query)
    query_weight, key_weight, query_bias, key_bias = ready(query_weight, key_weight, query_bias, key_bias)
    value_weight, value_bias = ready(value_weight, value_bias)
    for at, rows in placed(block, size, own, core, far, diagonal):
        x_all[pl.ds(at, size), :] = rows[...]
    query_out[...] = affine(x_all[...], query_weight, query_bias).astype(BF)
    key_out[...] = affine(x_all[...], key_weight, key_bias).astype(BF)
    value_out[...] = affine(x_all[...], value_weight, value_bias).astype(BF)
    step = lanes((1, 4 * size))
    position = ((block + 3 + step // size) % 4) * size + step % size
    mask_row = jnp.where(position < length, 0.0, -1e30)
    stat_lane = lanes((size, 128))
    log_ref[...] = jnp.zeros_like(log_ref)

    def pair_step(pair, carry):
        columns = pair_columns(pair)
        query_own = stacked(query_out[size : 2 * size, columns])
        slab_copy(terms, terms_ref, sems, pair).wait()
        s_ref[...] = terms_ref[pair]
        other_terms(
            block,
            s_ref,
            lambda slot: key_out[slot * size : (slot + 1) * size, columns],
            stacked(rel_query_out[:, columns]),
            0,
            (0, 2, 3),
        )
        before = s_ref[:, :size] + nt(query_own, key_out[:size, columns])
        s_ref[:, :size] = before * factor + mask_row[:, :size]
        s_ref[:, size : 2 * size] = s_ref[:, size : 2 * size] * factor + mask_row[:, size : 2 * size]
        after = s_ref[:, 2 * size :] + nt(query_own, key_out[2 * size :, columns])
        s_ref[:, 2 * size :] = after * factor + mask_row[:, 2 * size :]
        top = jnp.max(s_ref[...], axis=1, keepdims=True)
        raised = jnp.exp2(s_ref[...] - top)
        s_ref[...] = raised
        row_sum = jnp.sum(raised, axis=1, keepdims=True)
        chances = (s_ref[...] * (1.0 / row_sum)).astype(BF)
        chances_out[pair] = chances
        log_total = top + jnp.log2(row_sum)
        for side in range(2):
            log_ref[...] = jnp.where(
                stat_lane % 8 == 2 * pair + side, log_total[side * size : (side + 1) * size], log_ref[...]
            )
        total = nn(abreast(chances), stacked(value_out[:, columns]))
        mixture_ref[:, columns] = total
        return carry

    lax.fori_loop(0, HEADS // 2, pair_step, 0)

    (
        output_weight, output_bias, first_gain, first_bias, inner_weight, inner_bias, outer_weight, outer_bias,
        second_gain, second_bias, cotangent,
    ) = ready(
        output_weight, output_bias, first_gain, first_bias, inner_weight, inner_bias, outer_weight, outer_bias,
        second_gain, second_bias, cotangent,
    )
    inner_width = inner_weight.shape[1]
    chunks = inner_width // model_width
    mixture_low = mixture_ref[...].astype(BF)
    first_sum = own[...].astype(F32) + affine(mixture_low, output_weight, output_bias)
    first_hat, first_rate = norm_forward(first_sum)
    normed = (first_hat * as_row(first_gain) + as_row(first_bias)).astype(BF)
    root_half = math.sqrt(0.5)
    density = 1.0 / math.sqrt(2.0 * math.pi)

    sums_ref[...] = normed.astype(F32) + as_row(outer_bias)
    bias_ref[...] = as_row(inner_bias)

    def chunk_span(chunk):
        return pl.ds(chunk * model_width, model_width)

    def ahead(chunk, carry):
        span = chunk_span(chunk)
        inner_pre = nn(normed, inner_weight[:, span]) + bias_ref[:, span]
        below = 0.5 + 0.5 * lax.erf(inner_pre * root_half)
        slope_ref[:, span] = below + inner_pre * density * jnp.exp(-0.5 * inner_pre * inner_pre)
        active = (inner_pre * below).astype(BF)
        active_ref[:, span] = active
        sums_ref[...] += nn(active, outer_weight[span, :])
        return carry

    for chunk in range(chunks):
        ahead(chunk, 0)
    second_sum = sums_ref[...]
    second_hat, second_rate = norm_forward(second_sum)
    gain = as_row(second_gain)
    layer_store.ref[...] = second_hat * gain + as_row(second_bias)
    layer_store.push()
    cot = cotangent[...].astype(F32)
    grad_second = norm_backward(cot * gain, second_hat, second_rate)
    grad_outer = grad_second.astype(BF)
    outer_at, inner_at, output_at, small_at = 0, inner_width, 2 * inner_width, 2 * inner_width + model_width
    grads_out[small_at + 16 :, :] = jnp.zeros((grads_out.shape[0] - small_at - 16, model_width), BF)
    small_ref[...] = jnp.zeros_like(small_ref)
    for k, values in enumerate((column_sum(grad_outer), column_sum(cot * second_hat), column_sum(cot))):
        small_ref[k : k + 1, :] = values
    sums_ref[...] = grad_second
    outer_turned, normed_turned = grad_outer.T, normed.T

    def back(chunk, carry):
        span = chunk_span(chunk)
        at = outer_at + chunk * model_width
        grads_out[pl.ds(at, model_width), :] = nn(outer_turned, active_ref[:, span]).astype(BF)
        grad_inner = (nt(grad_outer, outer_weight[span, :]) * slope_ref[:, span]).astype(BF)
        small_ref[pl.ds(3 + chunk, 1), :] = column_sum(grad_inner)
        at = inner_at + chunk * model_width
        grads_out[pl.ds(at, model_width), :] = nn(normed_turned, grad_inner).astype(BF)
        sums_ref[...] += nt(grad_inner, inner_weight[:, span])
        return carry

    for chunk in range(chunks):
        back(chunk, 0)
    grad_normed = sums_ref[...].astype(BF).astype(F32)
    grad_first = norm_backward(grad_normed * as_row(first_gain), first_hat, first_rate)
    first_store.ref[...] = grad_first
    first_store.push()
    grad_branch = grad_first.astype(BF)
    grads_out[output_at : output_at + model_width, :] = tn(mixture_low, grad_branch).astype(BF)
    for k, values in enumerate(
        (column_sum(grad_normed * first_hat), column_sum(grad_normed), column_sum(grad_branch))
    ):
        small_ref[3 + chunks + k : 4 + chunks + k, :] = values
    grads_out[small_at : small_at + 16, :] = small_ref[...].astype(BF)
    push_halves(block % 2, place_ref[0], grads_out, (early_send_low, early_send_high), early_keep)
    grad_mixture = nt(grad_branch, output_weight[...]).astype(BF)
    sent_out[:size, :] = grad_mixture
    along = grad_mixture.astype(F32) * mixture_ref[...]
    stats = log_ref[...]
    for head in range(HEADS):
        columns = slice((head // 2) * 128, (head // 2 + 1) * 128)
        delta = jnp.sum(of_head(along[:, columns], head % 2), axis=1, keepdims=True)
        stats = jnp.where((stat_lane < 16) & (stat_lane % 8 == head), delta, stats)
    stats_store.ref[...] = stats
    upper = stats.astype(BF).astype(F32)
    parts = jnp.where((stat_lane // 8) % 2 == 0, upper, stats - upper).T[:32, :]
    sent_out[size:, :size] = parts.astype(BF)
    sent_out[size:, size:] = jnp.zeros((32, model_width - size), BF)
    sent_store.push()


def position_backward(block, grad_scores, flip, other_pair, ext_pair, own_rows_back, wall_ref, shift):
    size = flip.shape[0]
    full = grad_scores.shape[1]
    grad_back = nn(flip, abreast(grad_scores)).astype(BF)
    for side in range(2):
        unskewed(block, wall_ref.at[pl.ds(side * size, size)], grad_back[:, side * full : (side + 1) * full], shift)
    row_grad = nn(grad_back, stacked(other_pair)) + nn(abreast(wall_ref[...]), stacked(ext_pair))
    return row_grad, tn(stacked(own_rows_back), wall_ref[...])


def query_kernel(
    block_ref, rel_key, query_all, sent, stats, value_all, key_all, chances_load,
    query_store, rel_key_grad_store,
    ext_ref, wall_ref, back_ref, rows_ref,
):
    block = block_ref[0]
    size, model_width = query_store.shape
    scale = 1.0 / math.sqrt(3.0 * (model_width // HEADS))
    flip = reversal(size)
    chances = chances_load.buffer
    rel_key, query_all, sent, stats, value_all, key_all = ready(rel_key, query_all, sent, stats, value_all, key_all)
    extend_table(ext_ref, rel_key)
    back_ref[...] = nn(flip, query_all[size : 2 * size, :]).astype(BF)
    stat_lane = lanes((size, 128))

    def pair_step(pair, carry):
        columns = pair_columns(pair)
        delta = jnp.concatenate(
            [
                jnp.sum(jnp.where(stat_lane == head, stats[...], 0.0), axis=1, keepdims=True)
                for head in (2 * pair, 2 * pair + 1)
            ],
            axis=0,
        )
        grad_chances = nt(stacked(sent[:size, columns]), value_all[:, columns])
        grad_scores = (chances[pair].astype(F32) * (grad_chances - delta)).astype(BF)
        row_grad, table = position_backward(
            block, grad_scores, flip, key_all[:, columns], ext_ref[:, columns], back_ref[:, columns], wall_ref, 3 * size
        )
        rows_ref[:, columns] = (row_grad * scale).astype(BF)
        rel_key_grad_store.ref[columns, :] = table_grad(table, scale)
        return carry

    lax.fori_loop(0, HEADS // 2, pair_step, 0)
    query_store.ref[...] = nn(flip, rows_ref[...]).astype(BF)


def key_kernel(
    block_ref, length_ref, place_ref, rel_query, key_all, rel_key, query_all, value_all,
    sent_own, sent_core, sent_far, sent_diagonal,
    own, relative, grad_query, grad_rel_key, query_weight, key_weight, value_weight, grad_first,
    tokens_store, late_send_low, late_send_high, late_keep,
    grads_out, key_rows_ref, value_rows_ref, rel_grad_ref,
    sent_ref, s_ref, grad_ref, ext_ref, wall_ref, back_ref, stat_ref,
):
    block = block_ref[0]
    length = length_ref[0]
    size, model_width = key_rows_ref.shape
    scale = 1.0 / math.sqrt(3.0 * (model_width // HEADS))
    factor = LOG2E * scale
    flip = reversal(size)
    rel_query, key_all, rel_key, query_all, value_all = ready(rel_query, key_all, rel_key, query_all, value_all)
    extend_table(ext_ref, rel_query)
    back_ref[...] = nn(flip, key_all[size : 2 * size, :]).astype(BF)
    for at, rows in placed(block, size, *ready(sent_own, sent_core, sent_far, sent_diagonal)):
        sent_ref[pl.ds(at, size), :] = rows[:size, :]
        parts = rows[size:, :size].astype(F32)
        stat_ref[0:8, pl.ds(at, size)] = parts[0:8, :] + parts[8:16, :]
        stat_ref[8:16, pl.ds(at, size)] = parts[16:24, :] + parts[24:32, :]
    position = block * size + lax.broadcasted_iota(jnp.int32, (size, 1), 0)
    mask_column = jnp.where(position < length, 0.0, -1e30)

    def pair_step(pair, carry):
        columns = pair_columns(pair)
        key_pair = stacked(key_all[size : 2 * size, columns])
        own_terms(block, s_ref, key_pair, rel_query[:, columns], 0)
        other_terms(
            block,
            s_ref,
            lambda slot: query_all[slot * size : (slot + 1) * size, columns],
            stacked(rel_key[:, columns]),
            1,
            range(4),
        )
        content = nt(key_pair, query_all[:, columns])
        for side in range(2):
            rows = slice(side * size, (side + 1) * size)
            less = mask_column - stat_ref[pl.ds(8 + 2 * pair + side, 1), :]
            s_ref[rows, :] = jnp.exp2((s_ref[rows, :] + content[rows]) * factor + less)
        value_grad = nn(abreast(s_ref[...].astype(BF)), stacked(sent_ref[:, columns]))
        grad_chances = nt(stacked(value_all[size : 2 * size, columns]), sent_ref[:, columns])
        for side in range(2):
            rows = slice(side * size, (side + 1) * size)
            delta = stat_ref[pl.ds(2 * pair + side, 1), :]
            grad_ref[rows, :] = (s_ref[rows, :] * (grad_chances[rows] - delta)).astype(BF)
        row_grad, table = position_backward(
            block, grad_ref[...], flip, query_all[:, columns], ext_ref[:, columns], back_ref[:, columns], wall_ref,
            3 * size + 1,
        )
        key_rows_ref[:, columns] = (row_grad * scale).astype(BF)
        value_rows_ref[:, columns] = value_grad.astype(BF)
        rel_grad_ref[columns, :] = table_grad(table, scale)
        return carry

    lax.fori_loop(0, HEADS // 2, pair_step, 0)
    own, relative, grad_query, grad_rel_key = ready(own, relative, grad_query, grad_rel_key)
    rel = relative.shape[0]
    grad_key = nn(flip, key_rows_ref[...]).astype(BF)
    grad_value = value_rows_ref[...]
    rel_query_grad = rel_grad_ref[...]
    rel_key_grad = grad_rel_key[...]
    query_low = rel_query_grad.astype(BF)
    key_low = nn(rel_key_grad.astype(BF), reversal(rel)).astype(BF)
    tokens = own[...]
    table = relative[...]
    grads_out[0:model_width, :] = (tn(tokens, grad_query[...]) + tt(table, query_low)).astype(BF)
    grads_out[model_width : 2 * model_width, :] = (tn(tokens, grad_key) + tt(table, key_low)).astype(BF)
    grads_out[2 * model_width : 3 * model_width, :] = tn(tokens, grad_value).astype(BF)
    table_at = 3 * model_width
    query_weight, key_weight, value_weight, grad_first = ready(query_weight, key_weight, value_weight, grad_first)
    grads_out[table_at : table_at + rel, :] = (
        tt(query_low, query_weight[...]) + tt(key_low, key_weight[...])
    ).astype(BF)
    small_at = table_at + rel
    grads_out[small_at + 16 :, :] = jnp.zeros((grads_out.shape[0] - small_at - 16, model_width), BF)
    ones = jnp.ones((8, rel), BF)

    def lane_sums(values):
        high = values.astype(BF)
        low = (values - high.astype(F32)).astype(BF)
        return (nt(ones, high) + nt(ones, low))[0:1, :]

    small = [
        column_sum(grad_query[...]) + lane_sums(rel_query_grad),
        column_sum(grad_key) + lane_sums(rel_key_grad),
        column_sum(grad_value),
        jnp.zeros((13, model_width), F32),
    ]
    grads_out[small_at : small_at + 16, :] = jnp.concatenate(small, axis=0).astype(BF)
    push_halves(block % 2, place_ref[0], grads_out, (late_send_low, late_send_high), late_keep)
    tokens_store.ref[...] = (
        nt(grad_query[...], query_weight[...])
        + nt(grad_key, key_weight[...])
        + nt(grad_value, value_weight[...])
        + grad_first[...]
    )


class Load:
    def __init__(self, source, buffer, sem):
        self.copy, self.buffer, self.waiting = pltpu.make_async_copy(source, buffer, sem), buffer, True
        self.copy.start()

    def ready(self):
        if self.waiting:
            self.copy.wait()
        self.waiting = False
        return self.buffer


def ready(*loads):
    return [load.ready() for load in loads]


class Store:
    def __init__(self, target, buffer, sem):
        self.copy, self.ref, self.shape, self.waiting = pltpu.make_async_copy(buffer, target, sem), buffer, buffer.shape, False

    def push(self):
        self.copy.start()
        self.waiting = True

    def finish(self):
        if not self.waiting:
            self.push()
        self.copy.wait()


class Here:
    def __init__(self, ref):
        self.ref = self.buffer = ref
        self.shape = ref.shape

    def ready(self):
        return self.ref

    def push(self):
        pass

    def finish(self):
        pass


def terms_after(first, terms):
    arrays = in_order(first, [array for array, _, _ in terms])
    return [(array, start, blocks) for array, (_, start, blocks) in zip(arrays, terms)]


class Raw:
    def __init__(self, target, sems):
        self.target, self.sems, self.copies = target, sems, []
        self.shape = target.shape

    def push_from(self, source, there):
        copy = pltpu.make_async_copy(source, self.target.at[there], self.sems.at[len(self.copies)])
        copy.start()
        self.copies.append(copy)

    def finish(self):
        for copy in self.copies:
            copy.wait()


def push_halves(core, place, rows_ref, sends, keep):
    half = keep.shape[0]
    part = half // 4
    for k in range(4):
        at = (place ^ k) * part
        send, there = sends[k // 2], pl.ds(k % 2 * part, part)
        send.push_from(rows_ref.at[pl.ds(pl.multiple_of((1 - core) * half + at, 16), part)], there)
        keep.push_from(rows_ref.at[pl.ds(pl.multiple_of(core * half + at, 16), part)], pl.ds(k * part, part))


class Kept:
    def __init__(self, *what):
        self.what = what


class Bare:
    def __init__(self, *what):
        self.what = what


class Fetch:
    def __init__(self, what):
        self.what = what


def call(kernel, outs, scratch, *operands, scalars, micros, vmem):
    fetched = [k for k, operand in enumerate(operands) if isinstance(operand, Fetch)]
    bare_in = [k for k, operand in enumerate(operands) if isinstance(operand, Bare)]
    operands = [
        operand.what if isinstance(operand, Fetch) else operand.what[0] if isinstance(operand, Bare) else operand
        for operand in operands
    ]
    bare_out = [k for k, out in enumerate(outs) if isinstance(out, Bare)]
    outs = [out.what if isinstance(out, Bare) else out for out in outs]
    outs = list(outs) + [Kept(operands[k].shape, operands[k].dtype) for k in fetched]
    kept_in = [isinstance(operand, Kept) for operand in operands]
    kept_out = [isinstance(out, Kept) for out in outs]
    operands = [
        operand if k < scalars
        else pltpu.with_memory_space_constraint(operand.what[0], pltpu.VMEM) if kept
        else pltpu.with_memory_space_constraint(operand, pltpu.HBM)
        for k, (operand, kept) in enumerate(zip(operands, kept_in))
    ]
    outs = [out.what if kept else out for out, kept in zip(outs, kept_out)]
    raw = [len(out) > 2 for out in outs]
    loads = [k for k in range(scalars, len(operands)) if not kept_in[k] and k not in bare_in]
    stores = [k for k in range(len(outs)) if not kept_out[k] and k not in bare_out]
    buffered = [k for k in stores if not raw[k]]
    own_loads = [k for k in loads if k not in fetched]

    def body(*refs):
        n, m = len(operands), len(outs)
        ins, results, rest = list(refs[:n]), list(refs[n : n + m]), list(refs[n + m :])
        in_sems, out_sems = rest.pop(), rest.pop()
        buffers = [rest.pop() for _ in range(len(own_loads) + len(buffered))][::-1]
        targets = dict(zip(own_loads, buffers)) | dict(zip(fetched, results[m - len(fetched) :]))
        results = results[: m - len(fetched)]
        for k in range(scalars, n):
            if kept_in[k]:
                ins[k] = Here(ins[k])
        for place, k in enumerate(loads):
            ins[k] = Load(ins[k], targets[k], in_sems.at[place])
        buffers = buffers[len(own_loads) :]
        for k in range(len(results)):
            if kept_out[k]:
                results[k] = Here(results[k])
        for place, k in enumerate(stores):
            if raw[k]:
                results[k] = Raw(results[k], out_sems.at[place])
            else:
                results[k] = Store(results[k], buffers.pop(0), out_sems.at[place, 0])
        kernel(*ins, *results, *rest)
        for k in fetched:
            ins[k].ready()
        for k in stores:
            results[k].finish()

    spaces = [
        pltpu.SMEM if k < scalars else pltpu.VMEM if kept_in[k] else pltpu.HBM for k in range(len(operands))
    ]
    buffers = [(operands[k].shape, operands[k].dtype) for k in own_loads] + [outs[k][:2] for k in buffered]
    return pl.pallas_call(
        body,
        out_shape=[
            pltpu.VMEM(out[0], out[1]) if kept else pltpu.HBM(out[0], out[1])
            for out, kept in zip(outs, kept_out)
        ],
        in_specs=[pl.BlockSpec(memory_space=space) for space in spaces],
        out_specs=[pl.BlockSpec(memory_space=pltpu.VMEM if kept else pltpu.HBM) for kept in kept_out],
        scratch_shapes=[
            pltpu.SemaphoreType.DMA(space[0]) if space[1] is None else pltpu.VMEM(*space)
            for space in list(scratch) + buffers
        ]
        + [pltpu.SemaphoreType.DMA((max(len(stores), 1), 4)), pltpu.SemaphoreType.DMA((max(len(loads), 1),))],
        compiler_params=pltpu.CompilerParams(vmem_limit_bytes=vmem * MIB),
        cost_estimate=pl.CostEstimate(flops=micros * 10**9, bytes_accessed=micros * 10**6, transcendentals=0),
    )(*operands)


class Group:
    def __init__(self, blk_count, dp_count, bits):
        self.blk_count, self.dp_count, self.bits = blk_count, dp_count, bits
        self.size = 2 ** len(bits)
        place = {"blk": lax.axis_index("blk"), "dp": lax.axis_index("dp")}
        self.digits = [(place[axis] >> (bit.bit_length() - 1)) & 1 for axis, bit in bits]
        self.me = sum(digit << k for k, digit in enumerate(self.digits))

    def pairs(self, mask):
        change = {"blk": 0, "dp": 0}
        for k, (axis, bit) in enumerate(self.bits):
            if mask >> k & 1:
                change[axis] |= bit
        return [
            (blk * self.dp_count + dp, (blk ^ change["blk"]) * self.dp_count + (dp ^ change["dp"]))
            for blk in range(self.blk_count)
            for dp in range(self.dp_count)
        ]

    def send(self, values, mask):
        return lax.ppermute(values, ("blk", "dp"), self.pairs(mask))

    def scatter(self, terms):
        def part(index):
            return [
                (array, first + index * (blocks // self.size), blocks // self.size) for array, first, blocks in terms
            ]

        outs = [total(part(self.me ^ mask)) for mask in range(1, self.size)]
        arrived = [self.send(out, mask + 1) for mask, out in enumerate(outs)]
        return outs, part(self.me) + [whole(array) for array in arrived]

    def pieces(self, held):
        return [held] + [self.send(held, mask) for mask in range(1, self.size)]

    def gather(self, held):
        return self.arrange(self.pieces(held))

    def arrange(self, parts):
        for k, digit in enumerate(self.digits):
            parts = [
                jnp.where(digit == 0, parts[q], parts[q ^ (1 << k)]) for q in range(self.size)
            ]
        return jnp.concatenate(parts, axis=0)


def groups_of(blk_count, dp_count):
    bits, bit = [], 2
    while bit < dp_count:
        bits.append(("dp", bit))
        bit *= 2
    groups = [[("blk", 1)], [("blk", 2), ("dp", 1)]]
    groups += [bits[k : k + 2] for k in range(0, len(bits), 2)]
    return [Group(blk_count, dp_count, group) for group in groups]


def whole(array):
    return array, 0, array.shape[0]


def total(terms):
    spans = [
        array[first : first + blocks] if isinstance(first, int) else lax.dynamic_slice_in_dim(array, first, blocks, 0)
        for array, first, blocks in terms
    ]
    return sum(span.astype(F32) for span in spans).astype(BF)


def in_order(first, then):
    return lax.optimization_barrier((first, then))[1]


def halves_to_scratch(core_ref, place_ref, held, arrived, both_ref):
    held, arrived = ready(held, arrived)
    half = held.shape[0]
    part = half // 4
    for k in range(4):
        at = (place_ref[0] ^ k) * part
        span = slice(k * part, (k + 1) * part)
        both_ref[pl.ds(pl.multiple_of(core_ref[0] * half + at, 16), part), :] = held[span, :]
        both_ref[pl.ds(pl.multiple_of((1 - core_ref[0]) * half + at, 16), part), :] = arrived[span, :]


def early_kernel(
    core_ref, place_ref, held, arrived,
    outer_weight, inner_weight, output_weight, outer_bias, second_gain, second_bias, inner_bias, first_gain, first_bias,
    output_bias,
    both_ref,
):
    halves_to_scratch(core_ref, place_ref, held, arrived, both_ref)
    inner_width, width = outer_weight.shape
    chunks = inner_width // width
    for chunk in range(chunks):
        span = slice(chunk * width, (chunk + 1) * width)
        outer_weight.ref[span, :] = both_ref[span, :].T.astype(F32)
    outer_weight.push()
    for chunk in range(chunks):
        at = inner_width + chunk * width
        inner_weight.ref[:, chunk * width : (chunk + 1) * width] = both_ref[at : at + width, :].astype(F32)
    at = 2 * inner_width
    output_weight.ref[...] = both_ref[at : at + width, :].astype(F32)
    output_weight.push()
    small = both_ref[at + width : at + width + 16, :].astype(F32)

    def vector(out, row):
        out.ref[...] = small[row, :]
        out.push()

    vector(outer_bias, 0)
    vector(second_gain, 1)
    vector(second_bias, 2)
    inner_bias.ref[...] = jnp.concatenate([small[3 + k : 4 + k, :] for k in range(chunks)], axis=1)[0, :]
    inner_bias.push()
    vector(first_gain, 3 + chunks)
    vector(first_bias, 4 + chunks)
    vector(output_bias, 5 + chunks)


def late_kernel(
    core_ref, place_ref, held, arrived,
    query_weight, query_bias, key_weight, key_bias, value_weight, value_bias, relative,
    both_ref,
):
    halves_to_scratch(core_ref, place_ref, held, arrived, both_ref)
    width = query_weight.shape[0]
    rel = relative.shape[0]
    for k, out in enumerate((query_weight, key_weight, value_weight)):
        out.ref[...] = both_ref[k * width : (k + 1) * width, :].astype(F32)
        out.push()
    at = 3 * width
    relative.ref[...] = both_ref[at : at + rel, :].astype(F32)
    small = both_ref[at + rel : at + rel + 16, :].astype(F32)
    query_bias.ref[...] = small[0, :]
    key_bias.ref[...] = small[1, :]
    value_bias.ref[...] = small[2, :]


def on_device(
    blk_count, dp_count,
    tokens, lengths, query_weight, query_bias, key_weight, key_bias, value_weight, value_bias,
    output_weight, output_bias, first_gain, first_bias, inner_weight, inner_bias, outer_weight, outer_bias,
    second_gain, second_bias, relative_table, cotangent,
):
    seq_count, size, width = tokens.shape
    rel = relative_table.shape[0]
    inner_width = inner_weight.shape[1]
    own = tokens[0]
    block = lax.axis_index("blk").astype(jnp.int32).reshape(1)
    groups = groups_of(blk_count, dp_count)
    chips = groups[1:]
    place = chips[0].me.astype(jnp.int32).reshape(1)
    shards = blk_count * dp_count

    def along(values, bit):
        return lax.ppermute(values, "blk", [(i, i ^ bit) for i in range(blk_count)])

    def blocks(rows, share):
        return rows.reshape(shards // share, -1, width)

    def flat(values):
        return values.reshape(-1, width)

    def first_terms(keep, low, high):
        arrived = [groups[0].send(blocks(piece, 4), 1) for piece in (low, high)]
        keep, part = blocks(keep, 2), shards // 8
        return [[(keep, k * part, part), (arrived[k // 2], k % 2 * part, part)] for k in range(4)]

    def first_scatter(parts):
        outs = [total(terms) for terms in parts[1:]]
        return outs, parts[0] + [whole(chips[0].send(out, k + 1)) for k, out in enumerate(outs)]

    core = along(own, 1)
    far = along(own, 2)
    diagonal = along(own, 3)
    full = blk_count * size
    (
        rel_query, rel_key, terms, relative_kept, query_weight, key_weight, query_bias, key_bias, own, value_weight, value_bias,
    ) = call(
        first_kernel,
        [Kept((rel, width), BF), Kept((rel, width), BF), Bare((HEADS // 2, 2 * size, full), F32)],
        [((size, width), BF), ((size, width), BF), ((HEADS // 2, 2 * size, full), F32), ((HEADS // 2,), None)],
        block,
        *map(Fetch, (relative_table, query_weight, key_weight, query_bias, key_bias, own, value_weight, value_bias)),
        scalars=1, micros=9, vmem=14,
    )
    (
        layer_out, grad_first, chances, sent, stats, query_all, key_all, value_all,
        early_send_low, early_send_high, early_keep,
    ) = call(
        forward_kernel,
        [
            ((size, width), F32),
            Kept((size, width), F32),
            Kept((HEADS // 2, 2 * size, full), BF),
            Kept((size + 32, width), BF),
            Kept((size, 128), F32),
            Kept((full, width), BF),
            Kept((full, width), BF),
            Kept((full, width), BF),
            ((EARLY_ROWS // 4, width), BF, "raw"),
            ((EARLY_ROWS // 4, width), BF, "raw"),
            ((EARLY_ROWS // 2, width), BF, "raw"),
        ],
        [
            ((full, width), BF),
            ((2 * size, full), F32),
            ((size, width), F32),
            ((size, 128), F32),
            ((size, inner_width), BF),
            ((size, inner_width), F32),
            ((EARLY_ROWS, width), BF),
            ((HEADS // 2, 2 * size, full), F32),
            ((size, width), F32),
            ((16, width), F32),
            ((1, inner_width), F32),
            ((HEADS // 2,), None),
        ],
        block, lengths, place,
        *map(Kept, (own, core, far, diagonal, rel_query, rel_key)),
        Bare(terms),
        *map(Kept, (query_weight, key_weight, query_bias, key_bias, value_weight, value_bias)),
        output_weight, output_bias, first_gain, first_bias, inner_weight, inner_bias, outer_weight, outer_bias,
        second_gain, second_bias, cotangent[0],
        scalars=3, micros=20, vmem=26,
    )
    early_parts = first_terms(early_keep, early_send_low, early_send_high)
    sent_far = along(sent, 2)
    sent_core = along(sent, 1)
    position_scratch = [((2 * rel, width), BF), ((2 * size, 2 * rel), BF), ((size, width), BF)]
    grad_query, grad_rel_key = call(
        query_kernel,
        [Kept((size, width), BF), Kept((width, rel), F32)],
        position_scratch + [((size, width), BF)],
        block, *map(Kept, (rel_key, query_all, sent, stats, value_all, key_all, chances)),
        scalars=1, micros=8, vmem=10,
    )
    sent_diagonal = along(in_order(grad_query, sent_far), 1)
    key_scratch = (
        [((full, width), BF), ((2 * size, full), F32), ((2 * size, full), BF)] + position_scratch + [((16, full), F32)]
    )
    key_arrays = tuple(
        map(Kept, (rel_query, key_all, rel_key, query_all, value_all, sent, sent_core, sent_far, sent_diagonal))
    )
    sending, early_terms = first_scatter(early_parts)
    grad_tokens, late_send_low, late_send_high, late_keep = call(
        key_kernel,
        [((size, width), F32)] + [((LATE_ROWS // 4, width), BF, "raw")] * 2 + [((LATE_ROWS // 2, width), BF, "raw")],
        [((LATE_ROWS, width), BF), ((size, width), BF), ((size, width), BF), ((width, rel), F32)] + key_scratch,
        in_order(sending, block), lengths, place, *key_arrays,
        *map(Kept, (own, relative_kept, grad_query, grad_rel_key, query_weight, key_weight, value_weight, grad_first)),
        scalars=3, micros=17, vmem=18,
    )
    late_parts = first_terms(late_keep, late_send_low, late_send_high)
    early_terms = terms_after(late_send_low, early_terms)
    for group in chips[1:]:
        sending, early_terms = group.scatter(early_terms)
        late_parts = [terms_after(sending, terms) for terms in late_parts]
    sending, late_terms = first_scatter(late_parts)
    first_arrived = late_terms[1 - chips[0].size][0]
    early_held = total(terms_after(first_arrived, early_terms))
    for group in reversed(chips[2:]):
        early_held = group.gather(early_held)
    early_parts = chips[1].pieces(early_held)
    for group in chips[1:]:
        sending, late_terms = group.scatter(late_terms)
    first_arrived = late_terms[1 - chips[-1].size][0]
    early_pieces = chips[0].pieces(chips[1].arrange(in_order(first_arrived, early_parts)))
    late_held = total(late_terms)
    for group in reversed(chips[2:]):
        late_held = group.gather(late_held)
    late_parts = chips[1].pieces(late_held)
    late_parts, early_first = lax.optimization_barrier((late_parts, early_pieces[1]))
    early_pieces[1] = early_first
    late_held = chips[1].arrange(late_parts)
    early_held = jnp.concatenate(early_pieces, axis=0)
    late_pieces = chips[0].pieces(late_held)
    my_core = groups[0].me.astype(jnp.int32).reshape(1)
    square, vector = ((width, width), F32), ((width,), F32)
    (
        g_outer_weight, g_inner_weight, g_output_weight, g_outer_bias, g_second_gain, g_second_bias, g_inner_bias,
        g_first_gain, g_first_bias, g_output_bias,
    ) = call(
        early_kernel,
        [((inner_width, width), F32), ((width, inner_width), F32), square, vector, vector, vector,
         ((inner_width,), F32), vector, vector, vector],
        [((EARLY_ROWS, width), BF)],
        my_core, place, *(Kept(flat(piece)) for piece in groups[0].pieces(early_held)),
        scalars=2, micros=4, vmem=14,
    )
    late_held = jnp.concatenate(in_order(g_output_bias, late_pieces), axis=0)
    (
        g_query_weight, g_query_bias, g_key_weight, g_key_bias, g_value_weight, g_value_bias, g_relative,
    ) = call(
        late_kernel,
        [square, vector, square, vector, square, vector, ((rel, width), F32)],
        [((LATE_ROWS, width), BF)],
        my_core, place, *(Kept(flat(piece)) for piece in groups[0].pieces(late_held)),
        scalars=2, micros=2, vmem=10,
    )
    return (
        layer_out[None], grad_tokens[None], g_query_weight, g_query_bias, g_key_weight, g_key_bias,
        g_value_weight, g_value_bias, g_output_weight, g_output_bias, g_first_gain, g_first_bias,
        g_inner_weight, g_inner_bias, g_outer_weight, g_outer_bias, g_second_gain, g_second_bias, g_relative,
    )


def solution(mesh):
    blk_count, dp_count = mesh.shape["blk"], mesh.shape["dp"]
    rows = P("dp", "blk", None)
    in_specs = (rows, P("dp")) + (P(),) * 17 + (rows,)
    out_specs = (rows, rows) + (P(),) * 17

    def whole(*arrays):
        return on_device(blk_count, dp_count, *arrays)

    return jax.shard_map(whole, mesh=mesh, in_specs=in_specs, out_specs=out_specs, check_vma=False)
```

```python
import functools
import math

import jax
import jax.numpy as jnp
from jax import lax
from jax.experimental import pallas as pl
from jax.experimental.pallas import tpu as pltpu
from jax.sharding import PartitionSpec as P

HEADS = 6
BF = jnp.bfloat16
F32 = jnp.float32
LOG2E = math.log2(math.e)
EPS = 1e-07
MIB = 1024 * 1024
EARLY_ROWS = 3584
LATE_ROWS = 1792


def nn(left, right):
    return lax.dot_general(left, right, (((1,), (0,)), ((), ())), preferred_element_type=F32)


def nt(left, right):
    return lax.dot_general(left, right, (((1,), (1,)), ((), ())), preferred_element_type=F32)


def tn(left, right):
    return lax.dot_general(left, right, (((0,), (0,)), ((), ())), preferred_element_type=F32)


def tt(left, right):
    return lax.dot_general(left, right, (((0,), (1,)), ((), ())), preferred_element_type=F32)


def lanes(shape):
    return lax.broadcasted_iota(jnp.int32, shape, len(shape) - 1)


def of_head(values, head):
    inside = (lanes(values.shape) // 64) == head
    return jnp.where(inside, values, jnp.zeros_like(values))


def stacked(values):
    return jnp.concatenate([of_head(values, 0), of_head(values, 1)], axis=0)


def abreast(values):
    rows = values.shape[0] // 2
    return jnp.concatenate([values[:rows], values[rows:]], axis=1)


def pair_columns(pair):
    if isinstance(pair, int):
        return slice(pair * 128, (pair + 1) * 128)
    return pl.ds(pl.multiple_of(pair * 128, 128), 128)


def wide(column, width):
    return jnp.broadcast_to(column, (column.shape[0], width))


def reversal(size):
    rows = lax.broadcasted_iota(jnp.int32, (size, size), 0)
    cols = lax.broadcasted_iota(jnp.int32, (size, size), 1)
    return jnp.where(rows + cols == size - 1, 1.0, 0.0).astype(BF)


def placed(block, size, own, core, far, diagonal):
    even = block % 2 == 0
    core_at = pl.multiple_of(jnp.where(even, 2 * size, 0), size)
    diagonal_at = pl.multiple_of(jnp.where(even, 0, 2 * size), size)
    return (size, own), (3 * size, far), (core_at, core), (diagonal_at, diagonal)


def rolled_window(source, shift):
    half = source.shape[0] // 2
    upper = pltpu.roll(source[:half, half:], shift, 1, stride=1, stride_axis=0)[:, half:]
    lower = pltpu.roll(source[half:, : 3 * half], shift, 1, stride=1, stride_axis=0)[:, half:]
    return jnp.concatenate([upper, lower], axis=0)


def own_terms(block, s_ref, own_rows, own_table, shift):
    size = own_rows.shape[0] // 2
    rel = own_table.shape[0]
    scores = nt(own_rows, own_table)
    last, first = scores[:, rel - 1 : rel], scores[:, 0:1]
    source = jnp.concatenate([scores, wide(last, size), wide(first, size)], axis=1)
    for side in range(2):
        rows = slice(side * size, (side + 1) * size)
        s_ref[rows, : 3 * size] = pltpu.roll(source[rows], shift, 1, stride=1, stride_axis=0)[:, : 3 * size]
    s_ref[:, 3 * size :] = wide(jnp.where(block < 2, last, first), size)


def other_terms(block, s_ref, others, tables, shift, slots):
    size = s_ref.shape[0] // 2
    rel = tables.shape[0] // 2

    def both(start, rows):
        return jnp.concatenate([tables[start : start + rows], tables[rel + start : rel + start + rows]], axis=0)

    def near(slot):
        if slot == 1:
            product = nt(others(slot), tables)
            parts = [product[:, :rel], product[:, rel:]]
        else:
            product = nt(others(slot), both(size if slot == 0 else 0, size))
            parts = [product[:, :size], product[:, size:]]
        if slot == 0:
            parts = [jnp.concatenate([part, wide(part[:, size - 1 : size], size)], axis=1) for part in parts]
        elif slot == 2:
            parts = [jnp.concatenate([wide(part[:, 0:1], size), part], axis=1) for part in parts]
        return [rolled_window(part, shift).T for part in parts]

    def constant(slot):
        rows = others(slot)
        top = nt(both(0, 16), rows)
        bottom = nt(both(rel - 16, 16), rows)
        return [
            s_ref[side * size : (side + 1) * size, 3 * size :]
            + jnp.where(block < 2, top[16 * side : 16 * side + 1], bottom[16 * side + 15 : 16 * side + 16])
            for side in range(2)
        ]

    for slot in slots:
        span = slice(slot * size, (slot + 1) * size)
        terms = near(slot) if slot < 3 else None
        fixed = constant(slot) if slot != 1 else None
        past = block == (0 if slot == 0 else 3)
        for side in range(2):
            rows = slice(side * size, (side + 1) * size)
            if slot == 1:
                s_ref[rows, span] += terms[side]
            elif slot == 3:
                s_ref[rows, span] = fixed[side]
            else:
                s_ref[rows, span] = jnp.where(past, fixed[side], s_ref[rows, span] + terms[side])


def extend_table(ext_ref, table_ref):
    rel = table_ref.shape[0]
    half = rel // 2
    width = table_ref.shape[1]
    ext_ref[0:rel, :] = table_ref[...]
    ext_ref[rel : rel + half, :] = jnp.broadcast_to(table_ref[rel - 1 : rel, :], (half, width))
    ext_ref[rel + half : 2 * rel, :] = jnp.broadcast_to(table_ref[0:1, :], (half, width))


def unskewed(block, wall_ref, grad_rows, shift):
    size = grad_rows.shape[0]
    before, own, after, far = (grad_rows[:, k * size : (k + 1) * size] for k in range(4))
    none = jnp.zeros_like(own)
    no_before, no_after = block == 0, block == 3
    near = jnp.concatenate(
        [jnp.where(no_before, none, before), own, jnp.where(no_after, none, after), none], axis=1
    )
    rolled = pltpu.roll(near, shift, 1, stride=1, stride_axis=0)
    far = far + jnp.where(no_before, before, jnp.where(no_after, after, none))
    wall_ref[:, : 2 * size] = rolled[:, : 2 * size]
    wall_ref[:, 2 * size : 3 * size] = rolled[:, 2 * size : 3 * size] + jnp.where(block < 2, far, none)
    wall_ref[:, 3 * size :] = rolled[:, 3 * size :] + jnp.where(block < 2, none, far)


def table_grad(sums, scale):
    rel = sums.shape[1] // 2
    half = rel // 2
    over = jnp.sum(sums[:, rel : rel + half], axis=1, keepdims=True)
    under = jnp.sum(sums[:, rel + half :], axis=1, keepdims=True)
    at = lanes((sums.shape[0], rel))
    folded = sums[:, :rel] + jnp.where(at == rel - 1, over, 0.0) + jnp.where(at == 0, under, 0.0)
    return folded * scale


def as_row(vector_ref):
    return vector_ref[...].astype(F32).reshape(1, -1)


def affine(values, weight_ref, bias_ref):
    return nn(values, weight_ref[...]) + as_row(bias_ref)


def norm_forward(values):
    center = values - jnp.mean(values, axis=-1, keepdims=True)
    spread = jnp.mean(center * center, axis=-1, keepdims=True)
    rate = lax.rsqrt(spread + EPS)
    return center * rate, rate


def norm_backward(grad_hat, hat, rate):
    mean_grad = jnp.mean(grad_hat, axis=-1, keepdims=True)
    mean_along = jnp.mean(grad_hat * hat, axis=-1, keepdims=True)
    return rate * (grad_hat - mean_grad - hat * mean_along)


def column_sum(values):
    return jnp.sum(values.astype(F32), axis=0, keepdims=True)


def slab_copy(source, target, sems, k):
    return pltpu.make_async_copy(source.at[k], target.at[k], sems.at[k])


def first_kernel(
    block_ref, relative, query_weight, key_weight, query_bias, key_bias, own, value_weight,
    value_bias, *rest,
):
    rel_query_store, rel_key_store, terms_out, query_ref, key_ref, terms_ref, sems = rest
    block = block_ref[0]
    relative, query_weight, key_weight, query_bias, key_bias = ready(
        relative, query_weight, key_weight, query_bias, key_bias
    )
    rel_query_out, rel_key_out = rel_query_store.ref, rel_key_store.ref
    rel_query_out[...] = affine(relative[...], query_weight, query_bias).astype(BF)
    rel_key_out[...] = affine(
        nn(reversal(relative.shape[0]), relative[...]).astype(BF), key_weight, key_bias
    ).astype(BF)
    (own,) = ready(own)
    size = own.shape[0]
    query_ref[...] = affine(own[...], query_weight, query_bias).astype(BF)
    key_ref[...] = affine(own[...], key_weight, key_bias).astype(BF)

    def pair_step(pair, carry):
        columns = pair_columns(pair)
        s_ref = terms_ref.at[pair]
        query_own = stacked(query_ref[:, columns])
        own_terms(block, s_ref, query_own, rel_key_out[:, columns], 1)
        other_terms(block, s_ref, lambda slot: key_ref[:, columns], stacked(rel_query_out[:, columns]), 0, (1,))
        s_ref[:, size : 2 * size] += nt(query_own, key_ref[:, columns])
        slab_copy(terms_ref, terms_out, sems, pair).start()
        return carry

    lax.fori_loop(0, HEADS // 2, pair_step, 0)
    for pair in range(HEADS // 2):
        slab_copy(terms_ref, terms_out, sems, pair).wait()


def forward_kernel(
    block_ref, length_ref, place_ref, own, core, far, diagonal, rel_query, rel_key, *rest
):
    (
        terms, query_weight, key_weight, query_bias, key_bias, value_weight, value_bias, output_weight,
        output_bias, first_gain, first_bias, inner_weight, inner_bias, outer_weight, outer_bias, second_gain,
        second_bias, cotangent,
        layer_store, first_store, chances_store, sent_store, stats_store, query_store, key_store, value_store,
        early_send_low, early_send_high, early_keep,
        x_all, s_ref, mixture_ref, log_ref, active_ref, slope_ref, grads_out, terms_ref, sums_ref, small_ref, bias_ref, sems,
    ) = rest
    block = block_ref[0]
    length = length_ref[0]
    size, model_width = layer_store.shape
    head_dim = model_width // HEADS
    factor = LOG2E / math.sqrt(3.0 * head_dim)
    query_out, key_out, value_out = query_store.ref, key_store.ref, value_store.ref
    chances_out, sent_out = chances_store.ref, sent_store.ref
    for pair in range(HEADS // 2):
        slab_copy(terms, terms_ref, sems, pair).start()
    own, core, far, diagonal, rel_query_out = ready(own, core, far, diagonal, rel_query)
    query_weight, key_weight, query_bias, key_bias = ready(query_weight, key_weight, query_bias, key_bias)
    value_weight, value_bias = ready(value_weight, value_bias)
    for at, rows in placed(block, size, own, core, far, diagonal):
        x_all[pl.ds(at, size), :] = rows[...]
    query_out[...] = affine(x_all[...], query_weight, query_bias).astype(BF)
    key_out[...] = affine(x_all[...], key_weight, key_bias).astype(BF)
    value_out[...] = affine(x_all[...], value_weight, value_bias).astype(BF)
    step = lanes((1, 4 * size))
    position = ((block + 3 + step // size) % 4) * size + step % size
    mask_row = jnp.where(position < length, 0.0, -1e30)
    stat_lane = lanes((size, 128))
    log_ref[...] = jnp.zeros_like(log_ref)

    def pair_step(pair, carry):
        columns = pair_columns(pair)
        query_own = stacked(query_out[size : 2 * size, columns])
        slab_copy(terms, terms_ref, sems, pair).wait()
        s_ref[...] = terms_ref[pair]
        other_terms(
            block,
            s_ref,
            lambda slot: key_out[slot * size : (slot + 1) * size, columns],
            stacked(rel_query_out[:, columns]),
            0,
            (0, 2, 3),
        )
        before = s_ref[:, :size] + nt(query_own, key_out[:size, columns])
        s_ref[:, :size] = before * factor + mask_row[:, :size]
        s_ref[:, size : 2 * size] = s_ref[:, size : 2 * size] * factor + mask_row[:, size : 2 * size]
        after = s_ref[:, 2 * size :] + nt(query_own, key_out[2 * size :, columns])
        s_ref[:, 2 * size :] = after * factor + mask_row[:, 2 * size :]
        top = jnp.max(s_ref[...], axis=1, keepdims=True)
        raised = jnp.exp2(s_ref[...] - top)
        s_ref[...] = raised
        row_sum = jnp.sum(raised, axis=1, keepdims=True)
        chances = (s_ref[...] * (1.0 / row_sum)).astype(BF)
        chances_out[pair] = chances
        log_total = top + jnp.log2(row_sum)
        for side in range(2):
            log_ref[...] = jnp.where(
                stat_lane % 8 == 2 * pair + side, log_total[side * size : (side + 1) * size], log_ref[...]
            )
        total = nn(abreast(chances), stacked(value_out[:, columns]))
        mixture_ref[:, columns] = total
        return carry

    lax.fori_loop(0, HEADS // 2, pair_step, 0)

    (
        output_weight, output_bias, first_gain, first_bias, inner_weight, inner_bias, outer_weight, outer_bias,
        second_gain, second_bias, cotangent,
    ) = ready(
        output_weight, output_bias, first_gain, first_bias, inner_weight, inner_bias, outer_weight, outer_bias,
        second_gain, second_bias, cotangent,
    )
    inner_width = inner_weight.shape[1]
    chunks = inner_width // model_width
    mixture_low = mixture_ref[...].astype(BF)
    first_sum = own[...].astype(F32) + affine(mixture_low, output_weight, output_bias)
    first_hat, first_rate = norm_forward(first_sum)
    normed = (first_hat * as_row(first_gain) + as_row(first_bias)).astype(BF)
    root_half = math.sqrt(0.5)
    density = 1.0 / math.sqrt(2.0 * math.pi)

    sums_ref[...] = normed.astype(F32) + as_row(outer_bias)
    bias_ref[...] = as_row(inner_bias)

    def chunk_span(chunk):
        return pl.ds(chunk * model_width, model_width)

    def ahead(chunk, carry):
        span = chunk_span(chunk)
        inner_pre = nn(normed, inner_weight[:, span]) + bias_ref[:, span]
        below = 0.5 + 0.5 * lax.erf(inner_pre * root_half)
        slope_ref[:, span] = below + inner_pre * density * jnp.exp(-0.5 * inner_pre * inner_pre)
        active = (inner_pre * below).astype(BF)
        active_ref[:, span] = active
        sums_ref[...] += nn(active, outer_weight[span, :])
        return carry

    for chunk in range(chunks):
        ahead(chunk, 0)
    second_sum = sums_ref[...]
    second_hat, second_rate = norm_forward(second_sum)
    gain = as_row(second_gain)
    layer_store.ref[...] = second_hat * gain + as_row(second_bias)
    layer_store.push()
    cot = cotangent[...].astype(F32)
    grad_second = norm_backward(cot * gain, second_hat, second_rate)
    grad_outer = grad_second.astype(BF)
    outer_at, inner_at, output_at, small_at = 0, inner_width, 2 * inner_width, 2 * inner_width + model_width
    grads_out[small_at + 16 :, :] = jnp.zeros((grads_out.shape[0] - small_at - 16, model_width), BF)
    small_ref[...] = jnp.zeros_like(small_ref)
    for k, values in enumerate((column_sum(grad_outer), column_sum(cot * second_hat), column_sum(cot))):
        small_ref[k : k + 1, :] = values
    sums_ref[...] = grad_second
    outer_turned, normed_turned = grad_outer.T, normed.T

    def back(chunk, carry):
        span = chunk_span(chunk)
        at = outer_at + chunk * model_width
        grads_out[pl.ds(at, model_width), :] = nn(outer_turned, active_ref[:, span]).astype(BF)
        grad_inner = (nt(grad_outer, outer_weight[span, :]) * slope_ref[:, span]).astype(BF)
        small_ref[pl.ds(3 + chunk, 1), :] = column_sum(grad_inner)
        at = inner_at + chunk * model_width
        grads_out[pl.ds(at, model_width), :] = nn(normed_turned, grad_inner).astype(BF)
        sums_ref[...] += nt(grad_inner, inner_weight[:, span])
        return carry

    for chunk in range(chunks):
        back(chunk, 0)
    early_sends = (early_send_low, early_send_high)
    push_half(0, block % 2, place_ref[0], grads_out, early_sends, early_keep)
    grad_normed = sums_ref[...].astype(BF).astype(F32)
    grad_first = norm_backward(grad_normed * as_row(first_gain), first_hat, first_rate)
    first_store.ref[...] = grad_first
    first_store.push()
    grad_branch = grad_first.astype(BF)
    grads_out[output_at : output_at + model_width, :] = tn(mixture_low, grad_branch).astype(BF)
    for k, values in enumerate(
        (column_sum(grad_normed * first_hat), column_sum(grad_normed), column_sum(grad_branch))
    ):
        small_ref[3 + chunks + k : 4 + chunks + k, :] = values
    grads_out[small_at : small_at + 16, :] = small_ref[...].astype(BF)
    push_half(1, block % 2, place_ref[0], grads_out, early_sends, early_keep)
    grad_mixture = nt(grad_branch, output_weight[...]).astype(BF)
    sent_out[:size, :] = grad_mixture
    along = grad_mixture.astype(F32) * mixture_ref[...]
    stats = log_ref[...]
    for head in range(HEADS):
        columns = slice((head // 2) * 128, (head // 2 + 1) * 128)
        delta = jnp.sum(of_head(along[:, columns], head % 2), axis=1, keepdims=True)
        stats = jnp.where((stat_lane < 16) & (stat_lane % 8 == head), delta, stats)
    stats_store.ref[...] = stats
    upper = stats.astype(BF).astype(F32)
    parts = jnp.where((stat_lane // 8) % 2 == 0, upper, stats - upper).T[:32, :]
    sent_out[size:, :size] = parts.astype(BF)
    sent_out[size:, size:] = jnp.zeros((32, model_width - size), BF)
    sent_store.push()


def position_backward(block, grad_scores, flip, other_pair, ext_pair, own_rows_back, wall_ref, shift):
    size = flip.shape[0]
    full = grad_scores.shape[1]
    grad_back = nn(flip, abreast(grad_scores)).astype(BF)
    for side in range(2):
        unskewed(block, wall_ref.at[pl.ds(side * size, size)], grad_back[:, side * full : (side + 1) * full], shift)
    row_grad = nn(grad_back, stacked(other_pair)) + nn(abreast(wall_ref[...]), stacked(ext_pair))
    return row_grad, tn(stacked(own_rows_back), wall_ref[...])


def query_kernel(
    block_ref, rel_key, query_all, sent, stats, value_all, key_all, chances_load,
    query_store, rel_key_grad_store,
    ext_ref, wall_ref, back_ref, rows_ref,
):
    block = block_ref[0]
    size, model_width = query_store.shape
    scale = 1.0 / math.sqrt(3.0 * (model_width // HEADS))
    flip = reversal(size)
    chances = chances_load.buffer
    rel_key, query_all, sent, stats, value_all, key_all = ready(rel_key, query_all, sent, stats, value_all, key_all)
    extend_table(ext_ref, rel_key)
    back_ref[...] = nn(flip, query_all[size : 2 * size, :]).astype(BF)
    stat_lane = lanes((size, 128))

    def pair_step(pair, carry):
        columns = pair_columns(pair)
        delta = jnp.concatenate(
            [
                jnp.sum(jnp.where(stat_lane == head, stats[...], 0.0), axis=1, keepdims=True)
                for head in (2 * pair, 2 * pair + 1)
            ],
            axis=0,
        )
        grad_chances = nt(stacked(sent[:size, columns]), value_all[:, columns])
        grad_scores = (chances[pair].astype(F32) * (grad_chances - delta)).astype(BF)
        row_grad, table = position_backward(
            block, grad_scores, flip, key_all[:, columns], ext_ref[:, columns], back_ref[:, columns], wall_ref, 3 * size
        )
        rows_ref[:, columns] = (row_grad * scale).astype(BF)
        rel_key_grad_store.ref[columns, :] = table_grad(table, scale)
        return carry

    lax.fori_loop(0, HEADS // 2, pair_step, 0)
    query_store.ref[...] = nn(flip, rows_ref[...]).astype(BF)


def key_kernel(
    block_ref, length_ref, place_ref, rel_query, key_all, rel_key, query_all, value_all,
    sent_own, sent_core, sent_far, sent_diagonal,
    own, relative, grad_query, grad_rel_key, query_weight, key_weight, value_weight, grad_first,
    tokens_store, late_send_low, late_send_high, late_keep,
    grads_out, key_rows_ref, value_rows_ref, rel_grad_ref,
    sent_ref, s_ref, grad_ref, ext_ref, wall_ref, back_ref, stat_ref,
):
    block = block_ref[0]
    length = length_ref[0]
    size, model_width = key_rows_ref.shape
    scale = 1.0 / math.sqrt(3.0 * (model_width // HEADS))
    factor = LOG2E * scale
    flip = reversal(size)
    rel_query, key_all, rel_key, query_all, value_all = ready(rel_query, key_all, rel_key, query_all, value_all)
    extend_table(ext_ref, rel_query)
    back_ref[...] = nn(flip, key_all[size : 2 * size, :]).astype(BF)
    for at, rows in placed(block, size, *ready(sent_own, sent_core, sent_far, sent_diagonal)):
        sent_ref[pl.ds(at, size), :] = rows[:size, :]
        parts = rows[size:, :size].astype(F32)
        stat_ref[0:8, pl.ds(at, size)] = parts[0:8, :] + parts[8:16, :]
        stat_ref[8:16, pl.ds(at, size)] = parts[16:24, :] + parts[24:32, :]
    position = block * size + lax.broadcasted_iota(jnp.int32, (size, 1), 0)
    mask_column = jnp.where(position < length, 0.0, -1e30)

    def pair_step(pair, carry):
        columns = pair_columns(pair)
        key_pair = stacked(key_all[size : 2 * size, columns])
        own_terms(block, s_ref, key_pair, rel_query[:, columns], 0)
        other_terms(
            block,
            s_ref,
            lambda slot: query_all[slot * size : (slot + 1) * size, columns],
            stacked(rel_key[:, columns]),
            1,
            range(4),
        )
        content = nt(key_pair, query_all[:, columns])
        for side in range(2):
            rows = slice(side * size, (side + 1) * size)
            less = mask_column - stat_ref[pl.ds(8 + 2 * pair + side, 1), :]
            s_ref[rows, :] = jnp.exp2((s_ref[rows, :] + content[rows]) * factor + less)
        value_grad = nn(abreast(s_ref[...].astype(BF)), stacked(sent_ref[:, columns]))
        grad_chances = nt(stacked(value_all[size : 2 * size, columns]), sent_ref[:, columns])
        for side in range(2):
            rows = slice(side * size, (side + 1) * size)
            delta = stat_ref[pl.ds(2 * pair + side, 1), :]
            grad_ref[rows, :] = (s_ref[rows, :] * (grad_chances[rows] - delta)).astype(BF)
        row_grad, table = position_backward(
            block, grad_ref[...], flip, query_all[:, columns], ext_ref[:, columns], back_ref[:, columns], wall_ref,
            3 * size + 1,
        )
        key_rows_ref[:, columns] = (row_grad * scale).astype(BF)
        value_rows_ref[:, columns] = value_grad.astype(BF)
        rel_grad_ref[columns, :] = table_grad(table, scale)
        return carry

    lax.fori_loop(0, HEADS // 2, pair_step, 0)
    own, relative, grad_query, grad_rel_key = ready(own, relative, grad_query, grad_rel_key)
    rel = relative.shape[0]
    grad_key = nn(flip, key_rows_ref[...]).astype(BF)
    grad_value = value_rows_ref[...]
    rel_query_grad = rel_grad_ref[...]
    rel_key_grad = grad_rel_key[...]
    query_low = rel_query_grad.astype(BF)
    key_low = nn(rel_key_grad.astype(BF), reversal(rel)).astype(BF)
    tokens = own[...]
    table = relative[...]
    grads_out[0:model_width, :] = (tn(tokens, grad_query[...]) + tt(table, query_low)).astype(BF)
    grads_out[model_width : 2 * model_width, :] = (tn(tokens, grad_key) + tt(table, key_low)).astype(BF)
    grads_out[2 * model_width : 3 * model_width, :] = tn(tokens, grad_value).astype(BF)
    late_sends = (late_send_low, late_send_high)
    push_half(0, block % 2, place_ref[0], grads_out, late_sends, late_keep)
    table_at = 3 * model_width
    query_weight, key_weight, value_weight, grad_first = ready(query_weight, key_weight, value_weight, grad_first)
    grads_out[table_at : table_at + rel, :] = (
        tt(query_low, query_weight[...]) + tt(key_low, key_weight[...])
    ).astype(BF)
    small_at = table_at + rel
    grads_out[small_at + 16 :, :] = jnp.zeros((grads_out.shape[0] - small_at - 16, model_width), BF)
    ones = jnp.ones((8, rel), BF)

    def lane_sums(values):
        high = values.astype(BF)
        low = (values - high.astype(F32)).astype(BF)
        return (nt(ones, high) + nt(ones, low))[0:1, :]

    small = [
        column_sum(grad_query[...]) + lane_sums(rel_query_grad),
        column_sum(grad_key) + lane_sums(rel_key_grad),
        column_sum(grad_value),
        jnp.zeros((13, model_width), F32),
    ]
    grads_out[small_at : small_at + 16, :] = jnp.concatenate(small, axis=0).astype(BF)
    push_half(1, block % 2, place_ref[0], grads_out, late_sends, late_keep)
    tokens_store.ref[...] = (
        nt(grad_query[...], query_weight[...])
        + nt(grad_key, key_weight[...])
        + nt(grad_value, value_weight[...])
        + grad_first[...]
    )


class Load:
    def __init__(self, source, buffer, sem):
        self.copy, self.buffer, self.waiting = pltpu.make_async_copy(source, buffer, sem), buffer, True
        self.copy.start()

    def ready(self):
        if self.waiting:
            self.copy.wait()
        self.waiting = False
        return self.buffer


def ready(*loads):
    return [load.ready() for load in loads]


class Store:
    def __init__(self, target, buffer, sem):
        self.copy, self.ref, self.shape, self.waiting = pltpu.make_async_copy(buffer, target, sem), buffer, buffer.shape, False

    def push(self):
        self.copy.start()
        self.waiting = True

    def finish(self):
        if not self.waiting:
            self.push()
        self.copy.wait()


class Here:
    def __init__(self, ref):
        self.ref = self.buffer = ref
        self.shape = ref.shape

    def ready(self):
        return self.ref

    def push(self):
        pass

    def finish(self):
        pass


def terms_after(first, terms):
    arrays = in_order(first, [array for array, _, _ in terms])
    return [(array, start, blocks) for array, (_, start, blocks) in zip(arrays, terms)]


class Raw:
    def __init__(self, target, sems):
        self.target, self.sems = target, sems
        self.shape = target.shape

    def push_from(self, source, k, part):
        pltpu.make_async_copy(source, self.target.at[pl.ds(k * part, part)], self.sems.at[k]).start()
        self.part = part

    def finish(self):
        for k in range(self.shape[0] // self.part):
            there = self.target.at[pl.ds(k * self.part, self.part)]
            pltpu.make_async_copy(there, there, self.sems.at[k]).wait()


def push_half(which, core, place, rows_ref, sends, keep):
    half = keep.shape[0]
    part = half // 4

    def source(k):
        return rows_ref.at[pl.ds(pl.multiple_of(which * half + (place ^ k) * part, 16), part)]

    @pl.when(core == which)
    def _():
        for k in range(4):
            keep.push_from(source(k), k, part)

    @pl.when(core != which)
    def _():
        for k in range(4):
            sends[k // 2].push_from(source(k), k % 2, part)


class Kept:
    def __init__(self, *what):
        self.what = what


class Bare:
    def __init__(self, *what):
        self.what = what


class Fetch:
    def __init__(self, what):
        self.what = what


def call(kernel, outs, scratch, *operands, scalars, micros, vmem):
    fetched = [k for k, operand in enumerate(operands) if isinstance(operand, Fetch)]
    bare_in = [k for k, operand in enumerate(operands) if isinstance(operand, Bare)]
    operands = [
        operand.what if isinstance(operand, Fetch) else operand.what[0] if isinstance(operand, Bare) else operand
        for operand in operands
    ]
    bare_out = [k for k, out in enumerate(outs) if isinstance(out, Bare)]
    outs = [out.what if isinstance(out, Bare) else out for out in outs]
    outs = list(outs) + [Kept(operands[k].shape, operands[k].dtype) for k in fetched]
    kept_in = [isinstance(operand, Kept) for operand in operands]
    kept_out = [isinstance(out, Kept) for out in outs]
    operands = [
        operand if k < scalars
        else pltpu.with_memory_space_constraint(operand.what[0], pltpu.VMEM) if kept
        else pltpu.with_memory_space_constraint(operand, pltpu.HBM)
        for k, (operand, kept) in enumerate(zip(operands, kept_in))
    ]
    outs = [out.what if kept else out for out, kept in zip(outs, kept_out)]
    raw = [len(out) > 2 for out in outs]
    loads = [k for k in range(scalars, len(operands)) if not kept_in[k] and k not in bare_in]
    stores = [k for k in range(len(outs)) if not kept_out[k] and k not in bare_out]
    buffered = [k for k in stores if not raw[k]]
    own_loads = [k for k in loads if k not in fetched]

    def body(*refs):
        n, m = len(operands), len(outs)
        ins, results, rest = list(refs[:n]), list(refs[n : n + m]), list(refs[n + m :])
        in_sems, out_sems = rest.pop(), rest.pop()
        buffers = [rest.pop() for _ in range(len(own_loads) + len(buffered))][::-1]
        targets = dict(zip(own_loads, buffers)) | dict(zip(fetched, results[m - len(fetched) :]))
        results = results[: m - len(fetched)]
        for k in range(scalars, n):
            if kept_in[k]:
                ins[k] = Here(ins[k])
        for place, k in enumerate(loads):
            ins[k] = Load(ins[k], targets[k], in_sems.at[place])
        buffers = buffers[len(own_loads) :]
        for k in range(len(results)):
            if kept_out[k]:
                results[k] = Here(results[k])
        for place, k in enumerate(stores):
            if raw[k]:
                results[k] = Raw(results[k], out_sems.at[place])
            else:
                results[k] = Store(results[k], buffers.pop(0), out_sems.at[place, 0])
        kernel(*ins, *results, *rest)
        for k in fetched:
            ins[k].ready()
        for k in stores:
            results[k].finish()

    spaces = [
        pltpu.SMEM if k < scalars else pltpu.VMEM if kept_in[k] else pltpu.HBM for k in range(len(operands))
    ]
    buffers = [(operands[k].shape, operands[k].dtype) for k in own_loads] + [outs[k][:2] for k in buffered]
    return pl.pallas_call(
        body,
        out_shape=[
            pltpu.VMEM(out[0], out[1]) if kept else pltpu.HBM(out[0], out[1])
            for out, kept in zip(outs, kept_out)
        ],
        in_specs=[pl.BlockSpec(memory_space=space) for space in spaces],
        out_specs=[pl.BlockSpec(memory_space=pltpu.VMEM if kept else pltpu.HBM) for kept in kept_out],
        scratch_shapes=[
            pltpu.SemaphoreType.DMA(space[0]) if space[1] is None else pltpu.VMEM(*space)
            for space in list(scratch) + buffers
        ]
        + [pltpu.SemaphoreType.DMA((max(len(stores), 1), 4)), pltpu.SemaphoreType.DMA((max(len(loads), 1),))],
        compiler_params=pltpu.CompilerParams(vmem_limit_bytes=vmem * MIB),
        cost_estimate=pl.CostEstimate(flops=micros * 10**9, bytes_accessed=micros * 10**6, transcendentals=0),
    )(*operands)


class Group:
    def __init__(self, blk_count, dp_count, bits):
        self.blk_count, self.dp_count, self.bits = blk_count, dp_count, bits
        self.size = 2 ** len(bits)
        place = {"blk": lax.axis_index("blk"), "dp": lax.axis_index("dp")}
        self.digits = [(place[axis] >> (bit.bit_length() - 1)) & 1 for axis, bit in bits]
        self.me = sum(digit << k for k, digit in enumerate(self.digits))

    def pairs(self, mask):
        change = {"blk": 0, "dp": 0}
        for k, (axis, bit) in enumerate(self.bits):
            if mask >> k & 1:
                change[axis] |= bit
        return [
            (blk * self.dp_count + dp, (blk ^ change["blk"]) * self.dp_count + (dp ^ change["dp"]))
            for blk in range(self.blk_count)
            for dp in range(self.dp_count)
        ]

    def send(self, values, mask):
        return lax.ppermute(values, ("blk", "dp"), self.pairs(mask))

    def scatter(self, terms):
        def part(index):
            return [
                (array, first + index * (blocks // self.size), blocks // self.size) for array, first, blocks in terms
            ]

        outs = [total(part(self.me ^ mask)) for mask in range(1, self.size)]
        arrived = [self.send(out, mask + 1) for mask, out in enumerate(outs)]
        return outs, part(self.me) + [whole(array) for array in arrived]

    def pieces(self, held):
        return [held] + [self.send(held, mask) for mask in range(1, self.size)]

    def gather(self, held):
        return self.arrange(self.pieces(held))

    def arrange(self, parts):
        for k, digit in enumerate(self.digits):
            parts = [
                jnp.where(digit == 0, parts[q], parts[q ^ (1 << k)]) for q in range(self.size)
            ]
        return jnp.concatenate(parts, axis=0)


def groups_of(blk_count, dp_count):
    bits, bit = [], 2
    while bit < dp_count:
        bits.append(("dp", bit))
        bit *= 2
    groups = [[("blk", 1)], [("blk", 2), ("dp", 1)]]
    groups += [bits[k : k + 2] for k in range(0, len(bits), 2)]
    return [Group(blk_count, dp_count, group) for group in groups]


def whole(array):
    return array, 0, array.shape[0]


def total(terms):
    spans = [
        array[first : first + blocks] if isinstance(first, int) else lax.dynamic_slice_in_dim(array, first, blocks, 0)
        for array, first, blocks in terms
    ]
    return sum(span.astype(F32) for span in spans).astype(BF)


def in_order(first, then):
    return lax.optimization_barrier((first, then))[1]


def halves_to_scratch(core_ref, place_ref, held, arrived, both_ref):
    held, arrived = ready(held, arrived)
    half = held.shape[0]
    part = half // 4
    for k in range(4):
        at = (place_ref[0] ^ k) * part
        span = slice(k * part, (k + 1) * part)
        both_ref[pl.ds(pl.multiple_of(core_ref[0] * half + at, 16), part), :] = held[span, :]
        both_ref[pl.ds(pl.multiple_of((1 - core_ref[0]) * half + at, 16), part), :] = arrived[span, :]


def early_kernel(
    core_ref, place_ref, held, arrived,
    outer_weight, inner_weight, output_weight, outer_bias, second_gain, second_bias, inner_bias, first_gain, first_bias,
    output_bias,
    both_ref,
):
    halves_to_scratch(core_ref, place_ref, held, arrived, both_ref)
    inner_width, width = outer_weight.shape
    chunks = inner_width // width
    for chunk in range(chunks):
        span = slice(chunk * width, (chunk + 1) * width)
        outer_weight.ref[span, :] = both_ref[span, :].T.astype(F32)
    outer_weight.push()
    for chunk in range(chunks):
        at = inner_width + chunk * width
        inner_weight.ref[:, chunk * width : (chunk + 1) * width] = both_ref[at : at + width, :].astype(F32)
    at = 2 * inner_width
    output_weight.ref[...] = both_ref[at : at + width, :].astype(F32)
    output_weight.push()
    small = both_ref[at + width : at + width + 16, :].astype(F32)

    def vector(out, row):
        out.ref[...] = small[row, :]
        out.push()

    vector(outer_bias, 0)
    vector(second_gain, 1)
    vector(second_bias, 2)
    inner_bias.ref[...] = jnp.concatenate([small[3 + k : 4 + k, :] for k in range(chunks)], axis=1)[0, :]
    inner_bias.push()
    vector(first_gain, 3 + chunks)
    vector(first_bias, 4 + chunks)
    vector(output_bias, 5 + chunks)


def late_kernel(mine, shapes, core_ref, place_ref, held, *rest):
    outs, (rows_ref, wide_ref, vector_ref, sems) = rest[-11:-4], rest[-4:]
    query_weight, query_bias, key_weight, key_bias, value_weight, value_bias, relative = outs
    half, width = rows_ref.shape
    part = half // 4
    rel = relative.shape[0]
    for k in range(4):
        at = pl.multiple_of((place_ref[0] ^ k) * part, 16)
        rows_ref[pl.ds(at, part), :] = held[k * part : (k + 1) * part, :]
    split = half - 2 * width
    which = core_ref[0] if mine else 1 - core_ref[0]

    def copy(spans):
        copies = []
        for k, (at, rows, out, start) in enumerate(spans):
            wide_ref[at : at + rows, :] = rows_ref[at : at + rows, :].astype(F32)
            one = pltpu.make_async_copy(wide_ref.at[pl.ds(at, rows)], out.at[pl.ds(start, rows)], sems.at[k])
            one.start()
            copies.append(one)
        return copies

    @pl.when(which == 0)
    def _():
        spans = ((0, width, query_weight, 0), (width, width, key_weight, 0), (2 * width, split, value_weight, 0))
        for one in copy(spans):
            one.wait()

    @pl.when(which == 1)
    def _():
        rest_rows = width - split
        copies = copy(((rest_rows, rel, relative, 0), (0, rest_rows, value_weight, split)))
        small = rows_ref[rest_rows + rel : rest_rows + rel + 16, :].astype(F32)
        for k, out in enumerate((query_bias, key_bias, value_bias)):
            vector_ref[k, :] = small[k, :]
            one = pltpu.make_async_copy(vector_ref.at[k], out, sems.at[2 + k])
            one.start()
            copies.append(one)
        for one in copies:
            one.wait()


def late_call(mine, shapes, core, place, held, *before):
    hbm, smem = pl.BlockSpec(memory_space=pltpu.HBM), pl.BlockSpec(memory_space=pltpu.SMEM)
    width = held.shape[1]
    return pl.pallas_call(
        functools.partial(late_kernel, mine, shapes),
        out_shape=[pltpu.HBM(shape, F32) for shape in shapes],
        in_specs=[smem, smem, pl.BlockSpec(memory_space=pltpu.VMEM)] + [hbm] * len(before),
        out_specs=[hbm] * len(shapes),
        scratch_shapes=[
            pltpu.VMEM(held.shape, BF),
            pltpu.VMEM(held.shape, F32),
            pltpu.VMEM((8, width), F32),
            pltpu.SemaphoreType.DMA((5,)),
        ],
        input_output_aliases={3 + k: k for k in range(len(before))},
        compiler_params=pltpu.CompilerParams(vmem_limit_bytes=10 * MIB),
        cost_estimate=pl.CostEstimate(flops=2 * 10**9, bytes_accessed=2 * 10**6, transcendentals=0),
    )(core, place, pltpu.with_memory_space_constraint(held, pltpu.VMEM), *before)


def on_device(
    blk_count, dp_count,
    tokens, lengths, query_weight, query_bias, key_weight, key_bias, value_weight, value_bias,
    output_weight, output_bias, first_gain, first_bias, inner_weight, inner_bias, outer_weight, outer_bias,
    second_gain, second_bias, relative_table, cotangent,
):
    seq_count, size, width = tokens.shape
    rel = relative_table.shape[0]
    inner_width = inner_weight.shape[1]
    own = tokens[0]
    block = lax.axis_index("blk").astype(jnp.int32).reshape(1)
    groups = groups_of(blk_count, dp_count)
    chips = groups[1:]
    place = chips[0].me.astype(jnp.int32).reshape(1)
    shards = blk_count * dp_count

    def along(values, bit):
        return lax.ppermute(values, "blk", [(i, i ^ bit) for i in range(blk_count)])

    def blocks(rows, share):
        return rows.reshape(shards // share, -1, width)

    def flat(values):
        return values.reshape(-1, width)

    def first_terms(keep, low, high):
        arrived = [groups[0].send(blocks(piece, 4), 1) for piece in (low, high)]
        keep, part = blocks(keep, 2), shards // 8
        return [[(keep, k * part, part), (arrived[k // 2], k % 2 * part, part)] for k in range(4)]

    def first_scatter(parts):
        outs = [total(terms) for terms in parts[1:]]
        return outs, parts[0] + [whole(chips[0].send(out, k + 1)) for k, out in enumerate(outs)]

    core = along(own, 1)
    far = along(own, 2)
    diagonal = along(own, 3)
    full = blk_count * size
    (
        rel_query, rel_key, terms, relative_kept, query_weight, key_weight, query_bias, key_bias, own, value_weight, value_bias,
    ) = call(
        first_kernel,
        [Kept((rel, width), BF), Kept((rel, width), BF), Bare((HEADS // 2, 2 * size, full), F32)],
        [((size, width), BF), ((size, width), BF), ((HEADS // 2, 2 * size, full), F32), ((HEADS // 2,), None)],
        block,
        *map(Fetch, (relative_table, query_weight, key_weight, query_bias, key_bias, own, value_weight, value_bias)),
        scalars=1, micros=9, vmem=14,
    )
    (
        layer_out, grad_first, chances, sent, stats, query_all, key_all, value_all,
        early_send_low, early_send_high, early_keep,
    ) = call(
        forward_kernel,
        [
            ((size, width), F32),
            Kept((size, width), F32),
            Kept((HEADS // 2, 2 * size, full), BF),
            Kept((size + 32, width), BF),
            Kept((size, 128), F32),
            Kept((full, width), BF),
            Kept((full, width), BF),
            Kept((full, width), BF),
            ((EARLY_ROWS // 4, width), BF, "raw"),
            ((EARLY_ROWS // 4, width), BF, "raw"),
            ((EARLY_ROWS // 2, width), BF, "raw"),
        ],
        [
            ((full, width), BF),
            ((2 * size, full), F32),
            ((size, width), F32),
            ((size, 128), F32),
            ((size, inner_width), BF),
            ((size, inner_width), F32),
            ((EARLY_ROWS, width), BF),
            ((HEADS // 2, 2 * size, full), F32),
            ((size, width), F32),
            ((16, width), F32),
            ((1, inner_width), F32),
            ((HEADS // 2,), None),
        ],
        block, lengths, place,
        *map(Kept, (own, core, far, diagonal, rel_query, rel_key)),
        Bare(terms),
        *map(Kept, (query_weight, key_weight, query_bias, key_bias, value_weight, value_bias)),
        output_weight, output_bias, first_gain, first_bias, inner_weight, inner_bias, outer_weight, outer_bias,
        second_gain, second_bias, cotangent[0],
        scalars=3, micros=20, vmem=26,
    )
    early_parts = first_terms(early_keep, early_send_low, early_send_high)
    sent_far = along(sent, 2)
    sent_core = along(sent, 1)
    position_scratch = [((2 * rel, width), BF), ((2 * size, 2 * rel), BF), ((size, width), BF)]
    grad_query, grad_rel_key = call(
        query_kernel,
        [Kept((size, width), BF), Kept((width, rel), F32)],
        position_scratch + [((size, width), BF)],
        block, *map(Kept, (rel_key, query_all, sent, stats, value_all, key_all, chances)),
        scalars=1, micros=8, vmem=10,
    )
    sent_diagonal = along(in_order(grad_query, sent_far), 1)
    key_scratch = (
        [((full, width), BF), ((2 * size, full), F32), ((2 * size, full), BF)] + position_scratch + [((16, full), F32)]
    )
    key_arrays = tuple(
        map(Kept, (rel_query, key_all, rel_key, query_all, value_all, sent, sent_core, sent_far, sent_diagonal))
    )
    sending, early_terms = first_scatter(early_parts)
    grad_tokens, late_send_low, late_send_high, late_keep = call(
        key_kernel,
        [((size, width), F32)] + [((LATE_ROWS // 4, width), BF, "raw")] * 2 + [((LATE_ROWS // 2, width), BF, "raw")],
        [((LATE_ROWS, width), BF), ((size, width), BF), ((size, width), BF), ((width, rel), F32)] + key_scratch,
        in_order(sending, block), lengths, place, *key_arrays,
        *map(Kept, (own, relative_kept, grad_query, grad_rel_key, query_weight, key_weight, value_weight, grad_first)),
        scalars=3, micros=17, vmem=18,
    )
    late_parts = first_terms(late_keep, late_send_low, late_send_high)
    early_terms = terms_after(late_send_low, early_terms)
    for group in chips[1:]:
        sending, early_terms = group.scatter(early_terms)
        late_parts = [terms_after(sending, terms) for terms in late_parts]
    sending_xy, late_terms = first_scatter(late_parts)
    arrived = [array for array, _, _ in late_terms[1 - chips[0].size :]]
    early_held = total(early_terms)
    for group in reversed(chips[2:]):
        early_held = group.gather(early_held)
    early_parts = chips[1].pieces(early_held)
    for group in chips[1:]:
        sending_z, late_terms = group.scatter(late_terms)
    z_arrived = [array for array, _, _ in late_terms[1 - chips[-1].size :]]
    early_parts = in_order(z_arrived[0], early_parts)
    early_pieces = chips[0].pieces(chips[1].arrange(early_parts))
    late_held = total(late_terms)
    for group in reversed(chips[2:]):
        late_held = group.gather(late_held)
    late_parts = chips[1].pieces(late_held)
    late_parts, early_pieces[1] = lax.optimization_barrier((late_parts, early_pieces[1]))
    late_held = chips[1].arrange(late_parts)
    early_held = jnp.concatenate(early_pieces, axis=0)
    late_pieces = chips[0].pieces(late_held)
    my_core = groups[0].me.astype(jnp.int32).reshape(1)
    square, vector = ((width, width), F32), ((width,), F32)
    (
        g_outer_weight, g_inner_weight, g_output_weight, g_outer_bias, g_second_gain, g_second_bias, g_inner_bias,
        g_first_gain, g_first_bias, g_output_bias,
    ) = call(
        early_kernel,
        [((inner_width, width), F32), ((width, inner_width), F32), square, vector, vector, vector,
         ((inner_width,), F32), vector, vector, vector],
        [((EARLY_ROWS, width), BF)],
        my_core, place, *(Kept(flat(piece)) for piece in groups[0].pieces(early_held)),
        scalars=2, micros=4, vmem=14,
    )
    late_held = jnp.concatenate(in_order(g_output_bias, late_pieces), axis=0)
    own_half, other_half = (flat(piece) for piece in groups[0].pieces(late_held))
    shapes = [square[0], vector[0]] * 3 + [(rel, width)]
    late_grads = late_call(True, shapes, my_core, place, own_half)
    (
        g_query_weight, g_query_bias, g_key_weight, g_key_bias, g_value_weight, g_value_bias, g_relative,
    ) = late_call(False, shapes, my_core, place, other_half, *late_grads)
    return (
        layer_out[None], grad_tokens[None], g_query_weight, g_query_bias, g_key_weight, g_key_bias,
        g_value_weight, g_value_bias, g_output_weight, g_output_bias, g_first_gain, g_first_bias,
        g_inner_weight, g_inner_bias, g_outer_weight, g_outer_bias, g_second_gain, g_second_bias, g_relative,
    )


def solution(mesh):
    blk_count, dp_count = mesh.shape["blk"], mesh.shape["dp"]
    rows = P("dp", "blk", None)
    in_specs = (rows, P("dp")) + (P(),) * 17 + (rows,)
    out_specs = (rows, rows) + (P(),) * 17

    def whole(*arrays):
        return on_device(blk_count, dp_count, *arrays)

    return jax.shard_map(whole, mesh=mesh, in_specs=in_specs, out_specs=out_specs, check_vma=False)
```

```python
import functools
import math

import jax
import jax.numpy as jnp
from jax import lax
from jax.experimental import pallas as pl
from jax.experimental.pallas import tpu as pltpu
from jax.sharding import PartitionSpec as P

HEADS = 6
BF = jnp.bfloat16
F32 = jnp.float32
LOG2E = math.log2(math.e)
EPS = 1e-07
MIB = 1024 * 1024
QUERY_SPLIT = 1
EARLY_ROWS = 3584
LATE_ROWS = 1792


def nn(left, right):
    return lax.dot_general(left, right, (((1,), (0,)), ((), ())), preferred_element_type=F32)


def nt(left, right):
    return lax.dot_general(left, right, (((1,), (1,)), ((), ())), preferred_element_type=F32)


def tn(left, right):
    return lax.dot_general(left, right, (((0,), (0,)), ((), ())), preferred_element_type=F32)


def tt(left, right):
    return lax.dot_general(left, right, (((0,), (1,)), ((), ())), preferred_element_type=F32)


def lanes(shape):
    return lax.broadcasted_iota(jnp.int32, shape, len(shape) - 1)


def of_head(values, head):
    inside = (lanes(values.shape) // 64) == head
    return jnp.where(inside, values, jnp.zeros_like(values))


def stacked(values):
    return jnp.concatenate([of_head(values, 0), of_head(values, 1)], axis=0)


def abreast(values):
    rows = values.shape[0] // 2
    return jnp.concatenate([values[:rows], values[rows:]], axis=1)


def pair_columns(pair):
    if isinstance(pair, int):
        return slice(pair * 128, (pair + 1) * 128)
    return pl.ds(pl.multiple_of(pair * 128, 128), 128)


def wide(column, width):
    return jnp.broadcast_to(column, (column.shape[0], width))


def reversal(size):
    rows = lax.broadcasted_iota(jnp.int32, (size, size), 0)
    cols = lax.broadcasted_iota(jnp.int32, (size, size), 1)
    return jnp.where(rows + cols == size - 1, 1.0, 0.0).astype(BF)


def placed(block, size, own, core, far, diagonal):
    even = block % 2 == 0
    core_at = pl.multiple_of(jnp.where(even, 2 * size, 0), size)
    diagonal_at = pl.multiple_of(jnp.where(even, 0, 2 * size), size)
    return (size, own), (3 * size, far), (core_at, core), (diagonal_at, diagonal)


def rolled_window(source, shift):
    half = source.shape[0] // 2
    upper = pltpu.roll(source[:half, half:], shift, 1, stride=1, stride_axis=0)[:, half:]
    lower = pltpu.roll(source[half:, : 3 * half], shift, 1, stride=1, stride_axis=0)[:, half:]
    return jnp.concatenate([upper, lower], axis=0)


def own_terms(block, s_ref, own_rows, own_table, shift):
    size = own_rows.shape[0] // 2
    rel = own_table.shape[0]
    scores = nt(own_rows, own_table)
    last, first = scores[:, rel - 1 : rel], scores[:, 0:1]
    source = jnp.concatenate([scores, wide(last, size), wide(first, size)], axis=1)
    for side in range(2):
        rows = slice(side * size, (side + 1) * size)
        s_ref[rows, : 3 * size] = pltpu.roll(source[rows], shift, 1, stride=1, stride_axis=0)[:, : 3 * size]
    s_ref[:, 3 * size :] = wide(jnp.where(block < 2, last, first), s_ref.shape[1] - 3 * size)


def other_terms(block, s_ref, others, tables, shift, slots):
    size = s_ref.shape[0] // 2
    rel = tables.shape[0] // 2

    def both(start, rows):
        return jnp.concatenate([tables[start : start + rows], tables[rel + start : rel + start + rows]], axis=0)

    def near(slot):
        if slot == 1:
            product = nt(others(slot), tables)
            parts = [product[:, :rel], product[:, rel:]]
        else:
            product = nt(others(slot), both(size if slot == 0 else 0, size))
            parts = [product[:, :size], product[:, size:]]
        if slot == 0:
            parts = [jnp.concatenate([part, wide(part[:, size - 1 : size], size)], axis=1) for part in parts]
        elif slot == 2:
            parts = [jnp.concatenate([wide(part[:, 0:1], size), part], axis=1) for part in parts]
        return [rolled_window(part, shift).T for part in parts]

    def constant(slot):
        rows = others(slot)
        top = nt(both(0, 16), rows)
        bottom = nt(both(rel - 16, 16), rows)
        return [
            s_ref[side * size : (side + 1) * size, 3 * size :]
            + jnp.where(block < 2, top[16 * side : 16 * side + 1], bottom[16 * side + 15 : 16 * side + 16])
            for side in range(2)
        ]

    for slot in slots:
        span = slice(slot * size, (slot + 1) * size)
        terms = near(slot) if slot < 3 else None
        fixed = constant(slot) if slot != 1 else None
        past = block == (0 if slot == 0 else 3)
        for side in range(2):
            rows = slice(side * size, (side + 1) * size)
            if slot == 1:
                s_ref[rows, span] += terms[side]
            elif slot == 3:
                s_ref[rows, span] = fixed[side]
            else:
                s_ref[rows, span] = jnp.where(past, fixed[side], s_ref[rows, span] + terms[side])


def extend_table(ext_ref, table_ref):
    rel = table_ref.shape[0]
    half = rel // 2
    width = table_ref.shape[1]
    ext_ref[0:rel, :] = table_ref[...]
    ext_ref[rel : rel + half, :] = jnp.broadcast_to(table_ref[rel - 1 : rel, :], (half, width))
    ext_ref[rel + half : 2 * rel, :] = jnp.broadcast_to(table_ref[0:1, :], (half, width))


def unskewed(block, wall_ref, grad_rows, shift):
    size = grad_rows.shape[0]
    before, own, after, far = (grad_rows[:, k * size : (k + 1) * size] for k in range(4))
    none = jnp.zeros_like(own)
    no_before, no_after = block == 0, block == 3
    near = jnp.concatenate(
        [jnp.where(no_before, none, before), own, jnp.where(no_after, none, after), none], axis=1
    )
    rolled = pltpu.roll(near, shift, 1, stride=1, stride_axis=0)
    far = far + jnp.where(no_before, before, jnp.where(no_after, after, none))
    wall_ref[:, : 2 * size] = rolled[:, : 2 * size]
    wall_ref[:, 2 * size : 3 * size] = rolled[:, 2 * size : 3 * size] + jnp.where(block < 2, far, none)
    wall_ref[:, 3 * size :] = rolled[:, 3 * size :] + jnp.where(block < 2, none, far)


def table_grad(sums, scale):
    rel = sums.shape[1] // 2
    half = rel // 2
    over = jnp.sum(sums[:, rel : rel + half], axis=1, keepdims=True)
    under = jnp.sum(sums[:, rel + half :], axis=1, keepdims=True)
    at = lanes((sums.shape[0], rel))
    folded = sums[:, :rel] + jnp.where(at == rel - 1, over, 0.0) + jnp.where(at == 0, under, 0.0)
    return folded * scale


def as_row(vector_ref):
    return vector_ref[...].astype(F32).reshape(1, -1)


def affine(values, weight_ref, bias_ref):
    return nn(values, weight_ref[...]) + as_row(bias_ref)


def norm_forward(values):
    center = values - jnp.mean(values, axis=-1, keepdims=True)
    spread = jnp.mean(center * center, axis=-1, keepdims=True)
    rate = lax.rsqrt(spread + EPS)
    return center * rate, rate


def norm_backward(grad_hat, hat, rate):
    mean_grad = jnp.mean(grad_hat, axis=-1, keepdims=True)
    mean_along = jnp.mean(grad_hat * hat, axis=-1, keepdims=True)
    return rate * (grad_hat - mean_grad - hat * mean_along)


def column_sum(values):
    return jnp.sum(values.astype(F32), axis=0, keepdims=True)


def slab_copy(source, target, sems, k):
    return pltpu.make_async_copy(source.at[k], target.at[k], sems.at[k])


def first_kernel(
    block_ref, relative, query_weight, key_weight, query_bias, key_bias, own, value_weight,
    value_bias, *rest,
):
    rel_query_store, rel_key_store, terms_out, query_ref, key_ref, terms_ref, sems = rest
    block = block_ref[0]
    relative, query_weight, key_weight, query_bias, key_bias = ready(
        relative, query_weight, key_weight, query_bias, key_bias
    )
    rel_query_out, rel_key_out = rel_query_store.ref, rel_key_store.ref
    rel_query_out[...] = affine(relative[...], query_weight, query_bias).astype(BF)
    rel_key_out[...] = affine(
        nn(reversal(relative.shape[0]), relative[...]).astype(BF), key_weight, key_bias
    ).astype(BF)
    (own,) = ready(own)
    size = own.shape[0]
    query_ref[...] = affine(own[...], query_weight, query_bias).astype(BF)
    key_ref[...] = affine(own[...], key_weight, key_bias).astype(BF)

    def pair_step(pair, carry):
        columns = pair_columns(pair)
        s_ref = terms_ref.at[pair]
        query_own = stacked(query_ref[:, columns])
        own_terms(block, s_ref, query_own, rel_key_out[:, columns], 1)
        other_terms(block, s_ref, lambda slot: key_ref[:, columns], stacked(rel_query_out[:, columns]), 0, (1,))
        s_ref[:, size : 2 * size] += nt(query_own, key_ref[:, columns])
        slab_copy(terms_ref, terms_out, sems, pair).start()
        return carry

    lax.fori_loop(0, HEADS // 2, pair_step, 0)
    for pair in range(HEADS // 2):
        slab_copy(terms_ref, terms_out, sems, pair).wait()


def forward_kernel(
    block_ref, length_ref, place_ref, own, core, far, diagonal, rel_query, rel_key, *rest
):
    (
        terms, query_weight, key_weight, query_bias, key_bias, value_weight, value_bias, output_weight,
        output_bias, first_gain, first_bias, inner_weight, inner_bias, outer_weight, outer_bias, second_gain,
        second_bias, cotangent,
        layer_store, first_store, chances_store, sent_store, stats_store, query_store, key_store, value_store,
        early_send_low, early_send_high, early_keep,
        x_all, s_ref, mixture_ref, log_ref, active_ref, slope_ref, grads_out, terms_ref, sums_ref, small_ref, bias_ref, sems,
    ) = rest
    block = block_ref[0]
    length = length_ref[0]
    size, model_width = layer_store.shape
    head_dim = model_width // HEADS
    factor = LOG2E / math.sqrt(3.0 * head_dim)
    query_out, key_out, value_out = query_store.ref, key_store.ref, value_store.ref
    chances_out, sent_out = chances_store.ref, sent_store.ref
    for pair in range(HEADS // 2):
        slab_copy(terms, terms_ref, sems, pair).start()
    for load in (
        output_weight, output_bias, first_gain, first_bias, inner_weight, inner_bias, outer_weight, outer_bias,
        second_gain, second_bias, cotangent,
    ):
        load.begin()
    own, core, far, diagonal, rel_query_out = ready(own, core, far, diagonal, rel_query)
    query_weight, key_weight, query_bias, key_bias = ready(query_weight, key_weight, query_bias, key_bias)
    value_weight, value_bias = ready(value_weight, value_bias)
    for at, rows in placed(block, size, own, core, far, diagonal):
        x_all[pl.ds(at, size), :] = rows[...]
    query_out[...] = affine(x_all[...], query_weight, query_bias).astype(BF)
    key_out[...] = affine(x_all[...], key_weight, key_bias).astype(BF)
    value_out[...] = affine(x_all[...], value_weight, value_bias).astype(BF)
    step = lanes((1, 4 * size))
    position = ((block + 3 + step // size) % 4) * size + step % size
    mask_row = jnp.where(position < length, 0.0, -1e30)
    stat_lane = lanes((size, 128))
    log_ref[...] = jnp.zeros_like(log_ref)

    def pair_step(pair, carry):
        columns = pair_columns(pair)
        query_own = stacked(query_out[size : 2 * size, columns])
        slab_copy(terms, terms_ref, sems, pair).wait()
        s_ref[:, : 3 * size] = terms_ref[pair, :, : 3 * size]
        s_ref[:, 3 * size :] = wide(terms_ref[pair, :, 3 * size : 3 * size + 1], size)
        other_terms(
            block,
            s_ref,
            lambda slot: key_out[slot * size : (slot + 1) * size, columns],
            stacked(rel_query_out[:, columns]),
            0,
            (0, 2, 3),
        )
        before = s_ref[:, :size] + nt(query_own, key_out[:size, columns])
        s_ref[:, :size] = before * factor + mask_row[:, :size]
        s_ref[:, size : 2 * size] = s_ref[:, size : 2 * size] * factor + mask_row[:, size : 2 * size]
        after = s_ref[:, 2 * size :] + nt(query_own, key_out[2 * size :, columns])
        s_ref[:, 2 * size :] = after * factor + mask_row[:, 2 * size :]
        top = jnp.max(s_ref[...], axis=1, keepdims=True)
        raised = jnp.exp2(s_ref[...] - top)
        s_ref[...] = raised
        row_sum = jnp.sum(raised, axis=1, keepdims=True)
        chances = (s_ref[...] * (1.0 / row_sum)).astype(BF)
        chances_out[pair] = chances
        log_total = top + jnp.log2(row_sum)
        for side in range(2):
            log_ref[...] = jnp.where(
                stat_lane % 8 == 2 * pair + side, log_total[side * size : (side + 1) * size], log_ref[...]
            )
        total = nn(abreast(chances), stacked(value_out[:, columns]))
        mixture_ref[:, columns] = total
        return carry

    lax.fori_loop(0, HEADS // 2, pair_step, 0)

    (
        output_weight, output_bias, first_gain, first_bias, inner_weight, inner_bias, outer_weight, outer_bias,
        second_gain, second_bias, cotangent,
    ) = ready(
        output_weight, output_bias, first_gain, first_bias, inner_weight, inner_bias, outer_weight, outer_bias,
        second_gain, second_bias, cotangent,
    )
    inner_width = inner_weight.shape[1]
    chunks = inner_width // model_width
    mixture_low = mixture_ref[...].astype(BF)
    first_sum = own[...].astype(F32) + affine(mixture_low, output_weight, output_bias)
    first_hat, first_rate = norm_forward(first_sum)
    normed = (first_hat * as_row(first_gain) + as_row(first_bias)).astype(BF)
    root_half = math.sqrt(0.5)
    density = 1.0 / math.sqrt(2.0 * math.pi)

    sums_ref[...] = normed.astype(F32) + as_row(outer_bias)
    bias_ref[...] = as_row(inner_bias)

    def chunk_span(chunk):
        return pl.ds(chunk * model_width, model_width)

    def ahead(chunk, carry):
        span = chunk_span(chunk)
        inner_pre = nn(normed, inner_weight[:, span]) + bias_ref[:, span]
        below = 0.5 + 0.5 * lax.erf(inner_pre * root_half)
        slope_ref[:, span] = below + inner_pre * density * jnp.exp(-0.5 * inner_pre * inner_pre)
        active = (inner_pre * below).astype(BF)
        active_ref[:, span] = active
        sums_ref[...] += nn(active, outer_weight[span, :])
        return carry

    for chunk in range(chunks):
        ahead(chunk, 0)
    second_sum = sums_ref[...]
    second_hat, second_rate = norm_forward(second_sum)
    gain = as_row(second_gain)
    layer_store.ref[...] = second_hat * gain + as_row(second_bias)
    layer_store.push()
    cot = cotangent[...].astype(F32)
    grad_second = norm_backward(cot * gain, second_hat, second_rate)
    grad_outer = grad_second.astype(BF)
    outer_at, inner_at, output_at, small_at = 0, inner_width, 2 * inner_width, 2 * inner_width + model_width
    grads_out[small_at + 16 :, :] = jnp.zeros((grads_out.shape[0] - small_at - 16, model_width), BF)
    small_ref[...] = jnp.zeros_like(small_ref)
    for k, values in enumerate((column_sum(grad_outer), column_sum(cot * second_hat), column_sum(cot))):
        small_ref[k : k + 1, :] = values
    sums_ref[...] = grad_second
    outer_turned, normed_turned = grad_outer.T, normed.T

    def back(chunk, carry):
        span = chunk_span(chunk)
        at = outer_at + chunk * model_width
        grads_out[pl.ds(at, model_width), :] = nn(outer_turned, active_ref[:, span]).astype(BF)
        grad_inner = (nt(grad_outer, outer_weight[span, :]) * slope_ref[:, span]).astype(BF)
        small_ref[pl.ds(3 + chunk, 1), :] = column_sum(grad_inner)
        at = inner_at + chunk * model_width
        grads_out[pl.ds(at, model_width), :] = nn(normed_turned, grad_inner).astype(BF)
        sums_ref[...] += nt(grad_inner, inner_weight[:, span])
        return carry

    for chunk in range(chunks):
        back(chunk, 0)
    early_sends = (early_send_low, early_send_high)
    push_half(0, block % 2, place_ref[0], grads_out, early_sends, early_keep)
    grad_normed = sums_ref[...].astype(BF).astype(F32)
    grad_first = norm_backward(grad_normed * as_row(first_gain), first_hat, first_rate)
    first_store.ref[...] = grad_first
    first_store.push()
    grad_branch = grad_first.astype(BF)
    grads_out[output_at : output_at + model_width, :] = tn(mixture_low, grad_branch).astype(BF)
    for k, values in enumerate(
        (column_sum(grad_normed * first_hat), column_sum(grad_normed), column_sum(grad_branch))
    ):
        small_ref[3 + chunks + k : 4 + chunks + k, :] = values
    grads_out[small_at : small_at + 16, :] = small_ref[...].astype(BF)
    push_half(1, block % 2, place_ref[0], grads_out, early_sends, early_keep)
    grad_mixture = nt(grad_branch, output_weight[...]).astype(BF)
    sent_out[:size, :] = grad_mixture
    along = grad_mixture.astype(F32) * mixture_ref[...]
    stats = log_ref[...]
    for head in range(HEADS):
        columns = slice((head // 2) * 128, (head // 2 + 1) * 128)
        delta = jnp.sum(of_head(along[:, columns], head % 2), axis=1, keepdims=True)
        stats = jnp.where((stat_lane < 16) & (stat_lane % 8 == head), delta, stats)
    stats_store.ref[...] = stats
    upper = stats.astype(BF).astype(F32)
    parts = jnp.where((stat_lane // 8) % 2 == 0, upper, stats - upper).T[:32, :]
    sent_out[size:, :size] = parts.astype(BF)
    sent_out[size:, size:] = jnp.zeros((32, model_width - size), BF)
    sent_store.push()


def position_backward(block, grad_scores, flip, other_pair, ext_pair, own_rows_back, wall_ref, shift):
    size = flip.shape[0]
    full = grad_scores.shape[1]
    grad_back = nn(flip, abreast(grad_scores)).astype(BF)
    for side in range(2):
        unskewed(block, wall_ref.at[pl.ds(side * size, size)], grad_back[:, side * full : (side + 1) * full], shift)
    row_grad = nn(grad_back, stacked(other_pair)) + nn(abreast(wall_ref[...]), stacked(ext_pair))
    return row_grad, tn(stacked(own_rows_back), wall_ref[...])


def query_kernel(
    first, last, block_ref, rel_key, query_all, sent, stats, value_all, key_all, chances_load,
    query_store, rel_key_grad_store,
    ext_ref, wall_ref, back_ref,
):
    block = block_ref[0]
    size, model_width = query_store.shape[0], query_all.shape[1]
    scale = 1.0 / math.sqrt(3.0 * (model_width // HEADS))
    flip = reversal(size)
    chances = chances_load.buffer
    rel_key, query_all, sent, stats, value_all, key_all = ready(rel_key, query_all, sent, stats, value_all, key_all)
    extend_table(ext_ref, rel_key)
    back_ref[...] = nn(flip, query_all[size : 2 * size, :]).astype(BF)
    stat_lane = lanes((size, 128))

    def pair_step(pair, carry):
        columns = pair_columns(pair)
        delta = jnp.concatenate(
            [
                jnp.sum(jnp.where(stat_lane == head, stats[...], 0.0), axis=1, keepdims=True)
                for head in (2 * pair, 2 * pair + 1)
            ],
            axis=0,
        )
        grad_chances = nt(stacked(sent[:size, columns]), value_all[:, columns])
        grad_scores = (chances[pair].astype(F32) * (grad_chances - delta)).astype(BF)
        row_grad, table = position_backward(
            block, grad_scores, flip, key_all[:, columns], ext_ref[:, columns], back_ref[:, columns], wall_ref, 3 * size
        )
        there = pair_columns(pair - first)
        query_store.ref[:, there] = nn(flip, (row_grad * scale).astype(BF)).astype(BF)
        rel_key_grad_store.ref[there, :] = table_grad(table, scale)
        return carry

    lax.fori_loop(first, last, pair_step, 0)


def key_kernel(
    block_ref, length_ref, place_ref, rel_query, key_all, rel_key, query_all, value_all,
    sent_own, sent_core, sent_far, sent_diagonal,
    own, relative, grad_query_low, grad_rel_key_low, grad_query_high, grad_rel_key_high, query_weight, key_weight,
    value_weight, grad_first, tokens_store, late_send_low, late_send_high, late_keep,
    grads_out, key_rows_ref, value_rows_ref, rel_grad_ref,
    sent_ref, s_ref, grad_ref, ext_ref, wall_ref, back_ref, stat_ref,
):
    block = block_ref[0]
    length = length_ref[0]
    size, model_width = key_rows_ref.shape
    scale = 1.0 / math.sqrt(3.0 * (model_width // HEADS))
    factor = LOG2E * scale
    flip = reversal(size)
    rel_query, key_all, rel_key, query_all, value_all = ready(rel_query, key_all, rel_key, query_all, value_all)
    extend_table(ext_ref, rel_query)
    back_ref[...] = nn(flip, key_all[size : 2 * size, :]).astype(BF)
    for at, rows in placed(block, size, *ready(sent_own, sent_core, sent_far, sent_diagonal)):
        sent_ref[pl.ds(at, size), :] = rows[:size, :]
        parts = rows[size:, :size].astype(F32)
        stat_ref[0:8, pl.ds(at, size)] = parts[0:8, :] + parts[8:16, :]
        stat_ref[8:16, pl.ds(at, size)] = parts[16:24, :] + parts[24:32, :]
    position = block * size + lax.broadcasted_iota(jnp.int32, (size, 1), 0)
    mask_column = jnp.where(position < length, 0.0, -1e30)

    def pair_step(pair, carry):
        columns = pair_columns(pair)
        key_pair = stacked(key_all[size : 2 * size, columns])
        own_terms(block, s_ref, key_pair, rel_query[:, columns], 0)
        other_terms(
            block,
            s_ref,
            lambda slot: query_all[slot * size : (slot + 1) * size, columns],
            stacked(rel_key[:, columns]),
            1,
            range(4),
        )
        content = nt(key_pair, query_all[:, columns])
        for side in range(2):
            rows = slice(side * size, (side + 1) * size)
            less = mask_column - stat_ref[pl.ds(8 + 2 * pair + side, 1), :]
            s_ref[rows, :] = jnp.exp2((s_ref[rows, :] + content[rows]) * factor + less)
        value_grad = nn(abreast(s_ref[...].astype(BF)), stacked(sent_ref[:, columns]))
        grad_chances = nt(stacked(value_all[size : 2 * size, columns]), sent_ref[:, columns])
        for side in range(2):
            rows = slice(side * size, (side + 1) * size)
            delta = stat_ref[pl.ds(2 * pair + side, 1), :]
            grad_ref[rows, :] = (s_ref[rows, :] * (grad_chances[rows] - delta)).astype(BF)
        row_grad, table = position_backward(
            block, grad_ref[...], flip, query_all[:, columns], ext_ref[:, columns], back_ref[:, columns], wall_ref,
            3 * size + 1,
        )
        key_rows_ref[:, columns] = (row_grad * scale).astype(BF)
        value_rows_ref[:, columns] = value_grad.astype(BF)
        rel_grad_ref[columns, :] = table_grad(table, scale)
        return carry

    lax.fori_loop(0, HEADS // 2, pair_step, 0)
    own, relative, *grads = ready(
        own, relative, grad_query_low, grad_rel_key_low, grad_query_high, grad_rel_key_high
    )
    grad_query = jnp.concatenate([grads[0][...], grads[2][...]], axis=1)
    grad_rel_key = jnp.concatenate([grads[1][...], grads[3][...]], axis=0)
    rel = relative.shape[0]
    grad_key = nn(flip, key_rows_ref[...]).astype(BF)
    grad_value = value_rows_ref[...]
    rel_query_grad = rel_grad_ref[...]
    rel_key_grad = grad_rel_key
    query_low = rel_query_grad.astype(BF)
    key_low = nn(rel_key_grad.astype(BF), reversal(rel)).astype(BF)
    tokens = own[...]
    table = relative[...]
    grads_out[0:model_width, :] = (tn(tokens, grad_query) + tt(table, query_low)).astype(BF)
    grads_out[model_width : 2 * model_width, :] = (tn(tokens, grad_key) + tt(table, key_low)).astype(BF)
    grads_out[2 * model_width : 3 * model_width, :] = tn(tokens, grad_value).astype(BF)
    late_sends = (late_send_low, late_send_high)
    push_half(0, block % 2, place_ref[0], grads_out, late_sends, late_keep)
    table_at = 3 * model_width
    query_weight, key_weight, value_weight, grad_first = ready(query_weight, key_weight, value_weight, grad_first)
    grads_out[table_at : table_at + rel, :] = (
        tt(query_low, query_weight[...]) + tt(key_low, key_weight[...])
    ).astype(BF)
    small_at = table_at + rel
    grads_out[small_at + 16 :, :] = jnp.zeros((grads_out.shape[0] - small_at - 16, model_width), BF)
    ones = jnp.ones((8, rel), BF)

    def lane_sums(values):
        high = values.astype(BF)
        low = (values - high.astype(F32)).astype(BF)
        return (nt(ones, high) + nt(ones, low))[0:1, :]

    small = [
        column_sum(grad_query) + lane_sums(rel_query_grad),
        column_sum(grad_key) + lane_sums(rel_key_grad),
        column_sum(grad_value),
        jnp.zeros((13, model_width), F32),
    ]
    grads_out[small_at : small_at + 16, :] = jnp.concatenate(small, axis=0).astype(BF)
    push_half(1, block % 2, place_ref[0], grads_out, late_sends, late_keep)
    tokens_store.ref[...] = (
        nt(grad_query, query_weight[...])
        + nt(grad_key, key_weight[...])
        + nt(grad_value, value_weight[...])
        + grad_first[...]
    )


class Load:
    def __init__(self, source, buffer, sem):
        self.copy, self.buffer, self.waiting = pltpu.make_async_copy(source, buffer, sem), buffer, True

    def begin(self):
        self.copy.start()

    def ready(self):
        if self.waiting:
            self.copy.wait()
        self.waiting = False
        return self.buffer


def ready(*loads):
    return [load.ready() for load in loads]


class Store:
    def __init__(self, target, buffer, sem):
        self.copy, self.ref, self.shape, self.waiting = pltpu.make_async_copy(buffer, target, sem), buffer, buffer.shape, False

    def push(self):
        self.copy.start()
        self.waiting = True

    def finish(self):
        if not self.waiting:
            self.push()
        self.copy.wait()


class Here:
    def __init__(self, ref):
        self.ref = self.buffer = ref
        self.shape = ref.shape

    def ready(self):
        return self.ref

    def push(self):
        pass

    def finish(self):
        pass


def terms_after(first, terms):
    arrays = in_order(first, [array for array, _, _ in terms])
    return [(array, start, blocks) for array, (_, start, blocks) in zip(arrays, terms)]


class Raw:
    def __init__(self, target, sems):
        self.target, self.sems = target, sems
        self.shape = target.shape

    def push_from(self, source, k, part):
        pltpu.make_async_copy(source, self.target.at[pl.ds(k * part, part)], self.sems.at[k]).start()
        self.part = part

    def finish(self):
        for k in range(self.shape[0] // self.part):
            there = self.target.at[pl.ds(k * self.part, self.part)]
            pltpu.make_async_copy(there, there, self.sems.at[k]).wait()


def push_half(which, core, place, rows_ref, sends, keep):
    half = keep.shape[0]
    part = half // 4

    def source(k):
        return rows_ref.at[pl.ds(pl.multiple_of(which * half + (place ^ k) * part, 16), part)]

    @pl.when(core == which)
    def _():
        for k in range(4):
            keep.push_from(source(k), k, part)

    @pl.when(core != which)
    def _():
        for k in range(4):
            sends[k // 2].push_from(source(k), k % 2, part)


class Kept:
    def __init__(self, *what):
        self.what = what


class Bare:
    def __init__(self, *what):
        self.what = what


class Fetch:
    def __init__(self, what):
        self.what = what


def call(kernel, outs, scratch, *operands, scalars, micros, vmem, later=False):
    fetched = [k for k, operand in enumerate(operands) if isinstance(operand, Fetch)]
    bare_in = [k for k, operand in enumerate(operands) if isinstance(operand, Bare)]
    operands = [
        operand.what if isinstance(operand, Fetch) else operand.what[0] if isinstance(operand, Bare) else operand
        for operand in operands
    ]
    bare_out = [k for k, out in enumerate(outs) if isinstance(out, Bare)]
    outs = [out.what if isinstance(out, Bare) else out for out in outs]
    outs = list(outs) + [Kept(operands[k].shape, operands[k].dtype) for k in fetched]
    kept_in = [isinstance(operand, Kept) for operand in operands]
    kept_out = [isinstance(out, Kept) for out in outs]
    operands = [
        operand if k < scalars
        else pltpu.with_memory_space_constraint(operand.what[0], pltpu.VMEM) if kept
        else pltpu.with_memory_space_constraint(operand, pltpu.HBM)
        for k, (operand, kept) in enumerate(zip(operands, kept_in))
    ]
    outs = [out.what if kept else out for out, kept in zip(outs, kept_out)]
    raw = [len(out) > 2 for out in outs]
    loads = [k for k in range(scalars, len(operands)) if not kept_in[k] and k not in bare_in]
    stores = [k for k in range(len(outs)) if not kept_out[k] and k not in bare_out]
    buffered = [k for k in stores if not raw[k]]
    own_loads = [k for k in loads if k not in fetched]

    def body(*refs):
        n, m = len(operands), len(outs)
        ins, results, rest = list(refs[:n]), list(refs[n : n + m]), list(refs[n + m :])
        in_sems, out_sems = rest.pop(), rest.pop()
        buffers = [rest.pop() for _ in range(len(own_loads) + len(buffered))][::-1]
        targets = dict(zip(own_loads, buffers)) | dict(zip(fetched, results[m - len(fetched) :]))
        results = results[: m - len(fetched)]
        for k in range(scalars, n):
            if kept_in[k]:
                ins[k] = Here(ins[k])
        for place, k in enumerate(loads):
            ins[k] = Load(ins[k], targets[k], in_sems.at[place])
            if not later:
                ins[k].begin()
        buffers = buffers[len(own_loads) :]
        for k in range(len(results)):
            if kept_out[k]:
                results[k] = Here(results[k])
        for place, k in enumerate(stores):
            if raw[k]:
                results[k] = Raw(results[k], out_sems.at[place])
            else:
                results[k] = Store(results[k], buffers.pop(0), out_sems.at[place, 0])
        kernel(*ins, *results, *rest)
        for k in fetched:
            ins[k].ready()
        for k in stores:
            results[k].finish()

    spaces = [
        pltpu.SMEM if k < scalars else pltpu.VMEM if kept_in[k] else pltpu.HBM for k in range(len(operands))
    ]
    buffers = [(operands[k].shape, operands[k].dtype) for k in own_loads] + [outs[k][:2] for k in buffered]
    return pl.pallas_call(
        body,
        out_shape=[
            pltpu.VMEM(out[0], out[1]) if kept else pltpu.HBM(out[0], out[1])
            for out, kept in zip(outs, kept_out)
        ],
        in_specs=[pl.BlockSpec(memory_space=space) for space in spaces],
        out_specs=[pl.BlockSpec(memory_space=pltpu.VMEM if kept else pltpu.HBM) for kept in kept_out],
        scratch_shapes=[
            pltpu.SemaphoreType.DMA(space[0]) if space[1] is None else pltpu.VMEM(*space)
            for space in list(scratch) + buffers
        ]
        + [pltpu.SemaphoreType.DMA((max(len(stores), 1), 4)), pltpu.SemaphoreType.DMA((max(len(loads), 1),))],
        compiler_params=pltpu.CompilerParams(vmem_limit_bytes=vmem * MIB),
        cost_estimate=pl.CostEstimate(flops=micros * 10**9, bytes_accessed=micros * 10**6, transcendentals=0),
    )(*operands)


class Group:
    def __init__(self, blk_count, dp_count, bits):
        self.blk_count, self.dp_count, self.bits = blk_count, dp_count, bits
        self.size = 2 ** len(bits)
        place = {"blk": lax.axis_index("blk"), "dp": lax.axis_index("dp")}
        self.digits = [(place[axis] >> (bit.bit_length() - 1)) & 1 for axis, bit in bits]
        self.me = sum(digit << k for k, digit in enumerate(self.digits))

    def pairs(self, mask):
        change = {"blk": 0, "dp": 0}
        for k, (axis, bit) in enumerate(self.bits):
            if mask >> k & 1:
                change[axis] |= bit
        return [
            (blk * self.dp_count + dp, (blk ^ change["blk"]) * self.dp_count + (dp ^ change["dp"]))
            for blk in range(self.blk_count)
            for dp in range(self.dp_count)
        ]

    def send(self, values, mask):
        return lax.ppermute(values, ("blk", "dp"), self.pairs(mask))

    def scatter(self, terms):
        def part(index):
            return [
                (array, first + index * (blocks // self.size), blocks // self.size) for array, first, blocks in terms
            ]

        outs = [total(part(self.me ^ mask)) for mask in range(1, self.size)]
        arrived = [self.send(out, mask + 1) for mask, out in enumerate(outs)]
        return outs, part(self.me) + [whole(array) for array in arrived]

    def pieces(self, held):
        return [held] + [self.send(held, mask) for mask in range(1, self.size)]

    def gather(self, held):
        return self.arrange(self.pieces(held))

    def arrange(self, parts):
        for k, digit in enumerate(self.digits):
            parts = [
                jnp.where(digit == 0, parts[q], parts[q ^ (1 << k)]) for q in range(self.size)
            ]
        return jnp.concatenate(parts, axis=0)


def groups_of(blk_count, dp_count):
    bits, bit = [], 2
    while bit < dp_count:
        bits.append(("dp", bit))
        bit *= 2
    groups = [[("blk", 1)], [("blk", 2), ("dp", 1)]]
    groups += [bits[k : k + 2] for k in range(0, len(bits), 2)]
    return [Group(blk_count, dp_count, group) for group in groups]


def whole(array):
    return array, 0, array.shape[0]


def total(terms):
    spans = [
        array[first : first + blocks] if isinstance(first, int) else lax.dynamic_slice_in_dim(array, first, blocks, 0)
        for array, first, blocks in terms
    ]
    return sum(span.astype(F32) for span in spans).astype(BF)


def in_order(first, then):
    return lax.optimization_barrier((first, then))[1]


def halves_to_scratch(core_ref, place_ref, held, arrived, both_ref):
    held, arrived = ready(held, arrived)
    half = held.shape[0]
    part = half // 4
    for k in range(4):
        at = (place_ref[0] ^ k) * part
        span = slice(k * part, (k + 1) * part)
        both_ref[pl.ds(pl.multiple_of(core_ref[0] * half + at, 16), part), :] = held[span, :]
        both_ref[pl.ds(pl.multiple_of((1 - core_ref[0]) * half + at, 16), part), :] = arrived[span, :]


def early_kernel(
    core_ref, place_ref, held, arrived,
    outer_weight, inner_weight, output_weight, outer_bias, second_gain, second_bias, inner_bias, first_gain, first_bias,
    output_bias,
    both_ref,
):
    halves_to_scratch(core_ref, place_ref, held, arrived, both_ref)
    inner_width, width = outer_weight.shape
    chunks = inner_width // width
    for chunk in range(chunks):
        span = slice(chunk * width, (chunk + 1) * width)
        outer_weight.ref[span, :] = both_ref[span, :].T.astype(F32)
    outer_weight.push()
    for chunk in range(chunks):
        at = inner_width + chunk * width
        inner_weight.ref[:, chunk * width : (chunk + 1) * width] = both_ref[at : at + width, :].astype(F32)
    at = 2 * inner_width
    output_weight.ref[...] = both_ref[at : at + width, :].astype(F32)
    output_weight.push()
    small = both_ref[at + width : at + width + 16, :].astype(F32)

    def vector(out, row):
        out.ref[...] = small[row, :]
        out.push()

    vector(outer_bias, 0)
    vector(second_gain, 1)
    vector(second_bias, 2)
    inner_bias.ref[...] = jnp.concatenate([small[3 + k : 4 + k, :] for k in range(chunks)], axis=1)[0, :]
    inner_bias.push()
    vector(first_gain, 3 + chunks)
    vector(first_bias, 4 + chunks)
    vector(output_bias, 5 + chunks)


def late_kernel(mine, shapes, core_ref, place_ref, held, *rest):
    outs, (rows_ref, wide_ref, vector_ref, sems) = rest[-11:-4], rest[-4:]
    query_weight, query_bias, key_weight, key_bias, value_weight, value_bias, relative = outs
    half, width = rows_ref.shape
    part = half // 4
    rel = relative.shape[0]
    for k in range(4):
        at = pl.multiple_of((place_ref[0] ^ k) * part, 16)
        rows_ref[pl.ds(at, part), :] = held[k * part : (k + 1) * part, :]
    split = half - 2 * width
    which = core_ref[0] if mine else 1 - core_ref[0]

    def copy(spans):
        copies = []
        for k, (at, rows, out, start) in enumerate(spans):
            wide_ref[at : at + rows, :] = rows_ref[at : at + rows, :].astype(F32)
            one = pltpu.make_async_copy(wide_ref.at[pl.ds(at, rows)], out.at[pl.ds(start, rows)], sems.at[k])
            one.start()
            copies.append(one)
        return copies

    @pl.when(which == 0)
    def _():
        spans = ((0, width, query_weight, 0), (width, width, key_weight, 0), (2 * width, split, value_weight, 0))
        for one in copy(spans):
            one.wait()

    @pl.when(which == 1)
    def _():
        rest_rows = width - split
        copies = copy(((rest_rows, rel, relative, 0), (0, rest_rows, value_weight, split)))
        small = rows_ref[rest_rows + rel : rest_rows + rel + 16, :].astype(F32)
        for k, out in enumerate((query_bias, key_bias, value_bias)):
            vector_ref[k, :] = small[k, :]
            one = pltpu.make_async_copy(vector_ref.at[k], out, sems.at[2 + k])
            one.start()
            copies.append(one)
        for one in copies:
            one.wait()


def late_call(mine, shapes, core, place, held, *before):
    hbm, smem = pl.BlockSpec(memory_space=pltpu.HBM), pl.BlockSpec(memory_space=pltpu.SMEM)
    width = held.shape[1]
    return pl.pallas_call(
        functools.partial(late_kernel, mine, shapes),
        out_shape=[pltpu.HBM(shape, F32) for shape in shapes],
        in_specs=[smem, smem, pl.BlockSpec(memory_space=pltpu.VMEM)] + [hbm] * len(before),
        out_specs=[hbm] * len(shapes),
        scratch_shapes=[
            pltpu.VMEM(held.shape, BF),
            pltpu.VMEM(held.shape, F32),
            pltpu.VMEM((8, width), F32),
            pltpu.SemaphoreType.DMA((5,)),
        ],
        input_output_aliases={3 + k: k for k in range(len(before))},
        compiler_params=pltpu.CompilerParams(vmem_limit_bytes=10 * MIB),
        cost_estimate=pl.CostEstimate(flops=2 * 10**9, bytes_accessed=2 * 10**6, transcendentals=0),
    )(core, place, pltpu.with_memory_space_constraint(held, pltpu.VMEM), *before)


def on_device(
    blk_count, dp_count,
    tokens, lengths, query_weight, query_bias, key_weight, key_bias, value_weight, value_bias,
    output_weight, output_bias, first_gain, first_bias, inner_weight, inner_bias, outer_weight, outer_bias,
    second_gain, second_bias, relative_table, cotangent,
):
    seq_count, size, width = tokens.shape
    rel = relative_table.shape[0]
    inner_width = inner_weight.shape[1]
    own = tokens[0]
    block = lax.axis_index("blk").astype(jnp.int32).reshape(1)
    groups = groups_of(blk_count, dp_count)
    chips = groups[1:]
    place = chips[0].me.astype(jnp.int32).reshape(1)
    shards = blk_count * dp_count

    def along(values, bit):
        return lax.ppermute(values, "blk", [(i, i ^ bit) for i in range(blk_count)])

    def blocks(rows, share):
        return rows.reshape(shards // share, -1, width)

    def flat(values):
        return values.reshape(-1, width)

    def first_terms(keep, low, high):
        arrived = [groups[0].send(blocks(piece, 4), 1) for piece in (low, high)]
        keep, part = blocks(keep, 2), shards // 8
        return [[(keep, k * part, part), (arrived[k // 2], k % 2 * part, part)] for k in range(4)]

    def first_scatter(parts):
        outs = [total(terms) for terms in parts[1:]]
        return outs, parts[0] + [whole(chips[0].send(out, k + 1)) for k, out in enumerate(outs)]

    core = along(own, 1)
    far = along(own, 2)
    diagonal = along(own, 3)
    full = blk_count * size
    slabs = (HEADS // 2, 2 * size, 3 * size + 128)
    (
        rel_query, rel_key, terms, relative_kept, query_weight, key_weight, query_bias, key_bias, own, value_weight, value_bias,
    ) = call(
        first_kernel,
        [Kept((rel, width), BF), Kept((rel, width), BF), Bare(slabs, F32)],
        [((size, width), BF), ((size, width), BF), (slabs, F32), ((HEADS // 2,), None)],
        block,
        *map(Fetch, (relative_table, query_weight, key_weight, query_bias, key_bias, own, value_weight, value_bias)),
        scalars=1, micros=9, vmem=14,
    )
    (
        layer_out, grad_first, chances, sent, stats, query_all, key_all, value_all,
        early_send_low, early_send_high, early_keep,
    ) = call(
        forward_kernel,
        [
            ((size, width), F32),
            Kept((size, width), F32),
            Kept((HEADS // 2, 2 * size, full), BF),
            Kept((size + 32, width), BF),
            Kept((size, 128), F32),
            Kept((full, width), BF),
            Kept((full, width), BF),
            Kept((full, width), BF),
            ((EARLY_ROWS // 4, width), BF, "raw"),
            ((EARLY_ROWS // 4, width), BF, "raw"),
            ((EARLY_ROWS // 2, width), BF, "raw"),
        ],
        [
            ((full, width), BF),
            ((2 * size, full), F32),
            ((size, width), F32),
            ((size, 128), F32),
            ((size, inner_width), BF),
            ((size, inner_width), F32),
            ((EARLY_ROWS, width), BF),
            (slabs, F32),
            ((size, width), F32),
            ((16, width), F32),
            ((1, inner_width), F32),
            ((HEADS // 2,), None),
        ],
        block, lengths, place,
        *map(Kept, (own, core, far, diagonal, rel_query, rel_key)),
        Bare(terms),
        *map(Kept, (query_weight, key_weight, query_bias, key_bias, value_weight, value_bias)),
        output_weight, output_bias, first_gain, first_bias, inner_weight, inner_bias, outer_weight, outer_bias,
        second_gain, second_bias, cotangent[0],
        scalars=3, micros=20, vmem=26, later=True,
    )
    early_parts = first_terms(early_keep, early_send_low, early_send_high)
    sent_far = along(sent, 2)
    sent_core = along(sent, 1)
    position_scratch = [((2 * rel, width), BF), ((2 * size, 2 * rel), BF), ((size, width), BF)]
    query_arrays = tuple(map(Kept, (rel_key, query_all, sent, stats, value_all, key_all, chances)))

    def query_call(first, last, block_then):
        columns = (last - first) * 128
        return call(
            functools.partial(query_kernel, first, last),
            [Kept((size, columns), BF), Kept((columns, rel), F32)],
            position_scratch,
            block_then, *query_arrays,
            scalars=1, micros=2 * (last - first) + 1, vmem=10,
        )

    query_grads = query_call(0, QUERY_SPLIT, block)
    sending, early_terms = first_scatter([terms_after(query_grads[0], terms) for terms in early_parts])
    query_grads += query_call(QUERY_SPLIT, HEADS // 2, in_order(sending, block))
    sent_diagonal = along(in_order(query_grads[2], sent_far), 1)
    key_scratch = (
        [((full, width), BF), ((2 * size, full), F32), ((2 * size, full), BF)] + position_scratch + [((16, full), F32)]
    )
    key_arrays = tuple(
        map(Kept, (rel_query, key_all, rel_key, query_all, value_all, sent, sent_core, sent_far, sent_diagonal))
    )
    grad_tokens, late_send_low, late_send_high, late_keep = call(
        key_kernel,
        [((size, width), F32)] + [((LATE_ROWS // 4, width), BF, "raw")] * 2 + [((LATE_ROWS // 2, width), BF, "raw")],
        [((LATE_ROWS, width), BF), ((size, width), BF), ((size, width), BF), ((width, rel), F32)] + key_scratch,
        block, lengths, place, *key_arrays,
        *map(Kept, (own, relative_kept, *query_grads, query_weight, key_weight, value_weight, grad_first)),
        scalars=3, micros=17, vmem=18,
    )
    late_parts = first_terms(late_keep, late_send_low, late_send_high)
    early_terms = terms_after(late_send_low, early_terms)
    for group in chips[1:]:
        sending, early_terms = group.scatter(early_terms)
        late_parts = [terms_after(sending, terms) for terms in late_parts]
    sending_xy, late_terms = first_scatter(late_parts)
    arrived = [array for array, _, _ in late_terms[1 - chips[0].size :]]
    early_held = total(early_terms)
    for group in reversed(chips[2:]):
        early_held = group.gather(early_held)
    early_parts = chips[1].pieces(early_held)
    for group in chips[1:]:
        sending_z, late_terms = group.scatter(late_terms)
    z_arrived = [array for array, _, _ in late_terms[1 - chips[-1].size :]]
    early_parts = in_order(z_arrived[0], early_parts)
    early_pieces = chips[0].pieces(chips[1].arrange(early_parts))
    late_held = total(late_terms)
    for group in reversed(chips[2:]):
        late_held = group.gather(late_held)
    late_parts = chips[1].pieces(late_held)
    late_parts, early_pieces[1] = lax.optimization_barrier((late_parts, early_pieces[1]))
    late_held = chips[1].arrange(late_parts)
    early_held = jnp.concatenate(early_pieces, axis=0)
    late_pieces = chips[0].pieces(late_held)
    my_core = groups[0].me.astype(jnp.int32).reshape(1)
    square, vector = ((width, width), F32), ((width,), F32)
    (
        g_outer_weight, g_inner_weight, g_output_weight, g_outer_bias, g_second_gain, g_second_bias, g_inner_bias,
        g_first_gain, g_first_bias, g_output_bias,
    ) = call(
        early_kernel,
        [((inner_width, width), F32), ((width, inner_width), F32), square, vector, vector, vector,
         ((inner_width,), F32), vector, vector, vector],
        [((EARLY_ROWS, width), BF)],
        my_core, place, *(Kept(flat(piece)) for piece in groups[0].pieces(early_held)),
        scalars=2, micros=4, vmem=14,
    )
    late_held = jnp.concatenate(in_order(g_output_bias, late_pieces), axis=0)
    own_half, other_half = (flat(piece) for piece in groups[0].pieces(late_held))
    shapes = [square[0], vector[0]] * 3 + [(rel, width)]
    late_grads = late_call(True, shapes, my_core, place, own_half)
    (
        g_query_weight, g_query_bias, g_key_weight, g_key_bias, g_value_weight, g_value_bias, g_relative,
    ) = late_call(False, shapes, my_core, place, other_half, *late_grads)
    return (
        layer_out[None], grad_tokens[None], g_query_weight, g_query_bias, g_key_weight, g_key_bias,
        g_value_weight, g_value_bias, g_output_weight, g_output_bias, g_first_gain, g_first_bias,
        g_inner_weight, g_inner_bias, g_outer_weight, g_outer_bias, g_second_gain, g_second_bias, g_relative,
    )


def solution(mesh):
    blk_count, dp_count = mesh.shape["blk"], mesh.shape["dp"]
    rows = P("dp", "blk", None)
    in_specs = (rows, P("dp")) + (P(),) * 17 + (rows,)
    out_specs = (rows, rows) + (P(),) * 17

    def whole(*arrays):
        return on_device(blk_count, dp_count, *arrays)

    return jax.shard_map(whole, mesh=mesh, in_specs=in_specs, out_specs=out_specs, check_vma=False)
```

```python
import functools
import math

import jax
import jax.numpy as jnp
from jax import lax
from jax.experimental import pallas as pl
from jax.experimental.pallas import tpu as pltpu
from jax.sharding import PartitionSpec as P

HEADS = 6
BF = jnp.bfloat16
F32 = jnp.float32
LOG2E = math.log2(math.e)
EPS = 1e-07
MIB = 1024 * 1024
QUERY_SPLIT = 1
EARLY_ROWS = 3584
LATE_ROWS = 1792


def nn(left, right):
    return lax.dot_general(left, right, (((1,), (0,)), ((), ())), preferred_element_type=F32)


def nt(left, right):
    return lax.dot_general(left, right, (((1,), (1,)), ((), ())), preferred_element_type=F32)


def tn(left, right):
    return lax.dot_general(left, right, (((0,), (0,)), ((), ())), preferred_element_type=F32)


def tt(left, right):
    return lax.dot_general(left, right, (((0,), (1,)), ((), ())), preferred_element_type=F32)


def lanes(shape):
    return lax.broadcasted_iota(jnp.int32, shape, len(shape) - 1)


def of_head(values, head):
    inside = (lanes(values.shape) // 64) == head
    return jnp.where(inside, values, jnp.zeros_like(values))


def stacked(values):
    return jnp.concatenate([of_head(values, 0), of_head(values, 1)], axis=0)


def abreast(values):
    rows = values.shape[0] // 2
    return jnp.concatenate([values[:rows], values[rows:]], axis=1)


def pair_columns(pair):
    if isinstance(pair, int):
        return slice(pair * 128, (pair + 1) * 128)
    return pl.ds(pl.multiple_of(pair * 128, 128), 128)


def wide(column, width):
    return jnp.broadcast_to(column, (column.shape[0], width))


def reversal(size):
    rows = lax.broadcasted_iota(jnp.int32, (size, size), 0)
    cols = lax.broadcasted_iota(jnp.int32, (size, size), 1)
    return jnp.where(rows + cols == size - 1, 1.0, 0.0).astype(BF)


def placed(block, size, own, core, far, diagonal):
    even = block % 2 == 0
    core_at = pl.multiple_of(jnp.where(even, 2 * size, 0), size)
    diagonal_at = pl.multiple_of(jnp.where(even, 0, 2 * size), size)
    return (size, own), (3 * size, far), (core_at, core), (diagonal_at, diagonal)


def rolled_window(source, shift):
    half = source.shape[0] // 2
    upper = pltpu.roll(source[:half, half:], shift, 1, stride=1, stride_axis=0)[:, half:]
    lower = pltpu.roll(source[half:, : 3 * half], shift, 1, stride=1, stride_axis=0)[:, half:]
    return jnp.concatenate([upper, lower], axis=0)


def own_terms(block, s_ref, own_rows, own_table, shift):
    size = own_rows.shape[0] // 2
    rel = own_table.shape[0]
    scores = nt(own_rows, own_table)
    last, first = scores[:, rel - 1 : rel], scores[:, 0:1]
    source = jnp.concatenate([scores, wide(last, size), wide(first, size)], axis=1)
    for side in range(2):
        rows = slice(side * size, (side + 1) * size)
        s_ref[rows, : 3 * size] = pltpu.roll(source[rows], shift, 1, stride=1, stride_axis=0)[:, : 3 * size]
    s_ref[:, 3 * size :] = wide(jnp.where(block < 2, last, first), s_ref.shape[1] - 3 * size)


def other_terms(block, s_ref, others, tables, shift, slots):
    size = s_ref.shape[0] // 2
    rel = tables.shape[0] // 2

    def both(start, rows):
        return jnp.concatenate([tables[start : start + rows], tables[rel + start : rel + start + rows]], axis=0)

    def near(slot):
        if slot == 1:
            product = nt(others(slot), tables)
            parts = [product[:, :rel], product[:, rel:]]
        else:
            product = nt(others(slot), both(size if slot == 0 else 0, size))
            parts = [product[:, :size], product[:, size:]]
        if slot == 0:
            parts = [jnp.concatenate([part, wide(part[:, size - 1 : size], size)], axis=1) for part in parts]
        elif slot == 2:
            parts = [jnp.concatenate([wide(part[:, 0:1], size), part], axis=1) for part in parts]
        return [rolled_window(part, shift).T for part in parts]

    def constant(slot):
        rows = others(slot)
        top = nt(both(0, 16), rows)
        bottom = nt(both(rel - 16, 16), rows)
        return [
            s_ref[side * size : (side + 1) * size, 3 * size :]
            + jnp.where(block < 2, top[16 * side : 16 * side + 1], bottom[16 * side + 15 : 16 * side + 16])
            for side in range(2)
        ]

    for slot in slots:
        span = slice(slot * size, (slot + 1) * size)
        terms = near(slot) if slot < 3 else None
        fixed = constant(slot) if slot != 1 else None
        past = block == (0 if slot == 0 else 3)
        for side in range(2):
            rows = slice(side * size, (side + 1) * size)
            if slot == 1:
                s_ref[rows, span] += terms[side]
            elif slot == 3:
                s_ref[rows, span] = fixed[side]
            else:
                s_ref[rows, span] = jnp.where(past, fixed[side], s_ref[rows, span] + terms[side])


def extend_table(ext_ref, table_ref):
    rel = table_ref.shape[0]
    half = rel // 2
    width = table_ref.shape[1]
    ext_ref[0:rel, :] = table_ref[...]
    ext_ref[rel : rel + half, :] = jnp.broadcast_to(table_ref[rel - 1 : rel, :], (half, width))
    ext_ref[rel + half : 2 * rel, :] = jnp.broadcast_to(table_ref[0:1, :], (half, width))


def unskewed(block, wall_ref, grad_rows, shift):
    size = grad_rows.shape[0]
    before, own, after, far = (grad_rows[:, k * size : (k + 1) * size] for k in range(4))
    none = jnp.zeros_like(own)
    no_before, no_after = block == 0, block == 3
    near = jnp.concatenate(
        [jnp.where(no_before, none, before), own, jnp.where(no_after, none, after), none], axis=1
    )
    rolled = pltpu.roll(near, shift, 1, stride=1, stride_axis=0)
    far = far + jnp.where(no_before, before, jnp.where(no_after, after, none))
    wall_ref[:, : 2 * size] = rolled[:, : 2 * size]
    wall_ref[:, 2 * size : 3 * size] = rolled[:, 2 * size : 3 * size] + jnp.where(block < 2, far, none)
    wall_ref[:, 3 * size :] = rolled[:, 3 * size :] + jnp.where(block < 2, none, far)


def table_grad(sums, scale):
    rel = sums.shape[1] // 2
    half = rel // 2
    over = jnp.sum(sums[:, rel : rel + half], axis=1, keepdims=True)
    under = jnp.sum(sums[:, rel + half :], axis=1, keepdims=True)
    at = lanes((sums.shape[0], rel))
    folded = sums[:, :rel] + jnp.where(at == rel - 1, over, 0.0) + jnp.where(at == 0, under, 0.0)
    return folded * scale


def as_row(vector_ref):
    return vector_ref[...].astype(F32).reshape(1, -1)


def affine(values, weight_ref, bias_ref):
    return nn(values, weight_ref[...]) + as_row(bias_ref)


def norm_forward(values):
    center = values - jnp.mean(values, axis=-1, keepdims=True)
    spread = jnp.mean(center * center, axis=-1, keepdims=True)
    rate = lax.rsqrt(spread + EPS)
    return center * rate, rate


def norm_backward(grad_hat, hat, rate):
    mean_grad = jnp.mean(grad_hat, axis=-1, keepdims=True)
    mean_along = jnp.mean(grad_hat * hat, axis=-1, keepdims=True)
    return rate * (grad_hat - mean_grad - hat * mean_along)


def column_sum(values):
    return jnp.sum(values.astype(F32), axis=0, keepdims=True)


def slab_copy(source, target, sems, k):
    return pltpu.make_async_copy(source.at[k], target.at[k], sems.at[k])


def first_kernel(
    block_ref, relative, query_weight, key_weight, query_bias, key_bias, own, value_weight,
    value_bias, *rest,
):
    rel_query_store, rel_key_store, terms_out, query_ref, key_ref, terms_ref, sems = rest
    block = block_ref[0]
    relative, query_weight, key_weight, query_bias, key_bias = ready(
        relative, query_weight, key_weight, query_bias, key_bias
    )
    rel_query_out, rel_key_out = rel_query_store.ref, rel_key_store.ref
    rel_query_out[...] = affine(relative[...], query_weight, query_bias).astype(BF)
    rel_key_out[...] = affine(
        nn(reversal(relative.shape[0]), relative[...]).astype(BF), key_weight, key_bias
    ).astype(BF)
    (own,) = ready(own)
    size = own.shape[0]
    query_ref[...] = affine(own[...], query_weight, query_bias).astype(BF)
    key_ref[...] = affine(own[...], key_weight, key_bias).astype(BF)

    def pair_step(pair, carry):
        columns = pair_columns(pair)
        s_ref = terms_ref.at[pair]
        query_own = stacked(query_ref[:, columns])
        own_terms(block, s_ref, query_own, rel_key_out[:, columns], 1)
        other_terms(block, s_ref, lambda slot: key_ref[:, columns], stacked(rel_query_out[:, columns]), 0, (1,))
        s_ref[:, size : 2 * size] += nt(query_own, key_ref[:, columns])
        slab_copy(terms_ref, terms_out, sems, pair).start()
        return carry

    lax.fori_loop(0, HEADS // 2, pair_step, 0)
    for pair in range(HEADS // 2):
        slab_copy(terms_ref, terms_out, sems, pair).wait()


def forward_kernel(
    block_ref, length_ref, place_ref, own, core, far, diagonal, rel_query, rel_key, *rest
):
    (
        terms, query_weight, key_weight, query_bias, key_bias, value_weight, value_bias, output_weight,
        output_bias, first_gain, first_bias, inner_weight, inner_bias, outer_weight, outer_bias, second_gain,
        second_bias, cotangent,
        layer_store, first_store, chances_store, sent_store, stats_store, query_store, key_store, value_store,
        early_send_low, early_send_high, early_keep,
        x_all, s_ref, mixture_ref, log_ref, active_ref, slope_ref, grads_out, terms_ref, sums_ref, small_ref, bias_ref, sems,
    ) = rest
    block = block_ref[0]
    length = length_ref[0]
    size, model_width = layer_store.shape
    head_dim = model_width // HEADS
    factor = LOG2E / math.sqrt(3.0 * head_dim)
    query_out, key_out, value_out = query_store.ref, key_store.ref, value_store.ref
    chances_out, sent_out = chances_store.ref, sent_store.ref
    for pair in range(HEADS // 2):
        slab_copy(terms, terms_ref, sems, pair).start()
    for load in (
        output_weight, output_bias, first_gain, first_bias, inner_weight, inner_bias, outer_weight, outer_bias,
        second_gain, second_bias, cotangent,
    ):
        load.begin()
    own, core, far, diagonal, rel_query_out = ready(own, core, far, diagonal, rel_query)
    query_weight, key_weight, query_bias, key_bias = ready(query_weight, key_weight, query_bias, key_bias)
    value_weight, value_bias = ready(value_weight, value_bias)
    for at, rows in placed(block, size, own, core, far, diagonal):
        x_all[pl.ds(at, size), :] = rows[...]
    query_out[...] = affine(x_all[...], query_weight, query_bias).astype(BF)
    key_out[...] = affine(x_all[...], key_weight, key_bias).astype(BF)
    value_out[...] = affine(x_all[...], value_weight, value_bias).astype(BF)
    step = lanes((1, 4 * size))
    position = ((block + 3 + step // size) % 4) * size + step % size
    mask_row = jnp.where(position < length, 0.0, -1e30)
    stat_lane = lanes((size, 128))
    log_ref[...] = jnp.zeros_like(log_ref)

    def pair_step(pair, carry):
        columns = pair_columns(pair)
        query_own = stacked(query_out[size : 2 * size, columns])
        slab_copy(terms, terms_ref, sems, pair).wait()
        s_ref[:, : 3 * size] = terms_ref[pair, :, : 3 * size]
        s_ref[:, 3 * size :] = wide(terms_ref[pair, :, 3 * size : 3 * size + 1], size)
        other_terms(
            block,
            s_ref,
            lambda slot: key_out[slot * size : (slot + 1) * size, columns],
            stacked(rel_query_out[:, columns]),
            0,
            (0, 2, 3),
        )
        before = s_ref[:, :size] + nt(query_own, key_out[:size, columns])
        s_ref[:, :size] = before * factor + mask_row[:, :size]
        s_ref[:, size : 2 * size] = s_ref[:, size : 2 * size] * factor + mask_row[:, size : 2 * size]
        after = s_ref[:, 2 * size :] + nt(query_own, key_out[2 * size :, columns])
        s_ref[:, 2 * size :] = after * factor + mask_row[:, 2 * size :]
        top = jnp.max(s_ref[...], axis=1, keepdims=True)
        raised = jnp.exp2(s_ref[...] - top)
        s_ref[...] = raised
        row_sum = jnp.sum(raised, axis=1, keepdims=True)
        chances = (s_ref[...] * (1.0 / row_sum)).astype(BF)
        chances_out[pair] = chances
        log_total = top + jnp.log2(row_sum)
        for side in range(2):
            log_ref[...] = jnp.where(
                stat_lane % 8 == 2 * pair + side, log_total[side * size : (side + 1) * size], log_ref[...]
            )
        total = nn(abreast(chances), stacked(value_out[:, columns]))
        mixture_ref[:, columns] = total
        return carry

    lax.fori_loop(0, HEADS // 2, pair_step, 0)

    (
        output_weight, output_bias, first_gain, first_bias, inner_weight, inner_bias, outer_weight, outer_bias,
        second_gain, second_bias, cotangent,
    ) = ready(
        output_weight, output_bias, first_gain, first_bias, inner_weight, inner_bias, outer_weight, outer_bias,
        second_gain, second_bias, cotangent,
    )
    inner_width = inner_weight.shape[1]
    chunks = inner_width // model_width
    mixture_low = mixture_ref[...].astype(BF)
    first_sum = own[...].astype(F32) + affine(mixture_low, output_weight, output_bias)
    first_hat, first_rate = norm_forward(first_sum)
    normed = (first_hat * as_row(first_gain) + as_row(first_bias)).astype(BF)
    root_half = math.sqrt(0.5)
    density = 1.0 / math.sqrt(2.0 * math.pi)

    sums_ref[...] = normed.astype(F32) + as_row(outer_bias)
    bias_ref[...] = as_row(inner_bias)

    def chunk_span(chunk):
        return pl.ds(chunk * model_width, model_width)

    def ahead(chunk, carry):
        span = chunk_span(chunk)
        inner_pre = nn(normed, inner_weight[:, span]) + bias_ref[:, span]
        below = 0.5 + 0.5 * lax.erf(inner_pre * root_half)
        slope_ref[:, span] = below + inner_pre * density * jnp.exp(-0.5 * inner_pre * inner_pre)
        active = (inner_pre * below).astype(BF)
        active_ref[:, span] = active
        sums_ref[...] += nn(active, outer_weight[span, :])
        return carry

    for chunk in range(chunks):
        ahead(chunk, 0)
    second_sum = sums_ref[...]
    second_hat, second_rate = norm_forward(second_sum)
    gain = as_row(second_gain)
    layer_store.ref[...] = second_hat * gain + as_row(second_bias)
    layer_store.push()
    cot = cotangent[...].astype(F32)
    grad_second = norm_backward(cot * gain, second_hat, second_rate)
    grad_outer = grad_second.astype(BF)
    outer_at, inner_at, output_at, small_at = 0, inner_width, 2 * inner_width, 2 * inner_width + model_width
    grads_out[small_at + 16 :, :] = jnp.zeros((grads_out.shape[0] - small_at - 16, model_width), BF)
    small_ref[...] = jnp.zeros_like(small_ref)
    for k, values in enumerate((column_sum(grad_outer), column_sum(cot * second_hat), column_sum(cot))):
        small_ref[k : k + 1, :] = values
    sums_ref[...] = grad_second
    outer_turned, normed_turned = grad_outer.T, normed.T

    def back(chunk, carry):
        span = chunk_span(chunk)
        at = outer_at + chunk * model_width
        grads_out[pl.ds(at, model_width), :] = nn(outer_turned, active_ref[:, span]).astype(BF)
        grad_inner = (nt(grad_outer, outer_weight[span, :]) * slope_ref[:, span]).astype(BF)
        small_ref[pl.ds(3 + chunk, 1), :] = column_sum(grad_inner)
        at = inner_at + chunk * model_width
        grads_out[pl.ds(at, model_width), :] = nn(normed_turned, grad_inner).astype(BF)
        sums_ref[...] += nt(grad_inner, inner_weight[:, span])
        return carry

    for chunk in range(chunks):
        back(chunk, 0)
    early_sends = (early_send_low, early_send_high)
    push_half(0, block % 2, place_ref[0], grads_out, early_sends, early_keep)
    grad_normed = sums_ref[...].astype(BF).astype(F32)
    grad_first = norm_backward(grad_normed * as_row(first_gain), first_hat, first_rate)
    first_store.ref[...] = grad_first
    first_store.push()
    grad_branch = grad_first.astype(BF)
    grads_out[output_at : output_at + model_width, :] = tn(mixture_low, grad_branch).astype(BF)
    for k, values in enumerate(
        (column_sum(grad_normed * first_hat), column_sum(grad_normed), column_sum(grad_branch))
    ):
        small_ref[3 + chunks + k : 4 + chunks + k, :] = values
    grads_out[small_at : small_at + 16, :] = small_ref[...].astype(BF)
    push_half(1, block % 2, place_ref[0], grads_out, early_sends, early_keep)
    grad_mixture = nt(grad_branch, output_weight[...]).astype(BF)
    sent_out[:size, :] = grad_mixture
    along = grad_mixture.astype(F32) * mixture_ref[...]
    stats = log_ref[...]
    for head in range(HEADS):
        columns = slice((head // 2) * 128, (head // 2 + 1) * 128)
        delta = jnp.sum(of_head(along[:, columns], head % 2), axis=1, keepdims=True)
        stats = jnp.where((stat_lane < 16) & (stat_lane % 8 == head), delta, stats)
    stats_store.ref[...] = stats
    upper = stats.astype(BF).astype(F32)
    parts = jnp.where((stat_lane // 8) % 2 == 0, upper, stats - upper).T[:32, :]
    sent_out[size:, :size] = parts.astype(BF)
    sent_out[size:, size:] = jnp.zeros((32, model_width - size), BF)
    sent_store.push()


def position_backward(block, grad_scores, flip, other_pair, ext_pair, own_rows_back, wall_ref, shift):
    size = flip.shape[0]
    full = grad_scores.shape[1]
    grad_back = nn(flip, abreast(grad_scores)).astype(BF)
    for side in range(2):
        unskewed(block, wall_ref.at[pl.ds(side * size, size)], grad_back[:, side * full : (side + 1) * full], shift)
    row_grad = nn(grad_back, stacked(other_pair)) + nn(abreast(wall_ref[...]), stacked(ext_pair))
    return row_grad, tn(stacked(own_rows_back), wall_ref[...])


def query_kernel(
    first, last, block_ref, rel_key, query_all, sent, stats, value_all, key_all, chances_load,
    query_store, rel_key_grad_store,
    ext_ref, wall_ref, back_ref,
):
    block = block_ref[0]
    size, model_width = query_store.shape[0], query_all.shape[1]
    scale = 1.0 / math.sqrt(3.0 * (model_width // HEADS))
    flip = reversal(size)
    chances = chances_load.buffer
    rel_key, query_all, sent, stats, value_all, key_all = ready(rel_key, query_all, sent, stats, value_all, key_all)
    extend_table(ext_ref, rel_key)
    back_ref[...] = nn(flip, query_all[size : 2 * size, :]).astype(BF)
    stat_lane = lanes((size, 128))

    def pair_step(pair, carry):
        columns = pair_columns(pair)
        delta = jnp.concatenate(
            [
                jnp.sum(jnp.where(stat_lane == head, stats[...], 0.0), axis=1, keepdims=True)
                for head in (2 * pair, 2 * pair + 1)
            ],
            axis=0,
        )
        grad_chances = nt(stacked(sent[:size, columns]), value_all[:, columns])
        grad_scores = (chances[pair].astype(F32) * (grad_chances - delta)).astype(BF)
        row_grad, table = position_backward(
            block, grad_scores, flip, key_all[:, columns], ext_ref[:, columns], back_ref[:, columns], wall_ref, 3 * size
        )
        there = pair_columns(pair - first)
        query_store.ref[:, there] = nn(flip, (row_grad * scale).astype(BF)).astype(BF)
        rel_key_grad_store.ref[there, :] = table_grad(table, scale)
        return carry

    for pair in range(first, last):
        pair_step(pair, 0)


def key_kernel(
    block_ref, length_ref, place_ref, rel_query, key_all, rel_key, query_all, value_all,
    sent_own, sent_core, sent_far, sent_diagonal,
    own, relative, grad_query_low, grad_rel_key_low, grad_query_high, grad_rel_key_high, query_weight, key_weight,
    value_weight, grad_first, tokens_store, late_send_low, late_send_high, late_keep,
    grads_out, key_rows_ref, value_rows_ref, rel_grad_ref,
    sent_ref, s_ref, grad_ref, ext_ref, wall_ref, back_ref, stat_ref,
):
    block = block_ref[0]
    length = length_ref[0]
    size, model_width = key_rows_ref.shape
    scale = 1.0 / math.sqrt(3.0 * (model_width // HEADS))
    factor = LOG2E * scale
    flip = reversal(size)
    rel_query, key_all, rel_key, query_all, value_all = ready(rel_query, key_all, rel_key, query_all, value_all)
    extend_table(ext_ref, rel_query)
    back_ref[...] = nn(flip, key_all[size : 2 * size, :]).astype(BF)
    for at, rows in placed(block, size, *ready(sent_own, sent_core, sent_far, sent_diagonal)):
        sent_ref[pl.ds(at, size), :] = rows[:size, :]
        parts = rows[size:, :size].astype(F32)
        stat_ref[0:8, pl.ds(at, size)] = parts[0:8, :] + parts[8:16, :]
        stat_ref[8:16, pl.ds(at, size)] = parts[16:24, :] + parts[24:32, :]
    position = block * size + lax.broadcasted_iota(jnp.int32, (size, 1), 0)
    mask_column = jnp.where(position < length, 0.0, -1e30)

    def pair_step(pair, carry):
        columns = pair_columns(pair)
        key_pair = stacked(key_all[size : 2 * size, columns])
        own_terms(block, s_ref, key_pair, rel_query[:, columns], 0)
        other_terms(
            block,
            s_ref,
            lambda slot: query_all[slot * size : (slot + 1) * size, columns],
            stacked(rel_key[:, columns]),
            1,
            range(4),
        )
        content = nt(key_pair, query_all[:, columns])
        for side in range(2):
            rows = slice(side * size, (side + 1) * size)
            less = mask_column - stat_ref[pl.ds(8 + 2 * pair + side, 1), :]
            s_ref[rows, :] = jnp.exp2((s_ref[rows, :] + content[rows]) * factor + less)
        value_grad = nn(abreast(s_ref[...].astype(BF)), stacked(sent_ref[:, columns]))
        grad_chances = nt(stacked(value_all[size : 2 * size, columns]), sent_ref[:, columns])
        for side in range(2):
            rows = slice(side * size, (side + 1) * size)
            delta = stat_ref[pl.ds(2 * pair + side, 1), :]
            grad_ref[rows, :] = (s_ref[rows, :] * (grad_chances[rows] - delta)).astype(BF)
        row_grad, table = position_backward(
            block, grad_ref[...], flip, query_all[:, columns], ext_ref[:, columns], back_ref[:, columns], wall_ref,
            3 * size + 1,
        )
        key_rows_ref[:, columns] = (row_grad * scale).astype(BF)
        value_rows_ref[:, columns] = value_grad.astype(BF)
        rel_grad_ref[columns, :] = table_grad(table, scale)
        return carry

    lax.fori_loop(0, HEADS // 2, pair_step, 0)
    own, relative, *grads = ready(
        own, relative, grad_query_low, grad_rel_key_low, grad_query_high, grad_rel_key_high
    )
    grad_query = jnp.concatenate([grads[0][...], grads[2][...]], axis=1)
    grad_rel_key = jnp.concatenate([grads[1][...], grads[3][...]], axis=0)
    rel = relative.shape[0]
    grad_key = nn(flip, key_rows_ref[...]).astype(BF)
    grad_value = value_rows_ref[...]
    rel_query_grad = rel_grad_ref[...]
    rel_key_grad = grad_rel_key
    query_low = rel_query_grad.astype(BF)
    key_low = nn(rel_key_grad.astype(BF), reversal(rel)).astype(BF)
    tokens = own[...]
    table = relative[...]
    grads_out[0:model_width, :] = (tn(tokens, grad_query) + tt(table, query_low)).astype(BF)
    grads_out[model_width : 2 * model_width, :] = (tn(tokens, grad_key) + tt(table, key_low)).astype(BF)
    grads_out[2 * model_width : 3 * model_width, :] = tn(tokens, grad_value).astype(BF)
    late_sends = (late_send_low, late_send_high)
    push_half(0, block % 2, place_ref[0], grads_out, late_sends, late_keep)
    table_at = 3 * model_width
    query_weight, key_weight, value_weight, grad_first = ready(query_weight, key_weight, value_weight, grad_first)
    grads_out[table_at : table_at + rel, :] = (
        tt(query_low, query_weight[...]) + tt(key_low, key_weight[...])
    ).astype(BF)
    small_at = table_at + rel
    grads_out[small_at + 16 :, :] = jnp.zeros((grads_out.shape[0] - small_at - 16, model_width), BF)
    ones = jnp.ones((8, rel), BF)

    def lane_sums(values):
        high = values.astype(BF)
        low = (values - high.astype(F32)).astype(BF)
        return (nt(ones, high) + nt(ones, low))[0:1, :]

    small = [
        column_sum(grad_query) + lane_sums(rel_query_grad),
        column_sum(grad_key) + lane_sums(rel_key_grad),
        column_sum(grad_value),
        jnp.zeros((13, model_width), F32),
    ]
    grads_out[small_at : small_at + 16, :] = jnp.concatenate(small, axis=0).astype(BF)
    push_half(1, block % 2, place_ref[0], grads_out, late_sends, late_keep)
    tokens_store.ref[...] = (
        nt(grad_query, query_weight[...])
        + nt(grad_key, key_weight[...])
        + nt(grad_value, value_weight[...])
        + grad_first[...]
    )


class Load:
    def __init__(self, source, buffer, sem):
        self.copy, self.buffer, self.waiting = pltpu.make_async_copy(source, buffer, sem), buffer, True

    def begin(self):
        self.copy.start()

    def ready(self):
        if self.waiting:
            self.copy.wait()
        self.waiting = False
        return self.buffer


def ready(*loads):
    return [load.ready() for load in loads]


class Store:
    def __init__(self, target, buffer, sem):
        self.copy, self.ref, self.shape, self.waiting = pltpu.make_async_copy(buffer, target, sem), buffer, buffer.shape, False

    def push(self):
        self.copy.start()
        self.waiting = True

    def finish(self):
        if not self.waiting:
            self.push()
        self.copy.wait()


class Here:
    def __init__(self, ref):
        self.ref = self.buffer = ref
        self.shape = ref.shape

    def ready(self):
        return self.ref

    def push(self):
        pass

    def finish(self):
        pass


def terms_after(first, terms):
    arrays = in_order(first, [array for array, _, _ in terms])
    return [(array, start, blocks) for array, (_, start, blocks) in zip(arrays, terms)]


class Raw:
    def __init__(self, target, sems):
        self.target, self.sems = target, sems
        self.shape = target.shape

    def push_from(self, source, k, part):
        pltpu.make_async_copy(source, self.target.at[pl.ds(k * part, part)], self.sems.at[k]).start()
        self.part = part

    def finish(self):
        for k in range(self.shape[0] // self.part):
            there = self.target.at[pl.ds(k * self.part, self.part)]
            pltpu.make_async_copy(there, there, self.sems.at[k]).wait()


def push_half(which, core, place, rows_ref, sends, keep):
    half = keep.shape[0]
    part = half // 4

    def source(k):
        return rows_ref.at[pl.ds(pl.multiple_of(which * half + (place ^ k) * part, 16), part)]

    @pl.when(core == which)
    def _():
        for k in range(4):
            keep.push_from(source(k), k, part)

    @pl.when(core != which)
    def _():
        for k in range(4):
            sends[k // 2].push_from(source(k), k % 2, part)


class Kept:
    def __init__(self, *what):
        self.what = what


class Bare:
    def __init__(self, *what):
        self.what = what


class Fetch:
    def __init__(self, what):
        self.what = what


def call(kernel, outs, scratch, *operands, scalars, micros, vmem, later=False):
    fetched = [k for k, operand in enumerate(operands) if isinstance(operand, Fetch)]
    bare_in = [k for k, operand in enumerate(operands) if isinstance(operand, Bare)]
    operands = [
        operand.what if isinstance(operand, Fetch) else operand.what[0] if isinstance(operand, Bare) else operand
        for operand in operands
    ]
    bare_out = [k for k, out in enumerate(outs) if isinstance(out, Bare)]
    outs = [out.what if isinstance(out, Bare) else out for out in outs]
    outs = list(outs) + [Kept(operands[k].shape, operands[k].dtype) for k in fetched]
    kept_in = [isinstance(operand, Kept) for operand in operands]
    kept_out = [isinstance(out, Kept) for out in outs]
    operands = [
        operand if k < scalars
        else pltpu.with_memory_space_constraint(operand.what[0], pltpu.VMEM) if kept
        else pltpu.with_memory_space_constraint(operand, pltpu.HBM)
        for k, (operand, kept) in enumerate(zip(operands, kept_in))
    ]
    outs = [out.what if kept else out for out, kept in zip(outs, kept_out)]
    raw = [len(out) > 2 for out in outs]
    loads = [k for k in range(scalars, len(operands)) if not kept_in[k] and k not in bare_in]
    stores = [k for k in range(len(outs)) if not kept_out[k] and k not in bare_out]
    buffered = [k for k in stores if not raw[k]]
    own_loads = [k for k in loads if k not in fetched]

    def body(*refs):
        n, m = len(operands), len(outs)
        ins, results, rest = list(refs[:n]), list(refs[n : n + m]), list(refs[n + m :])
        in_sems, out_sems = rest.pop(), rest.pop()
        buffers = [rest.pop() for _ in range(len(own_loads) + len(buffered))][::-1]
        targets = dict(zip(own_loads, buffers)) | dict(zip(fetched, results[m - len(fetched) :]))
        results = results[: m - len(fetched)]
        for k in range(scalars, n):
            if kept_in[k]:
                ins[k] = Here(ins[k])
        for place, k in enumerate(loads):
            ins[k] = Load(ins[k], targets[k], in_sems.at[place])
            if not later:
                ins[k].begin()
        buffers = buffers[len(own_loads) :]
        for k in range(len(results)):
            if kept_out[k]:
                results[k] = Here(results[k])
        for place, k in enumerate(stores):
            if raw[k]:
                results[k] = Raw(results[k], out_sems.at[place])
            else:
                results[k] = Store(results[k], buffers.pop(0), out_sems.at[place, 0])
        kernel(*ins, *results, *rest)
        for k in fetched:
            ins[k].ready()
        for k in stores:
            results[k].finish()

    spaces = [
        pltpu.SMEM if k < scalars else pltpu.VMEM if kept_in[k] else pltpu.HBM for k in range(len(operands))
    ]
    buffers = [(operands[k].shape, operands[k].dtype) for k in own_loads] + [outs[k][:2] for k in buffered]
    return pl.pallas_call(
        body,
        out_shape=[
            pltpu.VMEM(out[0], out[1]) if kept else pltpu.HBM(out[0], out[1])
            for out, kept in zip(outs, kept_out)
        ],
        in_specs=[pl.BlockSpec(memory_space=space) for space in spaces],
        out_specs=[pl.BlockSpec(memory_space=pltpu.VMEM if kept else pltpu.HBM) for kept in kept_out],
        scratch_shapes=[
            pltpu.SemaphoreType.DMA(space[0]) if space[1] is None else pltpu.VMEM(*space)
            for space in list(scratch) + buffers
        ]
        + [pltpu.SemaphoreType.DMA((max(len(stores), 1), 4)), pltpu.SemaphoreType.DMA((max(len(loads), 1),))],
        compiler_params=pltpu.CompilerParams(vmem_limit_bytes=vmem * MIB),
        cost_estimate=pl.CostEstimate(flops=micros * 10**9, bytes_accessed=micros * 10**6, transcendentals=0),
    )(*operands)


class Group:
    def __init__(self, blk_count, dp_count, bits):
        self.blk_count, self.dp_count, self.bits = blk_count, dp_count, bits
        self.size = 2 ** len(bits)
        place = {"blk": lax.axis_index("blk"), "dp": lax.axis_index("dp")}
        self.digits = [(place[axis] >> (bit.bit_length() - 1)) & 1 for axis, bit in bits]
        self.me = sum(digit << k for k, digit in enumerate(self.digits))

    def pairs(self, mask):
        change = {"blk": 0, "dp": 0}
        for k, (axis, bit) in enumerate(self.bits):
            if mask >> k & 1:
                change[axis] |= bit
        return [
            (blk * self.dp_count + dp, (blk ^ change["blk"]) * self.dp_count + (dp ^ change["dp"]))
            for blk in range(self.blk_count)
            for dp in range(self.dp_count)
        ]

    def send(self, values, mask):
        return lax.ppermute(values, ("blk", "dp"), self.pairs(mask))

    def scatter(self, terms):
        def part(index):
            return [
                (array, first + index * (blocks // self.size), blocks // self.size) for array, first, blocks in terms
            ]

        outs = [total(part(self.me ^ mask)) for mask in range(1, self.size)]
        arrived = [self.send(out, mask + 1) for mask, out in enumerate(outs)]
        return outs, part(self.me) + [whole(array) for array in arrived]

    def pieces(self, held):
        return [held] + [self.send(held, mask) for mask in range(1, self.size)]

    def gather(self, held):
        return self.arrange(self.pieces(held))

    def arrange(self, parts):
        for k, digit in enumerate(self.digits):
            parts = [
                jnp.where(digit == 0, parts[q], parts[q ^ (1 << k)]) for q in range(self.size)
            ]
        return jnp.concatenate(parts, axis=0)


def groups_of(blk_count, dp_count):
    bits, bit = [], 2
    while bit < dp_count:
        bits.append(("dp", bit))
        bit *= 2
    groups = [[("blk", 1)], [("blk", 2), ("dp", 1)]]
    groups += [bits[k : k + 2] for k in range(0, len(bits), 2)]
    return [Group(blk_count, dp_count, group) for group in groups]


def whole(array):
    return array, 0, array.shape[0]


def total(terms):
    spans = [
        array[first : first + blocks] if isinstance(first, int) else lax.dynamic_slice_in_dim(array, first, blocks, 0)
        for array, first, blocks in terms
    ]
    return sum(span.astype(F32) for span in spans).astype(BF)


def in_order(first, then):
    return lax.optimization_barrier((first, then))[1]


def halves_to_scratch(core_ref, place_ref, held, arrived, both_ref):
    held, arrived = ready(held, arrived)
    half = held.shape[0]
    part = half // 4
    for k in range(4):
        at = (place_ref[0] ^ k) * part
        span = slice(k * part, (k + 1) * part)
        both_ref[pl.ds(pl.multiple_of(core_ref[0] * half + at, 16), part), :] = held[span, :]
        both_ref[pl.ds(pl.multiple_of((1 - core_ref[0]) * half + at, 16), part), :] = arrived[span, :]


def early_kernel(
    core_ref, place_ref, held, arrived,
    outer_weight, inner_weight, output_weight, outer_bias, second_gain, second_bias, inner_bias, first_gain, first_bias,
    output_bias,
    both_ref,
):
    halves_to_scratch(core_ref, place_ref, held, arrived, both_ref)
    inner_width, width = outer_weight.shape
    chunks = inner_width // width
    for chunk in range(chunks):
        span = slice(chunk * width, (chunk + 1) * width)
        outer_weight.ref[span, :] = both_ref[span, :].T.astype(F32)
    outer_weight.push()
    for chunk in range(chunks):
        at = inner_width + chunk * width
        inner_weight.ref[:, chunk * width : (chunk + 1) * width] = both_ref[at : at + width, :].astype(F32)
    at = 2 * inner_width
    output_weight.ref[...] = both_ref[at : at + width, :].astype(F32)
    output_weight.push()
    small = both_ref[at + width : at + width + 16, :].astype(F32)

    def vector(out, row):
        out.ref[...] = small[row, :]
        out.push()

    vector(outer_bias, 0)
    vector(second_gain, 1)
    vector(second_bias, 2)
    inner_bias.ref[...] = jnp.concatenate([small[3 + k : 4 + k, :] for k in range(chunks)], axis=1)[0, :]
    inner_bias.push()
    vector(first_gain, 3 + chunks)
    vector(first_bias, 4 + chunks)
    vector(output_bias, 5 + chunks)


def late_kernel(mine, shapes, core_ref, place_ref, held, *rest):
    outs, (rows_ref, wide_ref, vector_ref, sems) = rest[-11:-4], rest[-4:]
    query_weight, query_bias, key_weight, key_bias, value_weight, value_bias, relative = outs
    half, width = rows_ref.shape
    part = half // 4
    rel = relative.shape[0]
    for k in range(4):
        at = pl.multiple_of((place_ref[0] ^ k) * part, 16)
        rows_ref[pl.ds(at, part), :] = held[k * part : (k + 1) * part, :]
    split = half - 2 * width
    which = core_ref[0] if mine else 1 - core_ref[0]

    def copy(spans):
        copies = []
        for k, (at, rows, out, start) in enumerate(spans):
            wide_ref[at : at + rows, :] = rows_ref[at : at + rows, :].astype(F32)
            one = pltpu.make_async_copy(wide_ref.at[pl.ds(at, rows)], out.at[pl.ds(start, rows)], sems.at[k])
            one.start()
            copies.append(one)
        return copies

    @pl.when(which == 0)
    def _():
        spans = ((0, width, query_weight, 0), (width, width, key_weight, 0), (2 * width, split, value_weight, 0))
        for one in copy(spans):
            one.wait()

    @pl.when(which == 1)
    def _():
        rest_rows = width - split
        copies = copy(((rest_rows, rel, relative, 0), (0, rest_rows, value_weight, split)))
        small = rows_ref[rest_rows + rel : rest_rows + rel + 16, :].astype(F32)
        for k, out in enumerate((query_bias, key_bias, value_bias)):
            vector_ref[k, :] = small[k, :]
            one = pltpu.make_async_copy(vector_ref.at[k], out, sems.at[2 + k])
            one.start()
            copies.append(one)
        for one in copies:
            one.wait()


def late_call(mine, shapes, core, place, held, *before):
    hbm, smem = pl.BlockSpec(memory_space=pltpu.HBM), pl.BlockSpec(memory_space=pltpu.SMEM)
    width = held.shape[1]
    return pl.pallas_call(
        functools.partial(late_kernel, mine, shapes),
        out_shape=[pltpu.HBM(shape, F32) for shape in shapes],
        in_specs=[smem, smem, pl.BlockSpec(memory_space=pltpu.VMEM)] + [hbm] * len(before),
        out_specs=[hbm] * len(shapes),
        scratch_shapes=[
            pltpu.VMEM(held.shape, BF),
            pltpu.VMEM(held.shape, F32),
            pltpu.VMEM((8, width), F32),
            pltpu.SemaphoreType.DMA((5,)),
        ],
        input_output_aliases={3 + k: k for k in range(len(before))},
        compiler_params=pltpu.CompilerParams(vmem_limit_bytes=10 * MIB),
        cost_estimate=pl.CostEstimate(flops=2 * 10**9, bytes_accessed=2 * 10**6, transcendentals=0),
    )(core, place, pltpu.with_memory_space_constraint(held, pltpu.VMEM), *before)


def on_device(
    blk_count, dp_count,
    tokens, lengths, query_weight, query_bias, key_weight, key_bias, value_weight, value_bias,
    output_weight, output_bias, first_gain, first_bias, inner_weight, inner_bias, outer_weight, outer_bias,
    second_gain, second_bias, relative_table, cotangent,
):
    seq_count, size, width = tokens.shape
    rel = relative_table.shape[0]
    inner_width = inner_weight.shape[1]
    own = tokens[0]
    block = lax.axis_index("blk").astype(jnp.int32).reshape(1)
    groups = groups_of(blk_count, dp_count)
    chips = groups[1:]
    place = chips[0].me.astype(jnp.int32).reshape(1)
    shards = blk_count * dp_count

    def along(values, bit):
        return lax.ppermute(values, "blk", [(i, i ^ bit) for i in range(blk_count)])

    def blocks(rows, share):
        return rows.reshape(shards // share, -1, width)

    def flat(values):
        return values.reshape(-1, width)

    def first_terms(keep, low, high):
        arrived = [groups[0].send(blocks(piece, 4), 1) for piece in (low, high)]
        keep, part = blocks(keep, 2), shards // 8
        return [[(keep, k * part, part), (arrived[k // 2], k % 2 * part, part)] for k in range(4)]

    def first_scatter(parts):
        outs = [total(terms) for terms in parts[1:]]
        return outs, parts[0] + [whole(chips[0].send(out, k + 1)) for k, out in enumerate(outs)]

    core = along(own, 1)
    far = along(own, 2)
    diagonal = along(own, 3)
    full = blk_count * size
    slabs = (HEADS // 2, 2 * size, 3 * size + 128)
    (
        rel_query, rel_key, terms, relative_kept, query_weight, key_weight, query_bias, key_bias, own, value_weight, value_bias,
    ) = call(
        first_kernel,
        [Kept((rel, width), BF), Kept((rel, width), BF), Bare(slabs, F32)],
        [((size, width), BF), ((size, width), BF), (slabs, F32), ((HEADS // 2,), None)],
        block,
        *map(Fetch, (relative_table, query_weight, key_weight, query_bias, key_bias, own, value_weight, value_bias)),
        scalars=1, micros=9, vmem=14,
    )
    (
        layer_out, grad_first, chances, sent, stats, query_all, key_all, value_all,
        early_send_low, early_send_high, early_keep,
    ) = call(
        forward_kernel,
        [
            ((size, width), F32),
            Kept((size, width), F32),
            Kept((HEADS // 2, 2 * size, full), BF),
            Kept((size + 32, width), BF),
            Kept((size, 128), F32),
            Kept((full, width), BF),
            Kept((full, width), BF),
            Kept((full, width), BF),
            ((EARLY_ROWS // 4, width), BF, "raw"),
            ((EARLY_ROWS // 4, width), BF, "raw"),
            ((EARLY_ROWS // 2, width), BF, "raw"),
        ],
        [
            ((full, width), BF),
            ((2 * size, full), F32),
            ((size, width), F32),
            ((size, 128), F32),
            ((size, inner_width), BF),
            ((size, inner_width), F32),
            ((EARLY_ROWS, width), BF),
            (slabs, F32),
            ((size, width), F32),
            ((16, width), F32),
            ((1, inner_width), F32),
            ((HEADS // 2,), None),
        ],
        block, lengths, place,
        *map(Kept, (own, core, far, diagonal, rel_query, rel_key)),
        Bare(terms),
        *map(Kept, (query_weight, key_weight, query_bias, key_bias, value_weight, value_bias)),
        output_weight, output_bias, first_gain, first_bias, inner_weight, inner_bias, outer_weight, outer_bias,
        second_gain, second_bias, cotangent[0],
        scalars=3, micros=20, vmem=26, later=True,
    )
    early_parts = first_terms(early_keep, early_send_low, early_send_high)
    sent_far = along(sent, 2)
    sent_core = along(sent, 1)
    position_scratch = [((2 * rel, width), BF), ((2 * size, 2 * rel), BF), ((size, width), BF)]
    query_arrays = tuple(map(Kept, (rel_key, query_all, sent, stats, value_all, key_all, chances)))

    def query_call(first, last, block_then):
        columns = (last - first) * 128
        return call(
            functools.partial(query_kernel, first, last),
            [Kept((size, columns), BF), Kept((columns, rel), F32)],
            position_scratch,
            block_then, *query_arrays,
            scalars=1, micros=2 * (last - first) + 1, vmem=10,
        )

    query_grads = query_call(0, QUERY_SPLIT, block)
    sending, early_terms = first_scatter([terms_after(query_grads[0], terms) for terms in early_parts])
    query_grads += query_call(QUERY_SPLIT, HEADS // 2, in_order(sending, block))
    sent_diagonal = along(in_order(query_grads[2], sent_far), 1)
    key_scratch = (
        [((full, width), BF), ((2 * size, full), F32), ((2 * size, full), BF)] + position_scratch + [((16, full), F32)]
    )
    key_arrays = tuple(
        map(Kept, (rel_query, key_all, rel_key, query_all, value_all, sent, sent_core, sent_far, sent_diagonal))
    )
    grad_tokens, late_send_low, late_send_high, late_keep = call(
        key_kernel,
        [((size, width), F32)] + [((LATE_ROWS // 4, width), BF, "raw")] * 2 + [((LATE_ROWS // 2, width), BF, "raw")],
        [((LATE_ROWS, width), BF), ((size, width), BF), ((size, width), BF), ((width, rel), F32)] + key_scratch,
        block, lengths, place, *key_arrays,
        *map(Kept, (own, relative_kept, *query_grads, query_weight, key_weight, value_weight, grad_first)),
        scalars=3, micros=17, vmem=18,
    )
    late_parts = first_terms(late_keep, late_send_low, late_send_high)
    early_terms = terms_after(late_send_low, early_terms)
    for group in chips[1:]:
        sending, early_terms = group.scatter(early_terms)
        late_parts = [terms_after(sending, terms) for terms in late_parts]
    sending_xy, late_terms = first_scatter(late_parts)
    arrived = [array for array, _, _ in late_terms[1 - chips[0].size :]]
    early_held = total(early_terms)
    for group in reversed(chips[2:]):
        early_held = group.gather(early_held)
    early_parts = chips[1].pieces(early_held)
    for group in chips[1:]:
        sending_z, late_terms = group.scatter(late_terms)
    z_arrived = [array for array, _, _ in late_terms[1 - chips[-1].size :]]
    early_parts = in_order(z_arrived[0], early_parts)
    early_pieces = chips[0].pieces(chips[1].arrange(early_parts))
    late_held = total(late_terms)
    for group in reversed(chips[2:]):
        late_held = group.gather(late_held)
    late_parts = chips[1].pieces(late_held)
    late_parts, early_pieces[1] = lax.optimization_barrier((late_parts, early_pieces[1]))
    late_held = chips[1].arrange(late_parts)
    early_held = jnp.concatenate(early_pieces, axis=0)
    late_pieces = chips[0].pieces(late_held)
    my_core = groups[0].me.astype(jnp.int32).reshape(1)
    square, vector = ((width, width), F32), ((width,), F32)
    (
        g_outer_weight, g_inner_weight, g_output_weight, g_outer_bias, g_second_gain, g_second_bias, g_inner_bias,
        g_first_gain, g_first_bias, g_output_bias,
    ) = call(
        early_kernel,
        [((inner_width, width), F32), ((width, inner_width), F32), square, vector, vector, vector,
         ((inner_width,), F32), vector, vector, vector],
        [((EARLY_ROWS, width), BF)],
        my_core, place, *(Kept(flat(piece)) for piece in groups[0].pieces(early_held)),
        scalars=2, micros=4, vmem=14,
    )
    late_held = jnp.concatenate(in_order(g_output_bias, late_pieces), axis=0)
    own_half, other_half = (flat(piece) for piece in groups[0].pieces(late_held))
    shapes = [square[0], vector[0]] * 3 + [(rel, width)]
    late_grads = late_call(True, shapes, my_core, place, own_half)
    (
        g_query_weight, g_query_bias, g_key_weight, g_key_bias, g_value_weight, g_value_bias, g_relative,
    ) = late_call(False, shapes, my_core, place, other_half, *late_grads)
    return (
        layer_out[None], grad_tokens[None], g_query_weight, g_query_bias, g_key_weight, g_key_bias,
        g_value_weight, g_value_bias, g_output_weight, g_output_bias, g_first_gain, g_first_bias,
        g_inner_weight, g_inner_bias, g_outer_weight, g_outer_bias, g_second_gain, g_second_bias, g_relative,
    )


def solution(mesh):
    blk_count, dp_count = mesh.shape["blk"], mesh.shape["dp"]
    rows = P("dp", "blk", None)
    in_specs = (rows, P("dp")) + (P(),) * 17 + (rows,)
    out_specs = (rows, rows) + (P(),) * 17

    def whole(*arrays):
        return on_device(blk_count, dp_count, *arrays)

    return jax.shard_map(whole, mesh=mesh, in_specs=in_specs, out_specs=out_specs, check_vma=False)
```
